256 devices in a mesh: ctx: 32 (over y, x, core), head: 8 (over z).
Axes of the slice: x: 4, y: 4, z: 8, core: 2. Of those that a mesh axis runs over, the one named last changes fastest.
Arguments:
- x_in: bfloat16 [24576, 8192], P('ctx', 'head'), may hold values from -6 to 6
- z_in: bfloat16 [24576, 8192], P('ctx', 'head'), may hold values from -6 to 6
- bc_in: bfloat16 [24576, 2048], P('ctx', 'head'), may hold values from -6 to 6
- dt_in: bfloat16 [24576, 128], P('ctx', 'head'), may hold values from -4 to 4
- destination: int32 [24576], P('ctx'), may hold values from 0 to 24575, as said below
- doc_lengths: int32 [16], replicated, may hold values from 1 to 12288, 24576 in all
- conv_x: bfloat16 [4, 8192], P(None, 'head'), may hold values from -3 to 3
- conv_bc: bfloat16 [4, 2048], P(None, 'head'), may hold values from -3 to 3
- dt_bias: float32 [128], P('head'), may hold values from -4.5 to -3.5
- a_log: float32 [128], P('head'), may hold values from -12 to 1
- skip_gain: float32 [128], P('head'), may hold values from 0.5 to 1.5
- norm_gain: bfloat16 [8192], P('head'), may hold values from 0.25 to 1.75
- out_weight: bfloat16 [8192, 4096], P('head'), may hold values from -0.0625 to 0.0625
Outputs:
- mixed: bfloat16 [24576, 4096], P(('ctx', 'head'))
The draws below stay inside these ranges and needn't reach their ends.
Inputs may be any that keep to these rules, and one draw needn't show every extreme that they name: destination is a permutation of the pack positions. Loader row i * 768 + j (shard i) goes to pack shard i, i + 1 or i - 1. Rows of shard i bound for shard i + 1 take the first positions of that shard, at most 384 of them; rows bound for shard i - 1 take its last positions, at most 384. Some loader shard sends exactly 384 rows to the next shard.
All inputs are finite; a program needn't handle non-finite values.
Results may differ from the reference program's by a relative error of at most 0.02.
Values may be sent and summed in bfloat16 or wider, within the bound.
A program may use at most 128 MiB of HBM per device.

```python
import math
import jax
import jax.numpy as jnp
import numpy as np
from jax import lax

D = 4096
HEADS = 128
P_SIZE = 64
N = 128
G = 8
KCONV = 4
SPAN = 128
DOCS = 16
TOK_DEV = 768
TOKENS = 24576
CAP = 384
N_HEAD = 8


def draw_destination(key, part):
    key = jax.random.fold_in(key, 5)
    count_key, forced_key, shuffle_key = jax.random.split(key, 3)
    shard_count = TOKENS // TOK_DEV
    swap_count = jax.random.randint(count_key, (shard_count,), 0, CAP + 1)
    forced_at = jax.random.randint(forced_key, (), 0, shard_count - 1)
    shard_idx = jnp.arange(shard_count, dtype=jnp.int32)
    swap_count = jnp.where(shard_idx == forced_at, CAP, swap_count)
    swap_count = jnp.where(shard_idx == shard_count - 1, 0, swap_count)
    swap_before = jnp.concatenate([jnp.zeros((1,), jnp.int32), swap_count[:-1].astype(jnp.int32)])
    slot_idx = jnp.arange(TOK_DEV, dtype=jnp.int32)[None, :]
    shard_col = shard_idx[:, None]
    swap_here = swap_count[:, None].astype(jnp.int32)
    swap_prev = swap_before[:, None]
    pack_pos = jnp.where(slot_idx >= TOK_DEV - swap_here, (shard_col + 1) * TOK_DEV + slot_idx - (TOK_DEV - swap_here), jnp.where(slot_idx < swap_prev, (shard_col - 1) * TOK_DEV + TOK_DEV - swap_prev + slot_idx, shard_col * TOK_DEV + slot_idx))
    row_keys = jax.random.split(shuffle_key, shard_count)
    shuffle = jax.vmap(lambda row_key: jax.random.permutation(row_key, TOK_DEV))(row_keys)
    pack_pos = jnp.take_along_axis(pack_pos, shuffle, axis=1)
    return pack_pos.reshape(TOKENS).astype(jnp.int32)


def draw_dt_in(key, part):
    key = jax.random.fold_in(key, 11)
    phase_key, level_key, noise_key = jax.random.split(key, 3)
    shard_count = TOKENS // TOK_DEV
    phase = jax.random.randint(phase_key, (), 0, 2)
    shard_idx = jnp.arange(shard_count, dtype=jnp.int32)
    sign = jnp.where((shard_idx + phase) % 2 == 0, 1.0, -1.0).astype(jnp.float32)
    level = jax.random.uniform(level_key, (shard_count,), minval=2.7, maxval=3.3)
    offset = jnp.repeat(sign * level, TOK_DEV)[:, None]
    noise = 0.7 * jax.random.normal(noise_key, (TOKENS, HEADS))
    return jnp.clip(offset + noise, -4.0, 4.0).astype(jnp.bfloat16)


def draw_a_log(key, part):
    key = jax.random.fold_in(key, 7)
    pick_key, slow_key, fast_key = jax.random.split(key, 3)
    slow_share = 0.5
    low_rate = 0.5
    high_rate = 1.5
    is_slow = jax.random.uniform(pick_key, (HEADS,)) < slow_share
    slow_rate = jnp.exp(jax.random.uniform(slow_key, (HEADS,), minval=math.log(low_rate), maxval=math.log(high_rate))) / TOKENS
    fast_rate = jnp.exp(jax.random.uniform(fast_key, (HEADS,), minval=math.log(1.0 / 50.0), maxval=math.log(1.0 / 30.0)))
    chosen = jnp.where(is_slow, slow_rate, fast_rate)
    return jnp.log(chosen / 0.16).astype(jnp.float32)


def levels(stream_key, dims, shards, least, high):
    level = 1.0
    for position, blocks in shards:
        heights = jax.random.uniform(jax.random.fold_in(jax.random.fold_in(stream_key, 6), position), (blocks,), jnp.float32, least / len(shards), high / len(shards))
        level = level * jnp.repeat(jnp.exp(heights), dims[position] // blocks).reshape((-1,) + (1,) * (len(dims) - 1 - position))
    return level


def split_up(amount, total, most, lean):
    loads = [(1 << 20) // math.isqrt(rank ** lean) + 1 for rank in range(2, amount + 1)]
    surplus, holding = total - most - (amount - 1), [1] * (amount - 1)
    while surplus > 0:
        free = [i for i in range(amount - 1) if holding[i] < most]
        mass, budget = sum([loads[i] for i in free]), surplus
        for i in free:
            addition = min(most - holding[i], max(1, budget * loads[i] // mass), surplus)
            holding[i] = holding[i] + addition
            surplus = surplus - addition
    return np.array([most] + holding)


def ragged(rng, number_of, total, bound, lean):
    if number_of == 2:
        one = jax.random.randint(rng, (), max(1, total - bound), min(bound, total - 1) + 1)
        return jnp.stack([one, total - one])
    lengths = jnp.asarray(split_up(number_of, total, bound, lean), jnp.int32)
    twos = (number_of - 1) // 2
    source_of, receiver = lengths[1:1 + 2 * twos:2], lengths[2:2 + 2 * twos:2]
    margin = jnp.minimum(source_of - 1, bound - receiver)
    passed = jax.random.randint(jax.random.fold_in(rng, 1), (twos,), 0, 1 << 20) % (margin + 1)
    lengths = lengths.at[1:1 + 2 * twos:2].set(source_of - passed).at[2:2 + 2 * twos:2].set(receiver + passed)
    return lengths[jax.random.permutation(jax.random.fold_in(rng, 2), number_of)]


def centred(own_key, shape, deviation, most, pieces=(), held_as=jnp.bfloat16):
    result = deviation * jax.random.normal(own_key, shape, jnp.float32)
    if pieces:
        result = result * levels(own_key, shape, pieces, -0.22, 0.18)
    return jnp.clip(result, -most, most).astype(held_as)


def setup_inputs(seed: int = 0) -> dict:
    splits = jax.random.split(jax.random.key(seed), 14)
    x_in = centred(splits[0], (TOKENS, HEADS * P_SIZE), 1.0, 6.0, ((0, 32), (1, 8)))
    z_in = centred(splits[1], (TOKENS, HEADS * P_SIZE), 1.0, 6.0, ((0, 32), (1, 8)))
    bc_in = centred(splits[2], (TOKENS, 2 * G * N), 1.0, 6.0, ((0, 32), (1, 8)))
    dt_in = draw_dt_in(jax.random.fold_in(splits[13], 71), 0)
    destination = draw_destination(jax.random.fold_in(splits[13], 71), 0)
    doc_lengths = ragged(splits[5], DOCS, TOKENS, TOKENS // 2, 2).astype(jnp.int32)
    conv_x = centred(splits[6], (KCONV, HEADS * P_SIZE), KCONV ** -0.5, 3.0, ((1, 8),))
    conv_bc = centred(splits[7], (KCONV, 2 * G * N), KCONV ** -0.5, 3.0, ((1, 8),))
    dt_bias = jnp.clip(-4.5 + 1.0 * jax.random.uniform(splits[8], (HEADS,), jnp.float32) ** levels(splits[8], (HEADS,), ((0, 8),), -0.2, 0.2), -4.5, -3.5)
    a_log = draw_a_log(jax.random.fold_in(splits[13], 71), 0)
    skip_gain = jnp.clip(0.5 + 1.0 * jax.random.uniform(splits[10], (HEADS,), jnp.float32) ** levels(splits[10], (HEADS,), ((0, 8),), -0.2, 0.2), 0.5, 1.5)
    norm_gain = jnp.clip(1.0 + 0.15 * jax.random.normal(splits[11], (HEADS * P_SIZE,), jnp.float32), 0.25, 1.75).astype(jnp.bfloat16)
    out_weight = centred(splits[12], (HEADS * P_SIZE, D), (HEADS * P_SIZE) ** -0.5, 0.0625, ((0, 8),))
    return dict(x_in=x_in, z_in=z_in, bc_in=bc_in, dt_in=dt_in, destination=destination, doc_lengths=doc_lengths, conv_x=conv_x, conv_bc=conv_bc, dt_bias=dt_bias, a_log=a_log, skip_gain=skip_gain, norm_gain=norm_gain, out_weight=out_weight)


def doc_ids(doc_lengths, positions):
    lengths_int = doc_lengths.astype(jnp.int32)
    doc_ends = jnp.cumsum(lengths_int, dtype=jnp.int32).astype(jnp.int32)
    starts = (doc_ends - lengths_int).astype(jnp.int32)
    counted = lax.optimization_barrier(jnp.sum((starts[None, :] <= positions.astype(jnp.int32)[:, None]).astype(jnp.int32), axis=1, dtype=jnp.int32))
    return (counted - 1).astype(jnp.int32)

def ssd_block(carry_state, prev_doc, x_block, b_block, c_block, dt_block, rate_block, block_doc, skip_gain):
    block_len = block_doc.shape[0]
    cum_rate = jnp.cumsum(rate_block, axis=0)
    ordinal = jnp.arange(block_len, dtype=jnp.int32)
    same_doc = (block_doc[:, None] == block_doc[None, :]) & (ordinal[None, :] <= ordinal[:, None])
    cum_t = jnp.moveaxis(cum_rate, 0, -1)
    rate_gap = cum_t[..., :, None] - cum_t[..., None, :]
    decay_mat = jnp.where(same_doc, jnp.exp(jnp.where(same_doc, rate_gap, 0.0)), 0.0)
    b_float = b_block.astype(jnp.float32)
    c_float = c_block.astype(jnp.float32)
    x_float = x_block.astype(jnp.float32)
    scores = jnp.einsum('tgn,sgn->gts', c_float, b_float)
    dt_t = jnp.moveaxis(dt_block, 0, -1)
    mixing = (decay_mat * scores[:, None] * dt_t[:, :, None, :]).astype(jnp.bfloat16)
    mixing = lax.optimization_barrier(mixing).astype(jnp.float32)
    inner_part = jnp.einsum('ghts,sghp->tghp', mixing, x_float)
    linked = (block_doc == prev_doc).astype(jnp.float32)
    entry_fac = jnp.exp(cum_rate) * linked[:, None, None]
    state_low = lax.optimization_barrier(carry_state.astype(jnp.bfloat16)).astype(jnp.float32)
    from_state = jnp.einsum('tgn,ghpn->tghp', c_float, state_low) * entry_fac[..., None]
    y_block = inner_part + from_state + skip_gain[None, :, :, None] * x_float
    tail_doc = (block_doc == block_doc[-1]).astype(jnp.float32)
    weight = jnp.exp(cum_rate[-1][None] - cum_rate) * tail_doc[:, None, None] * dt_block
    weighted_x = lax.optimization_barrier((weight[..., None] * x_float).astype(jnp.bfloat16)).astype(jnp.float32)
    carried = jnp.exp(cum_rate[-1]) * (block_doc[-1] == prev_doc).astype(jnp.float32)
    new_state = carry_state * carried[..., None, None] + jnp.einsum('sghp,sgn->ghpn', weighted_x, b_float)
    return (new_state, y_block)

def gated_norm(y_rows, z_rows, norm_gain, groups):
    gated = y_rows.astype(jnp.float32) * jax.nn.silu(z_rows.astype(jnp.float32))
    row_count = gated.shape[0]
    grouped = gated.reshape(row_count, groups, -1)
    inv_rms = lax.rsqrt(lax.optimization_barrier(jnp.mean(grouped * grouped, axis=-1, keepdims=True)) + 1e-05)
    return ((grouped * inv_rms).reshape(row_count, -1) * norm_gain.astype(jnp.float32)).astype(jnp.bfloat16)

def reference(x_in, z_in, bc_in, dt_in, destination, doc_lengths, conv_x, conv_bc, dt_bias, a_log, skip_gain, norm_gain, out_weight):
    hp_width = HEADS * P_SIZE
    per_group = HEADS // G
    dest_pos = destination.astype(jnp.int32)
    payload = jnp.concatenate([x_in, bc_in, dt_in], axis=1)
    packed = jnp.zeros_like(payload).at[dest_pos].set(payload)
    xbc_width = hp_width + 2 * G * N
    ext_pos = jnp.arange(TOKENS + KCONV - 1, dtype=jnp.int32) - (KCONV - 1)
    ext_doc = doc_ids(doc_lengths, ext_pos)
    doc_here = ext_doc[KCONV - 1:]
    extended = jnp.concatenate([jnp.zeros((KCONV - 1, xbc_width), jnp.bfloat16), packed[:, :xbc_width]], axis=0)
    kernel = jnp.concatenate([conv_x, conv_bc], axis=1).astype(jnp.float32)
    conv_sum = jnp.zeros((TOKENS, xbc_width), jnp.float32)
    for tap in range(KCONV):
        usable = (ext_doc[tap:tap + TOKENS] == doc_here).astype(jnp.float32)
        conv_sum = conv_sum + kernel[tap] * extended[tap:tap + TOKENS].astype(jnp.float32) * usable[:, None]
    conv_out = lax.optimization_barrier(jax.nn.silu(conv_sum).astype(jnp.bfloat16))
    x_heads = conv_out[:, :hp_width].reshape(TOKENS, G, per_group, P_SIZE)
    bc_heads = conv_out[:, hp_width:].reshape(TOKENS, G, 2, N)
    dt_step = jax.nn.softplus(packed[:, xbc_width:].astype(jnp.float32) + dt_bias)
    log_decay = dt_step * -jnp.exp(a_log)
    num_blocks = TOKENS // SPAN
    sequence = (x_heads.reshape(num_blocks, SPAN, G, per_group, P_SIZE), bc_heads[:, :, 0].reshape(num_blocks, SPAN, G, N), bc_heads[:, :, 1].reshape(num_blocks, SPAN, G, N), dt_step.reshape(num_blocks, SPAN, G, per_group), log_decay.reshape(num_blocks, SPAN, G, per_group), doc_here.reshape(num_blocks, SPAN))
    skip_grid = skip_gain.reshape(G, per_group)

    def advance(state_pair, entry_item):
        carry_state, prev_doc = state_pair
        x_block, b_block, c_block, dt_block, rate_block, block_doc = entry_item
        new_state, y_block = ssd_block(carry_state, prev_doc, x_block, b_block, c_block, dt_block, rate_block, block_doc, skip_grid)
        return ((new_state, block_doc[-1].astype(jnp.int32)), y_block)
    start_pair = (jnp.zeros((G, per_group, P_SIZE, N), jnp.float32), jnp.int32(-1))
    _, y_blocks = lax.scan(advance, start_pair, sequence)
    y_pack = lax.optimization_barrier(y_blocks.reshape(TOKENS, hp_width).astype(jnp.bfloat16))
    y_loader = y_pack[dest_pos]
    normed = gated_norm(y_loader, z_in, norm_gain, G)
    block_width = hp_width // N_HEAD

    def add_block(running, shard_num):
        begin = (shard_num * block_width).astype(jnp.int32)
        partial_value = jnp.dot(lax.dynamic_slice_in_dim(normed, begin, block_width, 1), lax.dynamic_slice_in_dim(out_weight, begin, block_width, 0), preferred_element_type=jnp.float32).astype(jnp.bfloat16)
        partial_value = lax.optimization_barrier(partial_value)
        return (running + partial_value.astype(jnp.float32), None)
    running, _ = lax.scan(add_block, jnp.zeros((TOKENS, D), jnp.float32), jnp.arange(N_HEAD, dtype=jnp.int32))
    return running.astype(jnp.bfloat16)
```

```python
import jax
import jax.numpy as jnp
from jax import lax
from jax.experimental import pallas as pl
from jax.experimental.pallas import tpu as pltpu
from jax.sharding import PartitionSpec as P

N = 128
KCONV = 4
SPAN = 128


def padded(cells, sides, width):
    for axis, dim in sides:
        count = lax.axis_size(axis)
        ends = count - 1
        head = lax.slice_in_dim(cells, 0, width, axis=dim)
        tail = lax.slice_in_dim(cells, cells.shape[dim] - width, cells.shape[dim], axis=dim)
        cells = jnp.concatenate(
            [
                lax.ppermute(tail, axis, [(i, (i + 1) % count) for i in range(ends)]),
                cells,
                lax.ppermute(head, axis, [((i + 1) % count, i) for i in range(ends)]),
            ],
            axis=dim,
        )
    return cells


def passed_along(block, axis, distance):
    devices = range(lax.axis_size(axis))
    route = [(i - distance, i) for i in devices if i - distance in devices]
    return lax.ppermute(block, axis, route)


def prefix(x, axis, join, neutral):
    place = lax.axis_index(axis)
    gathered = jax.tree.map(
        lambda a, kind: lax.all_gather(a.astype(kind), axis), x, (jnp.bfloat16, jnp.bfloat16)
    )
    state = jax.tree.map(lambda a, e: jnp.zeros_like(a) + jnp.asarray(e, a.dtype), x, neutral)

    def one(lap, state):
        return join(
            state,
            jax.tree.map(
                lambda a, own: lax.dynamic_index_in_dim(a, lap, 0, False).astype(own.dtype),
                gathered,
                x,
            ),
        )

    return lax.fori_loop(0, place, one, state)


def doc_ids(doc_lengths, positions):
    doc_ends = jnp.cumsum(doc_lengths, dtype=jnp.int32)
    starts = doc_ends - doc_lengths
    counted = jnp.sum(
        (starts[None, :] <= positions[:, None]).astype(jnp.int32), axis=1, dtype=jnp.int32
    )
    return counted - 1


def ssd_block(
    carry_state, prev_doc, x_block, b_block, c_block, dt_block, rate_block, block_doc, skip_gain
):
    block_len = block_doc.shape[0]
    cum_rate = jnp.cumsum(rate_block, axis=0)
    ordinal = jnp.arange(block_len, dtype=jnp.int32)
    same_doc = (block_doc[:, None] == block_doc[None, :]) & (ordinal[None, :] <= ordinal[:, None])
    cum_t = jnp.moveaxis(cum_rate, 0, -1)
    rate_gap = cum_t[..., :, None] - cum_t[..., None, :]
    decay_mat = jnp.where(same_doc, jnp.exp(jnp.where(same_doc, rate_gap, 0.0)), 0.0)
    scores = jnp.einsum("tgn,sgn->gts", c_block, b_block, preferred_element_type=jnp.float32)
    dt_t = jnp.moveaxis(dt_block, 0, -1)
    mixing = (decay_mat * scores[:, None] * dt_t[:, :, None, :]).astype(jnp.bfloat16)
    inner_part = jnp.einsum("ghts,sghp->tghp", mixing, x_block, preferred_element_type=jnp.float32)
    linked = (block_doc == prev_doc).astype(jnp.float32)
    entry_fac = jnp.exp(cum_rate) * linked[:, None, None]
    from_state = (
        jnp.einsum(
            "tgn,ghpn->tghp",
            c_block,
            carry_state.astype(jnp.bfloat16),
            preferred_element_type=jnp.float32,
        )
        * entry_fac[..., None]
    )
    y_block = inner_part + from_state + skip_gain[None, :, :, None] * x_block.astype(jnp.float32)
    tail_doc = (block_doc == block_doc[-1]).astype(jnp.float32)
    weight = jnp.exp(cum_rate[-1][None] - cum_rate) * tail_doc[:, None, None] * dt_block
    weighted_x = (weight[..., None] * x_block.astype(jnp.float32)).astype(jnp.bfloat16)
    carried = jnp.exp(cum_rate[-1]) * (block_doc[-1] == prev_doc).astype(jnp.float32)
    new_state = carry_state * carried[..., None, None] + jnp.einsum(
        "sghp,sgn->ghpn", weighted_x, b_block, preferred_element_type=jnp.float32
    )
    return (new_state, y_block)


def gated_norm(y_rows, z_rows, norm_gain, groups):
    gated = y_rows.astype(jnp.float32) * jax.nn.silu(z_rows.astype(jnp.float32))
    row_count = gated.shape[0]
    grouped = gated.reshape(row_count, groups, -1)
    inv_rms = lax.rsqrt(jnp.mean(grouped * grouped, axis=-1, keepdims=True) + 1e-05)
    return ((grouped * inv_rms).reshape(row_count, -1) * norm_gain.astype(jnp.float32)).astype(
        jnp.bfloat16
    )


def to_loader(block, destination, first_pos, margin):
    framed = padded(block, (("ctx", 0),), margin)
    return framed[destination - first_pos + margin]


SUBS = 4


def ring_kernel(normed_ref, w_hbm, out_ref, w_ref, sbuf, rbuf, w_sems, send_sems, recv_sems):
    n = lax.axis_size("head")
    me = lax.axis_index("head")
    rows = out_ref.shape[0]
    wide = w_ref.shape[1]
    width = wide // (2 * SUBS)
    barrier = pltpu.get_barrier_semaphore()
    loads = []
    for sub in range(SUBS):
        for way in range(2):
            cols = pl.ds((way * SUBS + sub) * width, width)
            loads.append(
                pltpu.make_async_copy(w_hbm.at[:, cols], w_ref.at[:, cols], w_sems.at[way, sub])
            )
    for load in loads:
        load.start()
    hops = (lax.rem(me + 1, n), lax.rem(me + n - 1, n))
    for hop in hops:
        pl.semaphore_signal(barrier, inc=1, device_id={"head": hop})
    rbuf[0] = jnp.zeros_like(rbuf[0])
    pl.semaphore_wait(barrier, 2)
    for load in loads:
        load.wait()

    def copy(step, way, sub):
        return pltpu.make_async_remote_copy(
            src_ref=sbuf.at[step, way, sub],
            dst_ref=rbuf.at[step + 1, way, sub],
            send_sem=send_sems.at[step, way, sub],
            recv_sem=recv_sems.at[step, way, sub],
            device_id={"head": hops[way]},
        )

    def one(step, _):
        for sub in range(SUBS):
            for way in range(2):
                chunk = lax.rem(me + 2 * n - 1 - step, n) if way == 0 else lax.rem(me + 1 + step, n)
                begin = (way * SUBS + sub) * width
                part = jnp.dot(
                    normed_ref[pl.ds(pl.multiple_of(chunk * rows, rows), rows), :],
                    w_ref[:, begin : begin + width],
                    preferred_element_type=jnp.float32,
                )

                @pl.when(step > 0)
                def _():
                    copy(step - 1, way, sub).wait_recv()

                total = (part + rbuf[step, way, sub].astype(jnp.float32)).astype(jnp.bfloat16)

                @pl.when(step < n - 1)
                def _():
                    sbuf[step, way, sub] = total
                    copy(step, way, sub).start()

                @pl.when(step == n - 1)
                def _():
                    out_ref[:, begin : begin + width] = total

        return 0

    lax.fori_loop(0, n, one, 0)

    def drain(step, _):
        for sub in range(SUBS):
            for way in range(2):
                copy(step, way, sub).wait_send()
        return 0

    lax.fori_loop(0, n - 1, drain, 0)


def project_scatter(normed, out_weight):
    n = lax.axis_size("head")
    rows = normed.shape[0] // n
    depth, wide = out_weight.shape
    width = wide // (2 * SUBS)
    return pl.pallas_call(
        ring_kernel,
        out_shape=jax.ShapeDtypeStruct((rows, wide), jnp.bfloat16),
        in_specs=[pl.BlockSpec(memory_space=pltpu.VMEM), pl.BlockSpec(memory_space=pl.ANY)],
        out_specs=pl.BlockSpec(memory_space=pltpu.VMEM),
        scratch_shapes=[
            pltpu.VMEM((depth, wide), jnp.bfloat16),
            pltpu.VMEM((n - 1, 2, SUBS, rows, width), jnp.bfloat16),
            pltpu.VMEM((n, 2, SUBS, rows, width), jnp.bfloat16),
            pltpu.SemaphoreType.DMA((2, SUBS)),
            pltpu.SemaphoreType.DMA((n - 1, 2, SUBS)),
            pltpu.SemaphoreType.DMA((n - 1, 2, SUBS)),
        ],
        compiler_params=pltpu.CompilerParams(
            collective_id=0, has_side_effects=True, vmem_limit_bytes=48 << 20
        ),
    )(normed, out_weight)


def per_device(
    x_in,
    z_in,
    bc_in,
    dt_in,
    destination,
    doc_lengths,
    conv_x,
    conv_bc,
    dt_bias,
    a_log,
    skip_gain,
    norm_gain,
    out_weight,
):
    tok_rows = x_in.shape[0]
    channels = x_in.shape[1]
    heads_here = dt_in.shape[1]
    head_size = channels // heads_here
    bc_width = bc_in.shape[1]
    state_size = conv_bc.shape[1] * 0 + N
    groups_here = bc_width // (2 * state_size)
    per_group = heads_here // groups_here
    margin = tok_rows // 2
    shard_id = lax.axis_index("ctx")
    first_pos = shard_id * tok_rows
    target = destination // tok_rows
    offset = destination - target * tok_rows
    relative = target - shard_id
    payload = jnp.concatenate([x_in, bc_in, dt_in], axis=1)
    col_count = payload.shape[1]
    slot_index = jnp.where(
        relative == -1,
        offset - (tok_rows - margin),
        jnp.where(relative == 1, margin + offset, 2 * margin),
    )
    outgoing = (
        jnp.zeros((2 * margin + 1, col_count), jnp.bfloat16)
        .at[slot_index]
        .set(payload)[: 2 * margin]
    )
    home_slot = jnp.where(relative == 0, offset, tok_rows)
    packed = (
        jnp.zeros((tok_rows + 1, col_count), jnp.bfloat16).at[home_slot].set(payload)[:tok_rows]
    )
    framed = padded(outgoing, (("ctx", 0),), margin)
    packed = (
        packed.at[:margin].add(framed[:margin]).at[tok_rows - margin :].add(framed[3 * margin :])
    )
    xbc_width = channels + bc_width
    rim_rows = passed_along(packed[tok_rows - (KCONV - 1) :, :xbc_width], "ctx", 1)
    extended = jnp.concatenate([rim_rows, packed[:, :xbc_width]], axis=0)
    ext_pos = first_pos - (KCONV - 1) + jnp.arange(tok_rows + KCONV - 1, dtype=jnp.int32)
    ext_doc = doc_ids(doc_lengths, ext_pos)
    doc_here = ext_doc[KCONV - 1 :]
    doc_before = ext_doc[KCONV - 2]
    kernel = jnp.concatenate([conv_x, conv_bc], axis=1).astype(jnp.float32)
    conv_sum = jnp.zeros((tok_rows, xbc_width), jnp.float32)
    for tap in range(KCONV):
        usable = (ext_doc[tap : tap + tok_rows] == doc_here).astype(jnp.float32)
        conv_sum = (
            conv_sum
            + kernel[tap] * extended[tap : tap + tok_rows].astype(jnp.float32) * usable[:, None]
        )
    conv_out = jax.nn.silu(conv_sum).astype(jnp.bfloat16)
    x_heads = conv_out[:, :channels].reshape(tok_rows, groups_here, per_group, head_size)
    bc_heads = conv_out[:, channels:].reshape(tok_rows, groups_here, 2, state_size)
    c_heads = bc_heads[:, :, 1]
    dt_step = jax.nn.softplus(
        packed[:, xbc_width : xbc_width + heads_here].astype(jnp.float32) + dt_bias
    )
    log_decay = (dt_step * -jnp.exp(a_log)).reshape(tok_rows, groups_here, per_group)
    dt_grid = dt_step.reshape(tok_rows, groups_here, per_group)
    skip_grid = skip_gain.reshape(groups_here, per_group)
    num_blocks = tok_rows // SPAN
    sequence = (
        x_heads.reshape(num_blocks, SPAN, groups_here, per_group, head_size),
        bc_heads[:, :, 0].reshape(num_blocks, SPAN, groups_here, state_size),
        c_heads.reshape(num_blocks, SPAN, groups_here, state_size),
        dt_grid.reshape(num_blocks, SPAN, groups_here, per_group),
        log_decay.reshape(num_blocks, SPAN, groups_here, per_group),
        doc_here.reshape(num_blocks, SPAN),
    )

    def advance(state_pair, entry_item):
        carry_state, prev_doc = state_pair
        x_block, b_block, c_block, dt_block, rate_block, block_doc = entry_item
        new_state, y_block = ssd_block(
            carry_state,
            prev_doc,
            x_block,
            b_block,
            c_block,
            dt_block,
            rate_block,
            block_doc,
            skip_grid,
        )
        return ((new_state, block_doc[-1]), y_block)

    empty_state = jnp.zeros((groups_here, per_group, head_size, state_size), jnp.float32)
    (local_state, _), y_blocks = lax.scan(advance, (empty_state, doc_before), sequence)
    shard_rate = jnp.cumsum(log_decay, axis=0)
    linked = (doc_here == doc_before).astype(jnp.float32)
    entry_decay = jnp.exp(shard_rate) * linked[:, None, None]
    shard_decay = entry_decay[-1]

    def compose(earlier, later):
        return (earlier[0] * later[0], later[0][..., None, None] * earlier[1] + later[1])

    incoming = prefix(
        (shard_decay, local_state),
        "ctx",
        compose,
        (jnp.ones_like(shard_decay), jnp.zeros_like(local_state)),
    )[1]
    correction = (
        jnp.einsum(
            "tgn,ghpn->tghp",
            c_heads,
            incoming.astype(jnp.bfloat16),
            preferred_element_type=jnp.float32,
        )
        * entry_decay[..., None]
    )
    y_local = y_blocks.reshape(tok_rows, groups_here, per_group, head_size)
    y_pack = (y_local + correction).reshape(tok_rows, channels).astype(jnp.bfloat16)
    y_loader = to_loader(y_pack, destination, first_pos, margin)
    normed = gated_norm(y_loader, z_in, norm_gain, groups_here)
    return project_scatter(normed, out_weight)


def solution(mesh):
    placed = (
        P("ctx", "head"),
        P("ctx", "head"),
        P("ctx", "head"),
        P("ctx", "head"),
        P("ctx"),
        P(),
        P(None, "head"),
        P(None, "head"),
        P("head"),
        P("head"),
        P("head"),
        P("head"),
        P("head", None),
    )
    return jax.shard_map(
        per_device, mesh=mesh, in_specs=placed, out_specs=P(("ctx", "head"), None), check_vma=False
    )
```

```python
import jax
import jax.numpy as jnp
from jax import lax
from jax.experimental import pallas as pl
from jax.experimental.pallas import tpu as pltpu
from jax.sharding import PartitionSpec as P

N = 128
SPAN = 128
KCONV = 4
SUBS = 4
WIDE = 256
TILE = 16
F32 = jnp.float32
BF16 = jnp.bfloat16


def nt(a, b):
    return lax.dot_general(a, b, (((1,), (1,)), ((), ())), preferred_element_type=F32)


def mm(a, b):
    return jnp.dot(a, b, preferred_element_type=F32)


def iota(shape, dim):
    return lax.broadcasted_iota(jnp.int32, shape, dim)


def one_hot(hit):
    return jnp.where(hit, 1.0, 0.0).astype(BF16)


def half_silu(v):
    return 0.5 * v * (1.0 + jnp.tanh(0.5 * v))


def layer_kernel(
    x_hbm,
    z_hbm,
    bc_ref,
    dt_ref,
    dest_ref,
    lengths_ref,
    convx_ref,
    convbc_ref,
    bias_ref,
    alog_ref,
    skip_ref,
    gain_ref,
    w_hbm,
    out_ref,
    x_ref,
    z_ref,
    w_ref,
    pout_ref,
    home_ref,
    q_ref,
    snd,
    rcvp,
    rcvn,
    dts,
    dtr,
    xext,
    conv_ref,
    cols_ref,
    ds_ref,
    car_ref,
    rrow_ref,
    score_ref,
    bt_ref,
    sloc,
    ypart,
    es_ref,
    framed,
    ss_ref,
    normed_ref,
    sa,
    ra,
    ret,
    inc,
    sbuf,
    rbuf,
    x_sems,
    z_sem,
    w_sems,
    xs_sems,
    xr_sems,
    ds_sems,
    dr_sems,
    as_sems,
    ar_sems,
    rs_sems,
    rr_sems,
    ys_sems,
    yr_sems,
    send_sems,
    recv_sems,
):
    nctx = lax.axis_size("ctx")
    nhead = lax.axis_size("head")
    me = lax.axis_index("ctx")
    mz = lax.axis_index("head")
    tok = bc_ref.shape[0]
    margin = tok // 2
    blocks = tok // SPAN
    quads = x_ref.shape[0]
    groups = SPAN // TILE
    heads = dt_ref.shape[1]
    docs = lengths_ref.shape[0]
    first = me * tok
    around = (lax.rem(me + 1, nctx), lax.rem(me + nctx - 1, nctx))
    hops = (lax.rem(mz + 1, nhead), lax.rem(mz + nhead - 1, nhead))

    barrier = pltpu.get_barrier_semaphore()

    def greet(j, _):
        pl.semaphore_signal(barrier, inc=1, device_id={"ctx": lax.rem(me + j, nctx)})
        return 0

    lax.fori_loop(1, nctx, greet, 0)
    for hop in hops:
        pl.semaphore_signal(barrier, inc=1, device_id={"head": hop})

    x_loads = [
        pltpu.make_async_copy(x_hbm.at[:, pl.ds(c * WIDE, WIDE)], x_ref.at[c], x_sems.at[c])
        for c in range(quads)
    ]
    z_load = pltpu.make_async_copy(z_hbm, z_ref, z_sem)
    wide = w_ref.shape[1]
    width = wide // (2 * SUBS)
    w_loads = []
    for sub in range(SUBS):
        for way in range(2):
            w_cols = pl.ds((way * SUBS + sub) * width, width)
            w_loads.append(
                pltpu.make_async_copy(w_hbm.at[:, w_cols], w_ref.at[:, w_cols], w_sems.at[way, sub])
            )
    for load in x_loads:
        load.start()
    z_load.start()
    for load in w_loads:
        load.start()

    rel_row = jnp.concatenate([dest_ref[i : i + 1, :] for i in range(blocks)], axis=1) - first
    slot = iota((margin + TILE, tok), 0)
    goal = jnp.where(slot < margin, slot + tok, slot + (tok - TILE - margin))
    pout_ref[0 : margin + TILE, :] = one_hot(goal == rel_row)
    pout_ref[margin + TILE :, :] = one_hot(iota((margin, tok), 0) - margin == rel_row)

    def exchange(chunk, way):
        if way == 0:
            src, dst = snd.at[chunk, pl.ds(0, margin + TILE)], rcvp.at[chunk]
        else:
            src, dst = snd.at[chunk, pl.ds(margin + TILE, margin)], rcvn.at[chunk]
        return pltpu.make_async_remote_copy(
            src_ref=src,
            dst_ref=dst,
            send_sem=xs_sems.at[chunk, way],
            recv_sem=xr_sems.at[chunk, way],
            device_id={"ctx": around[way]},
        )

    def dt_copy(way):
        return pltpu.make_async_remote_copy(
            src_ref=dts.at[way],
            dst_ref=dtr.at[way],
            send_sem=ds_sems.at[way],
            recv_sem=dr_sems.at[way],
            device_id={"ctx": around[way]},
        )

    def source(chunk):
        return bc_ref[...] if chunk == 0 else x_ref[chunk - 1]

    eye_heads = one_hot(iota((heads, heads), 0) == iota((heads, heads), 1))
    dt_rows = nt(eye_heads, dt_ref[...]).astype(BF16)
    dts[0] = nt(dt_rows, pout_ref[0:margin, :]).astype(BF16)
    dts[1] = nt(dt_rows, pout_ref[margin + TILE :, :]).astype(BF16)
    snd[0] = mm(pout_ref[...], source(0)).astype(BF16)

    pl.semaphore_wait(barrier, nctx + 1)
    for way in range(2):
        dt_copy(way).start()
    for way in range(2):
        exchange(0, way).start()
    for chunk in range(1, quads + 1):
        x_loads[chunk - 1].wait()
        snd[chunk] = mm(pout_ref[...], source(chunk)).astype(BF16)
        for way in range(2):
            exchange(chunk, way).start()

    home_ref[...] = one_hot(iota((tok, tok), 0) == rel_row)

    row16 = iota((heads, SPAN), 0)
    bias = jnp.zeros((heads, SPAN), F32)
    alog = jnp.zeros((heads, SPAN), F32)
    for h in range(heads):
        bias = jnp.where(row16 == h, bias_ref[h], bias)
        alog = jnp.where(row16 == h, alog_ref[h], alog)
    neg_rate = -jnp.exp(alog)
    dt_home = nt(dt_rows, home_ref[...])
    for way in range(2):
        dt_copy(way).wait_recv()
    dt_raw = dt_home + jnp.concatenate([dtr[0].astype(F32), dtr[1].astype(F32)], axis=1)
    steps = []
    rates = []
    for b in range(blocks):
        logit = dt_raw[:, b * SPAN : (b + 1) * SPAN] + bias
        step = jnp.maximum(logit, 0.0) + jnp.log1p(jnp.exp(-jnp.abs(logit)))
        steps.append(step)
        rates.append(step * neg_rate)
    spare = SPAN - blocks * heads
    steps = jnp.concatenate(steps + [jnp.ones((spare, SPAN), F32)], axis=0)
    rates = jnp.concatenate(rates + [jnp.zeros((spare, SPAN), F32)], axis=0)
    row = iota((SPAN, SPAN), 0)
    lane = iota((SPAN, SPAN), 1)
    upper = jnp.where(row <= lane, 1.0, 0.0)
    cum_rows = jnp.dot(
        rates, upper, precision=lax.Precision.HIGHEST, preferred_element_type=F32
    )
    rrow_ref[...] = cum_rows - jnp.log(steps)
    cum = cum_rows.T
    step_cols = steps.T
    shift = heads.bit_length() - 1
    lane_block = lax.shift_right_logical(lane, shift)
    row_block = lax.shift_right_logical(row, shift)
    block_start = first + lane_block * SPAN
    pos = block_start + row
    doc_start = jnp.zeros((SPAN, SPAN), jnp.int32)
    begin = jnp.int32(0)
    for d in range(docs):
        doc_start = jnp.where(pos >= begin, begin, doc_start)
        begin = begin + lengths_ref[d]
    last_start = doc_start[SPAN - 1 : SPAN, :]
    last = cum[SPAN - 1 : SPAN, :]
    same_head = (lane & (heads - 1)) == (row & (heads - 1))
    before = jnp.where(same_head & (row_block < lane_block), 1.0, 0.0)
    offset = jnp.dot(
        jnp.broadcast_to(last, (8, SPAN)),
        before,
        precision=lax.Precision.HIGHEST,
        preferred_element_type=F32,
    )[0:1, :]
    w_cols = jnp.where(pos >= last_start, jnp.exp(last - cum) * step_cols, 0.0)
    entry = jnp.where(doc_start < block_start, jnp.exp(cum), 0.0)
    entry_shard = jnp.where(doc_start < first, jnp.exp(cum + offset), 0.0)
    carried = jnp.where(last_start < block_start[0:1, :], jnp.exp(last), 0.0)
    shard_decay = jnp.where(last_start < first, jnp.exp(last + offset), 0.0)
    carried = jnp.broadcast_to(carried, (8, SPAN))
    for b in range(blocks):
        turn = (SPAN - b * heads) % SPAN
        for kind, array in enumerate((cum, w_cols, entry, entry_shard)):
            cols_ref[kind, b] = pltpu.roll(array, turn, 1) if turn else array
        ds_ref[b] = pltpu.roll(doc_start, turn, 1) if turn else doc_start
        car_ref[b] = pltpu.roll(carried, turn, 1) if turn else carried
    decay_at = (blocks - 1) * heads

    low = iota((1, SPAN), 1) < SPAN // 2

    def spread(cols, quad, at=0):
        parts = []
        for pair in range(2):
            h = at + 4 * quad + 2 * pair
            parts.append(jnp.where(low, cols[:, h : h + 1], cols[:, h + 1 : h + 2]))
        return jnp.concatenate(parts, axis=1)

    def rows_of(b):
        return pl.ds(pl.multiple_of(b * SPAN, SPAN), SPAN)

    def pack_conv(chunk):
        home = mm(home_ref[...], source(chunk))
        for way in range(2):
            exchange(chunk, way).wait_recv()
        xext[0:TILE, :] = rcvp[chunk, margin : margin + TILE, :].astype(F32) + snd[
            chunk, tok : tok + TILE, :
        ].astype(F32)
        xext[TILE : TILE + margin, :] = home[0:margin] + rcvp[chunk, 0:margin, :].astype(F32)
        xext[TILE + margin :, :] = home[margin:] + rcvn[chunk].astype(F32)
        if chunk == 0:
            taps = convbc_ref[...].astype(F32)
        else:
            taps = convx_ref[:, (chunk - 1) * WIDE : chunk * WIDE].astype(F32)

        for b in range(blocks):
            begins = ds_ref[b][:, 0:1] - (first + b * SPAN) - iota((SPAN, 1), 0)
            for half in range(2):
                at = slice(half * SPAN, (half + 1) * SPAN)
                base = b * SPAN + TILE
                total = taps[3:4, at] * xext[base : base + SPAN, at]
                for tap in range(KCONV - 1):
                    back = KCONV - 1 - tap
                    piece = xext[base - back : base - back + SPAN, at]
                    total = total + taps[tap : tap + 1, at] * jnp.where(begins <= -back, piece, 0.0)
                conv_ref[chunk, b * SPAN : (b + 1) * SPAN, at] = half_silu(total).astype(BF16)

    pack_conv(0)

    eye = one_hot(row == lane)

    def prepare(b, _):
        bmat = conv_ref[0, rows_of(b), 0:N]
        cmat = conv_ref[0, rows_of(b), N : 2 * N]
        bt_ref[b] = nt(eye, bmat).astype(BF16)
        begins = ds_ref[b][:, 0:1] - (first + b * SPAN)
        score_ref[b] = jnp.where((lane <= row) & (lane >= begins), nt(cmat, bmat), 0.0)
        return 0

    lax.fori_loop(0, blocks, prepare, 0)

    def state_copy(quad, group, owner, source_id):
        return pltpu.make_async_remote_copy(
            src_ref=sa.at[quad, group],
            dst_ref=ra.at[source_id],
            send_sem=as_sems.at[owner],
            recv_sem=ar_sems.at[source_id],
            device_id={"ctx": owner},
        )

    row16 = iota((TILE, SPAN), 0)
    for quad in range(quads):
        pack_conv(quad + 1)

        def local(b, state, quad=quad):
            sloc[quad, b] = state.astype(BF16)
            weight = spread(cols_ref[1, b], quad)
            weighted = (weight * conv_ref[quad + 1, rows_of(b), :].astype(F32)).astype(BF16)
            return state * spread(car_ref[b][0:1, :], quad) + mm(bt_ref[b], weighted)

        state = lax.fori_loop(0, blocks, local, jnp.zeros((N, WIDE), F32))
        sa[quad, :, :, 0:WIDE] = state.astype(BF16).reshape(groups, TILE, WIDE)
        decay = spread(shard_decay, quad, decay_at)
        decay = jnp.where(row16 < TILE // 2, decay[:, 0:SPAN], decay[:, SPAN:])
        rough = decay.astype(BF16).astype(F32)
        decay = jnp.where((row16 & (TILE // 4)) == 0, rough, decay - rough).astype(BF16)
        for group in range(groups):
            sa[quad, group, :, WIDE:] = decay

        def give(j, _, quad=quad):
            group = lax.rem(j + me, groups)
            owner = group * quads + quad

            @pl.when(owner != me)
            def _():
                state_copy(quad, group, owner, me).start()

            @pl.when(owner == me)
            def _():
                ra[me] = sa[quad, group]

            return 0

        lax.fori_loop(0, groups, give, 0)

    def inner(quad):
        def block(b, _):
            xs = conv_ref[quad + 1, rows_of(b), :]
            cmat = conv_ref[0, rows_of(b), N : 2 * N]
            cum_cols = cols_ref[0, b]
            gaps = rrow_ref[pl.ds(pl.multiple_of(b * heads, heads), heads), :]
            score = score_ref[b]
            x_float = xs.astype(F32)
            y = mm(cmat, sloc[quad, b]) * spread(cols_ref[2, b], quad)
            parts = []
            for pair in range(2):
                mixing = []
                for h in (4 * quad + 2 * pair, 4 * quad + 2 * pair + 1):
                    gap = jnp.minimum(cum_cols[:, h : h + 1] - gaps[h : h + 1, :], 60.0)
                    mixing.append((jnp.exp(gap) * score).astype(BF16))
                x_pair = x_float[:, pair * SPAN : (pair + 1) * SPAN]
                x_both = jnp.concatenate(
                    [jnp.where(low, x_pair, 0.0), jnp.where(low, 0.0, x_pair)], axis=0
                ).astype(BF16)
                h = 4 * quad + 2 * pair
                skip = jnp.where(low, skip_ref[h], skip_ref[h + 1])
                parts.append(mm(jnp.concatenate(mixing, axis=1), x_both) + skip * x_pair)
            ypart[quad, rows_of(b), :] = y + jnp.concatenate(parts, axis=1)
            es_ref[quad, rows_of(b), :] = spread(cols_ref[3, b], quad)
            return 0

        lax.fori_loop(0, blocks, block, 0)

    for quad in range(quads // 2):
        inner(quad)

    my_quad = lax.rem(me, quads)
    my_group = lax.div(me, quads)

    def back_copy(shard, quad, group, owner):
        return pltpu.make_async_remote_copy(
            src_ref=ret.at[shard],
            dst_ref=inc.at[quad, group],
            send_sem=rs_sems.at[shard],
            recv_sem=rr_sems.at[owner],
            device_id={"ctx": shard},
        )

    def scan(shard, state):
        ret[shard] = state.astype(BF16)

        @pl.when(shard != me)
        def _():
            back_copy(shard, my_quad, my_group, me).start()
            state_copy(0, 0, 0, shard).wait_recv()

        @pl.when(shard == me)
        def _():
            inc[my_quad, my_group] = state.astype(BF16)

        held = ra[shard].astype(F32)
        quarter = TILE // 4
        decay = jnp.concatenate(
            [
                held[0:1, WIDE:] + held[quarter : quarter + 1, WIDE:],
                held[2 * quarter : 2 * quarter + 1, WIDE:]
                + held[3 * quarter : 3 * quarter + 1, WIDE:],
            ],
            axis=1,
        )
        return state * decay + held[:, 0:WIDE]

    lax.fori_loop(0, nctx, scan, jnp.zeros((TILE, WIDE), F32))

    for quad in range(quads // 2, quads):
        inner(quad)

    def y_copy(quad, way):
        if way == 0:
            src, dst = pl.ds(2 * margin, margin), pl.ds(0, margin)
        else:
            src, dst = pl.ds(margin, margin), pl.ds(3 * margin, margin)
        return pltpu.make_async_remote_copy(
            src_ref=framed.at[quad, src],
            dst_ref=framed.at[quad, dst],
            send_sem=ys_sems.at[quad, way],
            recv_sem=yr_sems.at[quad, way],
            device_id={"ctx": around[way]},
        )

    for quad in range(quads):

        def arrive(group, _, quad=quad):
            owner = group * quads + quad

            @pl.when(owner != me)
            def _():
                back_copy(0, quad, group, owner).wait_recv()

            return 0

        lax.fori_loop(0, groups, arrive, 0)
        incoming = inc[quad].reshape(N, WIDE)
        fix = mm(conv_ref[0, :, N : 2 * N], incoming)
        framed[quad, margin : margin + tok, :] = (ypart[quad] + fix * es_ref[quad]).astype(BF16)
        for way in range(2):
            y_copy(quad, way).start()

    for i in range(blocks):
        across = jnp.broadcast_to(dest_ref[i : i + 1, :], (SPAN, SPAN)).T - first + margin
        for j in range(2 * blocks):
            q_ref[i * SPAN : (i + 1) * SPAN, j * SPAN : (j + 1) * SPAN] = one_hot(
                across == lane + j * SPAN
            )
    z_load.wait()
    for quad in range(quads):
        for way in range(2):
            y_copy(quad, way).wait_recv()
        y_rows = mm(q_ref[...], framed[quad])
        z_cols = z_ref[:, quad * WIDE : (quad + 1) * WIDE].astype(F32)
        gated = y_rows * half_silu(z_cols)
        ypart[quad] = gated
        square = gated * gated
        square = square[:, 0:SPAN] + square[:, SPAN:]
        ss_ref[...] = square if quad == 0 else ss_ref[...] + square

    def norm(i, _):
        inv = lax.rsqrt(
            jnp.sum(ss_ref[rows_of(i), :], axis=1, keepdims=True) * (1.0 / (quads * WIDE)) + 1e-05
        )
        for quad in range(quads):
            at = slice(quad * WIDE, (quad + 1) * WIDE)
            gain = gain_ref[:, at].astype(F32)
            normed_ref[rows_of(i), at] = (ypart[quad, rows_of(i), :] * inv * gain).astype(BF16)
        return 0

    lax.fori_loop(0, blocks, norm, 0)

    rows = out_ref.shape[0]
    rbuf[0] = jnp.zeros_like(rbuf[0])
    for load in w_loads:
        load.wait()

    def ring(step, way, sub):
        return pltpu.make_async_remote_copy(
            src_ref=sbuf.at[step, way, sub],
            dst_ref=rbuf.at[step + 1, way, sub],
            send_sem=send_sems.at[step, way, sub],
            recv_sem=recv_sems.at[step, way, sub],
            device_id={"head": hops[way]},
        )

    def one(step, _):
        for sub in range(SUBS):
            for way in range(2):
                if way == 0:
                    chunk = lax.rem(mz + 2 * nhead - 1 - step, nhead)
                else:
                    chunk = lax.rem(mz + 1 + step, nhead)
                at = (way * SUBS + sub) * width
                part = mm(
                    normed_ref[pl.ds(pl.multiple_of(chunk * rows, rows), rows), :],
                    w_ref[:, at : at + width],
                )

                @pl.when(step > 0)
                def _():
                    ring(step - 1, way, sub).wait_recv()

                total = (part + rbuf[step, way, sub].astype(F32)).astype(BF16)

                @pl.when(step < nhead - 1)
                def _():
                    sbuf[step, way, sub] = total
                    ring(step, way, sub).start()

                @pl.when(step == nhead - 1)
                def _():
                    out_ref[:, at : at + width] = total

        return 0

    lax.fori_loop(0, nhead, one, 0)

    def drain(step, _):
        for sub in range(SUBS):
            for way in range(2):
                ring(step, way, sub).wait_send()
        return 0

    lax.fori_loop(0, nhead - 1, drain, 0)
    for way in range(2):
        dt_copy(way).wait_send()
        for chunk in range(quads + 1):
            exchange(chunk, way).wait_send()
        for quad in range(quads):
            y_copy(quad, way).wait_send()

    def drain_states(other, _):
        @pl.when(other != me)
        def _():
            state_copy(0, 0, other, 0).wait_send()
            back_copy(other, 0, 0, 0).wait_send()

        return 0

    lax.fori_loop(0, nctx, drain_states, 0)


def per_device(
    x_in,
    z_in,
    bc_in,
    dt_in,
    destination,
    doc_lengths,
    conv_x,
    conv_bc,
    dt_bias,
    a_log,
    skip_gain,
    norm_gain,
    out_weight,
):
    nctx = lax.axis_size("ctx")
    nhead = lax.axis_size("head")
    tok, channels = x_in.shape
    heads = dt_in.shape[1]
    margin = tok // 2
    blocks = tok // SPAN
    quads = channels // WIDE
    groups = N // TILE
    rows = tok // nhead
    depth, wide = out_weight.shape
    width = wide // (2 * SUBS)
    dma = pltpu.SemaphoreType.DMA
    vmem = pl.BlockSpec(memory_space=pltpu.VMEM)
    smem = pl.BlockSpec(memory_space=pltpu.SMEM)
    anywhere = pl.BlockSpec(memory_space=pl.ANY)
    scratch = [
        pltpu.VMEM((quads, tok, WIDE), BF16),
        pltpu.VMEM((tok, channels), BF16),
        pltpu.VMEM((depth, wide), BF16),
        pltpu.VMEM((tok + TILE, tok), BF16),
        pltpu.VMEM((tok, tok), BF16),
        pltpu.VMEM((tok, 2 * tok), BF16),
        pltpu.VMEM((quads + 1, tok + TILE, WIDE), BF16),
        pltpu.VMEM((quads + 1, margin + TILE, WIDE), BF16),
        pltpu.VMEM((quads + 1, margin, WIDE), BF16),
        pltpu.VMEM((2, heads, margin), BF16),
        pltpu.VMEM((2, heads, margin), BF16),
        pltpu.VMEM((tok + TILE, WIDE), F32),
        pltpu.VMEM((quads + 1, tok, WIDE), BF16),
        pltpu.VMEM((4, blocks, SPAN, SPAN), F32),
        pltpu.VMEM((blocks, SPAN, SPAN), jnp.int32),
        pltpu.VMEM((blocks, 8, SPAN), F32),
        pltpu.VMEM((SPAN, SPAN), F32),
        pltpu.VMEM((blocks, SPAN, SPAN), F32),
        pltpu.VMEM((blocks, N, SPAN), BF16),
        pltpu.VMEM((quads, blocks, N, WIDE), BF16),
        pltpu.VMEM((quads, tok, WIDE), F32),
        pltpu.VMEM((quads, tok, WIDE), F32),
        pltpu.VMEM((quads, 2 * tok, WIDE), BF16),
        pltpu.VMEM((tok, SPAN), F32),
        pltpu.VMEM((tok, channels), BF16),
        pltpu.VMEM((quads, groups, TILE, WIDE + SPAN), BF16),
        pltpu.VMEM((nctx, TILE, WIDE + SPAN), BF16),
        pltpu.VMEM((nctx, TILE, WIDE), BF16),
        pltpu.VMEM((quads, groups, TILE, WIDE), BF16),
        pltpu.VMEM((nhead - 1, 2, SUBS, rows, width), BF16),
        pltpu.VMEM((nhead, 2, SUBS, rows, width), BF16),
        dma((quads,)),
        dma(()),
        dma((2, SUBS)),
        dma((quads + 1, 2)),
        dma((quads + 1, 2)),
        dma((2,)),
        dma((2,)),
        dma((nctx,)),
        dma((nctx,)),
        dma((nctx,)),
        dma((nctx,)),
        dma((quads, 2)),
        dma((quads, 2)),
        dma((nhead - 1, 2, SUBS)),
        dma((nhead - 1, 2, SUBS)),
    ]
    return pl.pallas_call(
        layer_kernel,
        out_shape=jax.ShapeDtypeStruct((rows, wide), BF16),
        in_specs=[
            anywhere,
            anywhere,
            vmem,
            vmem,
            vmem,
            smem,
            vmem,
            vmem,
            smem,
            smem,
            smem,
            vmem,
            anywhere,
        ],
        out_specs=vmem,
        scratch_shapes=scratch,
        compiler_params=pltpu.CompilerParams(
            collective_id=0, has_side_effects=True, vmem_limit_bytes=60 << 20
        ),
    )(
        x_in,
        z_in,
        bc_in,
        dt_in,
        destination.reshape(blocks, SPAN),
        doc_lengths,
        conv_x,
        conv_bc,
        dt_bias,
        a_log,
        skip_gain,
        norm_gain.reshape(1, channels),
        out_weight,
    )


def solution(mesh):
    placed = (
        P("ctx", "head"),
        P("ctx", "head"),
        P("ctx", "head"),
        P("ctx", "head"),
        P("ctx"),
        P(),
        P(None, "head"),
        P(None, "head"),
        P("head"),
        P("head"),
        P("head"),
        P("head"),
        P("head", None),
    )
    return jax.shard_map(
        per_device, mesh=mesh, in_specs=placed, out_specs=P(("ctx", "head"), None), check_vma=False
    )
```

```python
import jax
import jax.numpy as jnp
from jax import lax
from jax.experimental import pallas as pl
from jax.experimental.pallas import tpu as pltpu
from jax.sharding import PartitionSpec as P

N = 128
SPAN = 128
KCONV = 4
SUBS = 4
WIDE = 256
TILE = 16
LOG2E = 1.4426950408889634
F32 = jnp.float32
BF16 = jnp.bfloat16


def nt(a, b):
    return lax.dot_general(a, b, (((1,), (1,)), ((), ())), preferred_element_type=F32)


def mm(a, b):
    return jnp.dot(a, b, preferred_element_type=F32)


def iota(shape, dim):
    return lax.broadcasted_iota(jnp.int32, shape, dim)


def one_hot(hit):
    return jnp.where(hit, 1.0, 0.0).astype(BF16)


def half_silu(v):
    half = 0.5 * v
    return half + half * jnp.tanh(half)


def scope(name):
    return jax.named_scope(name)


def layer_kernel(
    x_hbm,
    z_hbm,
    bc_hbm,
    dt_ref,
    dest_ref,
    lengths_ref,
    convx_ref,
    convbc_ref,
    bias_ref,
    alog_ref,
    skip_ref,
    gain_ref,
    w_hbm,
    out_ref,
    bc_ref,
    x_ref,
    z_ref,
    w_ref,
    pout_ref,
    home_ref,
    qhome_ref,
    qaway_ref,
    snd,
    rcvp,
    rcvn,
    dts,
    dtr,
    xext,
    mask_ref,
    conv_ref,
    cols_ref,
    part_ref,
    head_ref,
    ds_ref,
    car_ref,
    rrow_ref,
    score_ref,
    bt_ref,
    sloc,
    ypart,
    es_ref,
    y_home,
    y_away,
    ss_ref,
    normed_ref,
    sa,
    ra,
    da,
    rd,
    ret,
    inc,
    sbuf,
    rbuf,
    bc_sem,
    x_sems,
    z_sem,
    w_sems,
    xs_sems,
    xr_sems,
    ds_sems,
    dr_sems,
    as_sems,
    ar_sems,
    ads_sems,
    adr_sems,
    rs_sems,
    rr_sems,
    ys_sems,
    yr_sems,
    send_sems,
    recv_sems,
):
    nctx = lax.axis_size("ctx")
    nhead = lax.axis_size("head")
    me = lax.axis_index("ctx")
    mz = lax.axis_index("head")
    tok = bc_ref.shape[0]
    margin = tok // 2
    blocks = tok // SPAN
    quads = x_ref.shape[0]
    groups = SPAN // TILE
    heads = dt_ref.shape[0]
    docs = lengths_ref.shape[0]
    first = me * tok
    around = (lax.rem(me + 1, nctx), lax.rem(me + nctx - 1, nctx))
    hops = (lax.rem(mz + 1, nhead), lax.rem(mz + nhead - 1, nhead))

    barrier = pltpu.get_barrier_semaphore()

    def greet(j, _):
        pl.semaphore_signal(barrier, inc=1, device_id={"ctx": lax.rem(me + j, nctx)})
        return 0

    lax.fori_loop(1, nctx, greet, 0)
    for hop in hops:
        pl.semaphore_signal(barrier, inc=1, device_id={"head": hop})

    bc_load = pltpu.make_async_copy(bc_hbm, bc_ref, bc_sem)
    bc_load.start()
    x_loads = [
        pltpu.make_async_copy(x_hbm.at[:, pl.ds(c * WIDE, WIDE)], x_ref.at[c], x_sems.at[c])
        for c in range(quads)
    ]
    z_load = pltpu.make_async_copy(z_hbm, z_ref, z_sem)
    wide = w_ref.shape[1]
    width = wide // (2 * SUBS)
    w_loads = []
    for sub in range(SUBS):
        for way in range(2):
            w_cols = pl.ds((way * SUBS + sub) * width, width)
            w_loads.append(
                pltpu.make_async_copy(w_hbm.at[:, w_cols], w_ref.at[:, w_cols], w_sems.at[way, sub])
            )

    rel_row = jnp.concatenate([dest_ref[i : i + 1, :] for i in range(blocks)], axis=1) - first
    slot = iota((margin + TILE, tok), 0)
    goal = jnp.where(slot < margin, slot + tok, slot + (tok - TILE - margin))
    pout_ref[0 : margin + TILE, :] = one_hot(goal == rel_row)
    pout_ref[margin + TILE :, :] = one_hot(iota((margin, tok), 0) - margin == rel_row)

    def exchange(chunk, way):
        if way == 0:
            src, dst = snd.at[chunk, pl.ds(0, margin + TILE)], rcvp.at[chunk]
        else:
            src, dst = snd.at[chunk, pl.ds(margin + TILE, margin)], rcvn.at[chunk]
        return pltpu.make_async_remote_copy(
            src_ref=src,
            dst_ref=dst,
            send_sem=xs_sems.at[chunk, way],
            recv_sem=xr_sems.at[chunk, way],
            device_id={"ctx": around[way]},
        )

    def dt_copy(way):
        return pltpu.make_async_remote_copy(
            src_ref=dts.at[way],
            dst_ref=dtr.at[way],
            send_sem=ds_sems.at[way],
            recv_sem=dr_sems.at[way],
            device_id={"ctx": around[way]},
        )

    def source(chunk):
        return bc_ref[...] if chunk == 0 else x_ref[chunk - 1]

    dt_rows = dt_ref[...]
    dts[0] = nt(dt_rows, pout_ref[0:margin, :]).astype(BF16)
    dts[1] = nt(dt_rows, pout_ref[margin + TILE :, :]).astype(BF16)
    bc_load.wait()
    for load in x_loads:
        load.start()
    snd[0] = mm(pout_ref[...], source(0)).astype(BF16)

    pl.semaphore_wait(barrier, nctx + 1)
    for way in range(2):
        dt_copy(way).start()
    for way in range(2):
        exchange(0, way).start()
    for chunk in range(1, quads + 1):
        x_loads[chunk - 1].wait()
        snd[chunk] = mm(pout_ref[...], source(chunk)).astype(BF16)
        for way in range(2):
            exchange(chunk, way).start()

    z_load.start()
    for load in w_loads:
        load.start()

    home_ref[...] = one_hot(iota((tok, tok), 0) == rel_row)

    row16 = iota((heads, SPAN), 0)
    bias = jnp.zeros((heads, SPAN), F32)
    alog = jnp.zeros((heads, SPAN), F32)
    for h in range(heads):
        bias = jnp.where(row16 == h, bias_ref[h], bias)
        alog = jnp.where(row16 == h, alog_ref[h], alog)
    neg_rate = -jnp.exp(alog)
    for way in range(2):
        dt_copy(way).wait_recv()
    dt_home = nt(dt_rows, home_ref[...])
    home_first = mm(home_ref[...], source(0))
    dt_raw = dt_home + jnp.concatenate([dtr[0].astype(F32), dtr[1].astype(F32)], axis=1)
    steps = []
    rates = []
    for b in range(blocks):
        logit = dt_raw[:, b * SPAN : (b + 1) * SPAN] + bias
        step = jnp.maximum(logit, 0.0) + jnp.log1p(jnp.exp(-jnp.abs(logit)))
        steps.append(step)
        rates.append(step * neg_rate)
    spare = SPAN - blocks * heads
    steps = jnp.concatenate(steps + [jnp.ones((spare, SPAN), F32)], axis=0)
    rates = jnp.concatenate(rates + [jnp.zeros((spare, SPAN), F32)], axis=0)
    row = iota((SPAN, SPAN), 0)
    lane = iota((SPAN, SPAN), 1)
    upper = jnp.where(row <= lane, 1.0, 0.0)
    cum_rows = jnp.dot(
        rates, upper, precision=lax.Precision.HIGHEST, preferred_element_type=F32
    )
    rrow_ref[...] = LOG2E * (cum_rows - jnp.log(steps))
    cum = cum_rows.T
    step_cols = steps.T
    shift = heads.bit_length() - 1
    lane_block = lax.shift_right_logical(lane, shift)
    row_block = lax.shift_right_logical(row, shift)
    block_start = first + lane_block * SPAN
    pos = block_start + row
    doc_start = jnp.zeros((SPAN, SPAN), jnp.int32)
    begin = jnp.int32(0)
    for d in range(docs):
        doc_start = jnp.where(pos >= begin, begin, doc_start)
        begin = begin + lengths_ref[d]
    last_start = doc_start[SPAN - 1 : SPAN, :]
    last = cum[SPAN - 1 : SPAN, :]
    same_head = (lane & (heads - 1)) == (row & (heads - 1))
    before = jnp.where(same_head & (row_block < lane_block), 1.0, 0.0)
    offset = jnp.dot(
        jnp.broadcast_to(last, (8, SPAN)),
        before,
        precision=lax.Precision.HIGHEST,
        preferred_element_type=F32,
    )[0:1, :]
    w_cols = jnp.where(pos >= last_start, jnp.exp(last - cum) * step_cols, 0.0)
    entry = jnp.where(doc_start < block_start, jnp.exp(cum), 0.0)
    entry_shard = jnp.where(doc_start < first, jnp.exp(cum + offset), 0.0)
    carried = jnp.where(last_start < block_start[0:1, :], jnp.exp(last), 0.0)
    shard_decay = jnp.where(last_start < first, jnp.exp(last + offset), 0.0)
    carried = jnp.broadcast_to(carried, (8, SPAN))
    for b in range(blocks):
        turn = (SPAN - b * heads) % SPAN
        cols_ref[b] = pltpu.roll(LOG2E * cum, turn, 1) if turn else LOG2E * cum
        for kind, array in enumerate((w_cols, entry, entry_shard)):
            array = pltpu.roll(array, turn, 1) if turn else array
            rough = array.astype(BF16)
            fine = (array - rough.astype(F32)).astype(BF16)
            part_ref[kind, b * SPAN : (b + 1) * SPAN, 0:SPAN] = rough
            part_ref[kind, b * SPAN : (b + 1) * SPAN, SPAN:] = fine
        ds_ref[b] = pltpu.roll(doc_start, turn, 1) if turn else doc_start
        car_ref[b] = pltpu.roll(carried, turn, 1) if turn else carried
    for quad in range(quads):
        key = iota((2 * SPAN, WIDE), 0) & (SPAN - 1)
        head = lax.shift_right_logical(iota((2 * SPAN, WIDE), 1), 6) + 4 * quad
        head_ref[quad] = one_hot(key == head)
    decay_at = (blocks - 1) * heads

    low = iota((1, SPAN), 1) < SPAN // 2

    def spread(cols, quad, at=0):
        parts = []
        for pair in range(2):
            h = at + 4 * quad + 2 * pair
            parts.append(jnp.where(low, cols[:, h : h + 1], cols[:, h + 1 : h + 2]))
        return jnp.concatenate(parts, axis=1)

    def rows_of(b):
        return pl.ds(pl.multiple_of(b * SPAN, SPAN), SPAN)

    def pack_conv(chunk, home=None):
        if home is None:
            home = mm(home_ref[...], source(chunk))
        for way in range(2):
            exchange(chunk, way).wait_recv()
        if chunk == 0:
            taps = convbc_ref[...].astype(F32)
        else:
            taps = convx_ref[:, (chunk - 1) * WIDE : chunk * WIDE].astype(F32)
        for half in range(2):
            at = slice(half * SPAN, (half + 1) * SPAN)
            xext[half, 0:TILE, :] = rcvp[chunk, margin : margin + TILE, at].astype(F32) + snd[
                chunk, tok : tok + TILE, at
            ].astype(F32)
            xext[half, TILE : TILE + margin, :] = home[0:margin, at] + rcvp[
                chunk, 0:margin, at
            ].astype(F32)
            xext[half, TILE + margin :, :] = home[margin:, at] + rcvn[chunk, :, at].astype(F32)
        with scope("conv"):
            for half in range(2):
                at = slice(half * SPAN, (half + 1) * SPAN)
                for b in range(blocks):
                    base = b * SPAN + TILE
                    total = taps[3:4, at] * xext[half, base : base + SPAN, :]
                    for tap in range(KCONV - 1):
                        back = KCONV - 1 - tap
                        piece = xext[half, base - back : base - back + SPAN, :]
                        usable = mask_ref[tap, b * SPAN : (b + 1) * SPAN, :]
                        total = total + taps[tap : tap + 1, at] * (usable * piece)
                    conv_ref[chunk, b * SPAN : (b + 1) * SPAN, at] = half_silu(total).astype(BF16)

    for b in range(blocks):
        begins = jnp.broadcast_to(ds_ref[b][:, 0:1], (SPAN, SPAN)) - (first + b * SPAN) - row
        for tap in range(KCONV - 1):
            usable = jnp.where(begins <= tap + 1 - KCONV, 1.0, 0.0)
            mask_ref[tap, b * SPAN : (b + 1) * SPAN, :] = usable

    pack_conv(0, home_first)

    eye = one_hot(row == lane)

    def prepare(b, _):
        bmat = conv_ref[0, rows_of(b), 0:N]
        cmat = conv_ref[0, rows_of(b), N : 2 * N]
        bt_ref[b] = nt(eye, bmat).astype(BF16)
        begins = ds_ref[b][:, 0:1] - (first + b * SPAN)
        score_ref[b] = jnp.where((lane <= row) & (lane >= begins), nt(cmat, bmat), 0.0)
        return 0

    lax.fori_loop(0, blocks, prepare, 0, unroll=True)

    def state_copy(quad, group, owner, source_id):
        return pltpu.make_async_remote_copy(
            src_ref=sa.at[quad, group],
            dst_ref=ra.at[source_id],
            send_sem=as_sems.at[owner],
            recv_sem=ar_sems.at[source_id],
            device_id={"ctx": owner},
        )

    def decay_copy(quad, owner, source_id):
        return pltpu.make_async_remote_copy(
            src_ref=da.at[quad, pl.ds(0, 1)],
            dst_ref=rd.at[source_id, pl.ds(0, 1)],
            send_sem=ads_sems.at[owner],
            recv_sem=adr_sems.at[source_id],
            device_id={"ctx": owner},
        )

    def shard_state(quad):
        weights = mm(part_ref[0], head_ref[quad])
        state = jnp.zeros((N, WIDE), F32)
        for b in range(blocks):
            sloc[quad, b] = state.astype(BF16)
            weight = weights[b * SPAN : (b + 1) * SPAN]
            x_float = conv_ref[quad + 1, b * SPAN : (b + 1) * SPAN, :].astype(F32)
            inner_sum = mm(bt_ref[b], (weight * x_float).astype(BF16))
            state = state * spread(car_ref[b][0:1, :], quad) + inner_sum

        sa[quad] = state.astype(BF16).reshape(groups, TILE, WIDE)
        da[quad] = jnp.broadcast_to(spread(shard_decay, quad, decay_at), (8, WIDE))

        def give(j, _):
            group = lax.rem(j + me, groups)
            owner = group * quads + quad

            @pl.when(owner != me)
            def _():
                state_copy(quad, group, owner, me).start()
                decay_copy(quad, owner, me).start()

            @pl.when(owner == me)
            def _():
                ra[me] = sa[quad, group]
                rd[me] = da[quad]

            return 0

        lax.fori_loop(0, groups, give, 0)

    def inner(quad):
        entries = mm(part_ref[1], head_ref[quad])
        es_ref[quad] = mm(part_ref[2], head_ref[quad])

        for b in range(blocks):
            xs = conv_ref[quad + 1, rows_of(b), :]
            cmat = conv_ref[0, rows_of(b), N : 2 * N]
            cum_cols = cols_ref[b]
            gaps = rrow_ref[b * heads : (b + 1) * heads, :]
            score = score_ref[b]
            x_float = xs.astype(F32)
            y = mm(cmat, sloc[quad, b]) * entries[b * SPAN : (b + 1) * SPAN]
            parts = []
            for pair in range(2):
                mixing = []
                for h in (4 * quad + 2 * pair, 4 * quad + 2 * pair + 1):
                    gap = jnp.minimum(cum_cols[:, h : h + 1] - gaps[h : h + 1, :], 80.0)
                    mixing.append((jnp.exp2(gap) * score).astype(BF16))
                x_pair = x_float[:, pair * SPAN : (pair + 1) * SPAN]
                x_both = jnp.concatenate(
                    [jnp.where(low, x_pair, 0.0), jnp.where(low, 0.0, x_pair)], axis=0
                ).astype(BF16)
                h = 4 * quad + 2 * pair
                skip = jnp.where(low, skip_ref[h], skip_ref[h + 1])
                parts.append(mm(jnp.concatenate(mixing, axis=1), x_both) + skip * x_pair)
            ypart[quad, rows_of(b), :] = y + jnp.concatenate(parts, axis=1)

    my_quad = lax.rem(me, quads)
    my_group = lax.div(me, quads)

    def back_copy(shard, quad, group, owner):
        return pltpu.make_async_remote_copy(
            src_ref=ret.at[shard],
            dst_ref=inc.at[quad, group],
            send_sem=rs_sems.at[shard],
            recv_sem=rr_sems.at[owner],
            device_id={"ctx": shard},
        )

    def scan(shard, state):
        ret[shard] = state.astype(BF16)

        @pl.when(shard != me)
        def _():
            back_copy(shard, my_quad, my_group, me).start()
            state_copy(0, 0, 0, shard).wait_recv()
            decay_copy(0, 0, shard).wait_recv()

        @pl.when(shard == me)
        def _():
            inc[my_quad, my_group] = state.astype(BF16)

        return state * rd[shard, 0:1, :] + ra[shard].astype(F32)

    def scan_slice(quad):
        @pl.when(my_quad == quad)
        def _():
            lax.fori_loop(0, nctx, scan, jnp.zeros((TILE, WIDE), F32))

    def y_copy(quad, way):
        if way == 0:
            src, dst = pl.ds(margin, margin), pl.ds(0, margin)
        else:
            src, dst = pl.ds(0, margin), pl.ds(margin, margin)
        return pltpu.make_async_remote_copy(
            src_ref=y_home.at[quad, src],
            dst_ref=y_away.at[quad, dst],
            send_sem=ys_sems.at[quad, way],
            recv_sem=yr_sems.at[quad, way],
            device_id={"ctx": around[way]},
        )

    def finish(quad):
        def arrive(group, _):
            owner = group * quads + quad

            @pl.when(owner != me)
            def _():
                back_copy(0, quad, group, owner).wait_recv()

            return 0

        lax.fori_loop(0, groups, arrive, 0)
        incoming = inc[quad].reshape(N, WIDE)
        fix = mm(conv_ref[0, :, N : 2 * N], incoming)
        y_home[quad] = (ypart[quad] + fix * es_ref[quad]).astype(BF16)
        for way in range(2):
            y_copy(quad, way).start()

    for quad in range(quads):
        with scope("pack%d" % quad):
            pack_conv(quad + 1)
        with scope("state%d" % quad):
            shard_state(quad)
        if quad == 2:
            with scope("inner0"):
                inner(0)
    with scope("scan"):
        scan_slice(0)
        scan_slice(1)
    with scope("inner1"):
        inner(1)
        inner(2)
    with scope("scan2"):
        scan_slice(2)
    with scope("inner3"):
        inner(3)
    with scope("scan3"):
        scan_slice(3)
    with scope("finish0"):
        finish(0)
    with scope("finish1"):
        finish(1)
    with scope("finish2"):
        finish(2)
    with scope("finish3"):
        finish(3)

    for i in range(blocks):
        across = jnp.broadcast_to(dest_ref[i : i + 1, :], (SPAN, SPAN)).T - first
        beside = across + jnp.where(across < 0, margin, -margin)
        beside = jnp.where((across < 0) | (across >= tok), beside, -1)
        for j in range(blocks):
            at = slice(i * SPAN, (i + 1) * SPAN), slice(j * SPAN, (j + 1) * SPAN)
            qhome_ref[at] = one_hot(across == lane + j * SPAN)
            qaway_ref[at] = one_hot(beside == lane + j * SPAN)
    for quad in range(quads):
        ypart[quad] = mm(qhome_ref[...], y_home[quad])
    z_load.wait()
    for quad in range(quads):
        for way in range(2):
            y_copy(quad, way).wait_recv()
        y_rows = ypart[quad] + mm(qaway_ref[...], y_away[quad])
        z_cols = z_ref[:, quad * WIDE : (quad + 1) * WIDE].astype(F32)
        gated = y_rows * half_silu(z_cols)
        ypart[quad] = gated
        square = gated * gated
        square = square[:, 0:SPAN] + square[:, SPAN:]
        ss_ref[...] = square if quad == 0 else ss_ref[...] + square

    def norm(i, _):
        inv = lax.rsqrt(
            jnp.sum(ss_ref[rows_of(i), :], axis=1, keepdims=True) * (1.0 / (quads * WIDE)) + 1e-05
        )
        for quad in range(quads):
            at = slice(quad * WIDE, (quad + 1) * WIDE)
            gain = jnp.concatenate([gain_ref[2 * quad + i : 2 * quad + i + 1, :] for i in range(2)], axis=1)
            gain = gain.astype(F32)
            normed_ref[rows_of(i), at] = (ypart[quad, rows_of(i), :] * inv * gain).astype(BF16)
        return 0

    lax.fori_loop(0, blocks, norm, 0)

    rows = out_ref.shape[0]
    rbuf[0] = jnp.zeros_like(rbuf[0])
    for load in w_loads:
        load.wait()

    def ring(step, way, sub):
        return pltpu.make_async_remote_copy(
            src_ref=sbuf.at[step, way, sub],
            dst_ref=rbuf.at[step + 1, way, sub],
            send_sem=send_sems.at[step, way, sub],
            recv_sem=recv_sems.at[step, way, sub],
            device_id={"head": hops[way]},
        )

    def one(step, _):
        for sub in range(SUBS):
            for way in range(2):
                if way == 0:
                    chunk = lax.rem(mz + 2 * nhead - 1 - step, nhead)
                else:
                    chunk = lax.rem(mz + 1 + step, nhead)
                at = (way * SUBS + sub) * width
                part = mm(
                    normed_ref[pl.ds(pl.multiple_of(chunk * rows, rows), rows), :],
                    w_ref[:, at : at + width],
                )

                @pl.when(step > 0)
                def _():
                    ring(step - 1, way, sub).wait_recv()

                total = (part + rbuf[step, way, sub].astype(F32)).astype(BF16)

                @pl.when(step < nhead - 1)
                def _():
                    sbuf[step, way, sub] = total
                    ring(step, way, sub).start()

                @pl.when(step == nhead - 1)
                def _():
                    out_ref[:, at : at + width] = total

        return 0

    lax.fori_loop(0, nhead, one, 0)

    def drain(step, _):
        for sub in range(SUBS):
            for way in range(2):
                ring(step, way, sub).wait_send()
        return 0

    lax.fori_loop(0, nhead - 1, drain, 0)
    for way in range(2):
        dt_copy(way).wait_send()
        for chunk in range(quads + 1):
            exchange(chunk, way).wait_send()
        for quad in range(quads):
            y_copy(quad, way).wait_send()

    def drain_states(other, _):
        @pl.when(other != me)
        def _():
            state_copy(0, 0, other, 0).wait_send()
            decay_copy(0, other, 0).wait_send()
            back_copy(other, 0, 0, 0).wait_send()

        return 0

    lax.fori_loop(0, nctx, drain_states, 0)


def per_device(
    x_in,
    z_in,
    bc_in,
    dt_in,
    destination,
    doc_lengths,
    conv_x,
    conv_bc,
    dt_bias,
    a_log,
    skip_gain,
    norm_gain,
    out_weight,
):
    nctx = lax.axis_size("ctx")
    nhead = lax.axis_size("head")
    tok, channels = x_in.shape
    heads = dt_in.shape[1]
    bc_width = bc_in.shape[1]
    margin = tok // 2
    blocks = tok // SPAN
    quads = channels // WIDE
    groups = N // TILE
    rows = tok // nhead
    depth, wide = out_weight.shape
    width = wide // (2 * SUBS)
    dma = pltpu.SemaphoreType.DMA
    vmem = pl.BlockSpec(memory_space=pltpu.VMEM)
    smem = pl.BlockSpec(memory_space=pltpu.SMEM)
    anywhere = pl.BlockSpec(memory_space=pl.ANY)
    scratch = [
        pltpu.VMEM((tok, bc_width), BF16),
        pltpu.VMEM((quads, tok, WIDE), BF16),
        pltpu.VMEM((tok, channels), BF16),
        pltpu.VMEM((depth, wide), BF16),
        pltpu.VMEM((tok + TILE, tok), BF16),
        pltpu.VMEM((tok, tok), BF16),
        pltpu.VMEM((tok, tok), BF16),
        pltpu.VMEM((tok, tok), BF16),
        pltpu.VMEM((quads + 1, tok + TILE, WIDE), BF16),
        pltpu.VMEM((quads + 1, margin + TILE, WIDE), BF16),
        pltpu.VMEM((quads + 1, margin, WIDE), BF16),
        pltpu.VMEM((2, heads, margin), BF16),
        pltpu.VMEM((2, heads, margin), BF16),
        pltpu.VMEM((2, tok + TILE, SPAN), F32),
        pltpu.VMEM((KCONV - 1, tok, SPAN), F32),
        pltpu.VMEM((quads + 1, tok, WIDE), BF16),
        pltpu.VMEM((blocks, SPAN, SPAN), F32),
        pltpu.VMEM((3, tok, 2 * SPAN), BF16),
        pltpu.VMEM((quads, 2 * SPAN, WIDE), BF16),
        pltpu.VMEM((blocks, SPAN, SPAN), jnp.int32),
        pltpu.VMEM((blocks, 8, SPAN), F32),
        pltpu.VMEM((SPAN, SPAN), F32),
        pltpu.VMEM((blocks, SPAN, SPAN), F32),
        pltpu.VMEM((blocks, N, SPAN), BF16),
        pltpu.VMEM((quads, blocks, N, WIDE), BF16),
        pltpu.VMEM((quads, tok, WIDE), F32),
        pltpu.VMEM((quads, tok, WIDE), F32),
        pltpu.VMEM((quads, tok, WIDE), BF16),
        pltpu.VMEM((quads, tok, WIDE), BF16),
        pltpu.VMEM((tok, SPAN), F32),
        pltpu.VMEM((tok, channels), BF16),
        pltpu.VMEM((quads, groups, TILE, WIDE), BF16),
        pltpu.VMEM((nctx, TILE, WIDE), BF16),
        pltpu.VMEM((quads, 8, WIDE), F32),
        pltpu.VMEM((nctx, 8, WIDE), F32),
        pltpu.VMEM((nctx, TILE, WIDE), BF16),
        pltpu.VMEM((quads, groups, TILE, WIDE), BF16),
        pltpu.VMEM((nhead - 1, 2, SUBS, rows, width), BF16),
        pltpu.VMEM((nhead, 2, SUBS, rows, width), BF16),
        dma(()),
        dma((quads,)),
        dma(()),
        dma((2, SUBS)),
        dma((quads + 1, 2)),
        dma((quads + 1, 2)),
        dma((2,)),
        dma((2,)),
        dma((nctx,)),
        dma((nctx,)),
        dma((nctx,)),
        dma((nctx,)),
        dma((nctx,)),
        dma((nctx,)),
        dma((quads, 2)),
        dma((quads, 2)),
        dma((nhead - 1, 2, SUBS)),
        dma((nhead - 1, 2, SUBS)),
    ]
    return pl.pallas_call(
        layer_kernel,
        out_shape=pltpu.VMEM((rows, wide), BF16),
        in_specs=[
            anywhere,
            anywhere,
            anywhere,
            vmem,
            vmem,
            smem,
            vmem,
            vmem,
            smem,
            smem,
            smem,
            vmem,
            anywhere,
        ],
        out_specs=vmem,
        scratch_shapes=scratch,
        compiler_params=pltpu.CompilerParams(
            collective_id=0, has_side_effects=True, vmem_limit_bytes=60 << 20
        ),
    )(
        x_in,
        z_in,
        bc_in,
        dt_in.T,
        destination.reshape(blocks, SPAN),
        doc_lengths,
        conv_x,
        conv_bc,
        dt_bias,
        a_log,
        skip_gain,
        norm_gain.reshape(channels // SPAN, SPAN),
        out_weight,
    )


def solution(mesh):
    placed = (
        P("ctx", "head"),
        P("ctx", "head"),
        P("ctx", "head"),
        P("ctx", "head"),
        P("ctx"),
        P(),
        P(None, "head"),
        P(None, "head"),
        P("head"),
        P("head"),
        P("head"),
        P("head"),
        P("head", None),
    )
    return jax.shard_map(
        per_device, mesh=mesh, in_specs=placed, out_specs=P(("ctx", "head"), None), check_vma=False
    )
```

```python
import jax
import jax.numpy as jnp
from jax import lax
from jax.experimental import pallas as pl
from jax.experimental.pallas import tpu as pltpu
from jax.sharding import PartitionSpec as P

N = 128
SPAN = 128
KCONV = 4
SUBS = 4
WIDE = 256
TILE = 16
LOG2E = 1.4426950408889634
F32 = jnp.float32
BF16 = jnp.bfloat16


def nt(a, b):
    return lax.dot_general(a, b, (((1,), (1,)), ((), ())), preferred_element_type=F32)


def mm(a, b):
    return jnp.dot(a, b, preferred_element_type=F32)


def iota(shape, dim):
    return lax.broadcasted_iota(jnp.int32, shape, dim)


def one_hot(hit):
    return jnp.where(hit, 1.0, 0.0).astype(BF16)


def half_silu(v):
    half = 0.5 * v
    return half + half * jnp.tanh(half)


def scope(name):
    return jax.named_scope(name)


def layer_kernel(
    x_hbm,
    z_hbm,
    bc_hbm,
    dt_hbm,
    dest_hbm,
    lengths_ref,
    convx_hbm,
    convbc_hbm,
    bias_ref,
    alog_ref,
    skip_ref,
    gain_hbm,
    w_hbm,
    out_ref,
    dt_ref,
    dest_ref,
    convx_ref,
    convbc_ref,
    gain_ref,
    bc_ref,
    x_ref,
    z_ref,
    w_ref,
    pout_ref,
    home_ref,
    qhome_ref,
    qaway_ref,
    snd,
    rcvp,
    rcvn,
    dts,
    dtr,
    xext,
    mask_ref,
    conv_ref,
    cols_ref,
    part_ref,
    head_ref,
    ds_ref,
    car_ref,
    rrow_ref,
    score_ref,
    bt_ref,
    sloc,
    ypart,
    es_ref,
    y_home,
    y_away,
    ss_ref,
    normed_ref,
    sa,
    ra,
    da,
    rd,
    ret,
    inc,
    sbuf,
    rbuf,
    small_sems,
    bc_sem,
    x_sems,
    z_sem,
    w_sem,
    xs_sems,
    xr_sems,
    ds_sems,
    dr_sems,
    as_sem,
    ar_sem,
    ads_sem,
    adr_sem,
    rs_sem,
    rr_sems,
    ys_sems,
    yr_sems,
    send_sems,
    recv_sems,
):
    nctx = lax.axis_size("ctx")
    nhead = lax.axis_size("head")
    me = lax.axis_index("ctx")
    mz = lax.axis_index("head")
    tok = bc_ref.shape[0]
    margin = tok // 2
    blocks = tok // SPAN
    quads = x_ref.shape[0]
    groups = SPAN // TILE
    heads = dt_ref.shape[0]
    docs = lengths_ref.shape[0]
    first = me * tok
    around = (lax.rem(me + 1, nctx), lax.rem(me + nctx - 1, nctx))
    hops = (lax.rem(mz + 1, nhead), lax.rem(mz + nhead - 1, nhead))

    barrier = pltpu.get_barrier_semaphore()

    def greet(j, _):
        pl.semaphore_signal(barrier, inc=1, device_id={"ctx": lax.rem(me + j, nctx)})
        return 0

    lax.fori_loop(1, nctx, greet, 0, unroll=True)
    for hop in hops:
        pl.semaphore_signal(barrier, inc=1, device_id={"head": hop})

    may_send = (me != nctx - 1, me != 0)
    may_get = (me != 0, me != nctx - 1)

    def wait_for(ref, sem):
        pltpu.make_async_copy(ref, ref, sem).wait()

    small_loads = [
        pltpu.make_async_copy(src, dst, small_sems.at[i])
        for i, (src, dst) in enumerate(
            (
                (dest_hbm, dest_ref),
                (dt_hbm, dt_ref),
                (convx_hbm, convx_ref),
                (convbc_hbm, convbc_ref),
                (gain_hbm, gain_ref),
            )
        )
    ]
    bc_load = pltpu.make_async_copy(bc_hbm, bc_ref, bc_sem)
    small_loads[0].start()
    bc_load.start()
    for load in small_loads[1:]:
        load.start()

    x_loads = [
        pltpu.make_async_copy(x_hbm.at[:, pl.ds(c * WIDE, WIDE)], x_ref.at[c], x_sems.at[c])
        for c in range(quads)
    ]
    z_load = pltpu.make_async_copy(z_hbm, z_ref, z_sem)
    wide = w_ref.shape[1]
    rows = out_ref.shape[0]
    width = wide // (2 * SUBS)
    w_loads = []
    for sub in range(SUBS):
        for way in range(2):
            w_cols = pl.ds((way * SUBS + sub) * width, width)
            w_loads.append(
                pltpu.make_async_copy(w_hbm.at[:, w_cols], w_ref.at[:, w_cols], w_sem)
            )

    small_loads[0].wait()
    rel_row = jnp.concatenate([dest_ref[i : i + 1, :] for i in range(blocks)], axis=1) - first
    slot = iota((margin + TILE, tok), 0)
    goal = jnp.where(slot < margin, slot + tok, slot + (tok - TILE - margin))
    pout_ref[0 : margin + TILE, :] = one_hot(goal == rel_row)
    pout_ref[margin + TILE :, :] = one_hot(iota((margin, tok), 0) - margin == rel_row)

    def exchange(chunk, way):
        if way == 0:
            src, dst = snd.at[chunk, pl.ds(0, margin + TILE)], rcvp.at[chunk]
        else:
            src, dst = snd.at[chunk, pl.ds(margin + TILE, margin)], rcvn.at[chunk]
        return pltpu.make_async_remote_copy(
            src_ref=src,
            dst_ref=dst,
            send_sem=xs_sems.at[way],
            recv_sem=xr_sems.at[chunk, way],
            device_id={"ctx": around[way]},
        )

    def dt_copy(way):
        return pltpu.make_async_remote_copy(
            src_ref=dts.at[way],
            dst_ref=dtr.at[way],
            send_sem=ds_sems.at[way],
            recv_sem=dr_sems.at[way],
            device_id={"ctx": around[way]},
        )

    def source(chunk):
        return bc_ref[...] if chunk == 0 else x_ref[chunk - 1]

    for load in small_loads[1:]:
        load.wait()
    dt_rows = dt_ref[...]
    dts[0] = nt(dt_rows, pout_ref[0:margin, :]).astype(BF16)
    dts[1] = nt(dt_rows, pout_ref[margin + TILE :, :]).astype(BF16)
    bc_load.wait()
    for load in x_loads:
        load.start()
    snd[0] = mm(pout_ref[...], source(0)).astype(BF16)

    pl.semaphore_wait(barrier, nctx + 1)
    for way in range(2):

        @pl.when(may_send[way])
        def _():
            dt_copy(way).start()
            exchange(0, way).start()


    def send_out(chunk):
        x_loads[chunk - 1].wait()
        snd[chunk] = mm(pout_ref[...], source(chunk)).astype(BF16)
        for way in range(2):

            @pl.when(may_send[way])
            def _():
                exchange(chunk, way).start()


    send_out(1)
    send_out(2)

    z_load.start()
    for load in w_loads:
        load.start()

    home_ref[...] = one_hot(iota((tok, tok), 0) == rel_row)
    for way in range(2):

        @pl.when(jnp.logical_not(may_get[way]))
        def _():
            landing = (rcvp, rcvn)[way]
            landing[...] = jnp.zeros_like(landing)
            dtr[way] = jnp.zeros_like(dtr[way])
            at = pl.ds(way * margin, margin)
            y_away[:, at, :] = jnp.zeros((quads, margin, WIDE), BF16)


    row16 = iota((heads, SPAN), 0)
    bias = jnp.zeros((heads, SPAN), F32)
    alog = jnp.zeros((heads, SPAN), F32)
    for h in range(heads):
        bias = jnp.where(row16 == h, bias_ref[h], bias)
        alog = jnp.where(row16 == h, alog_ref[h], alog)
    neg_rate = -jnp.exp(alog)
    for way in range(2):

        @pl.when(may_get[way])
        def _():
            dt_copy(way).wait_recv()

    dt_home = nt(dt_rows, home_ref[...])
    home_first = mm(home_ref[...], source(0))
    dt_raw = dt_home + jnp.concatenate([dtr[0].astype(F32), dtr[1].astype(F32)], axis=1)
    steps = []
    rates = []
    for b in range(blocks):
        logit = dt_raw[:, b * SPAN : (b + 1) * SPAN] + bias
        step = jnp.maximum(logit, 0.0) + jnp.log1p(jnp.exp(-jnp.abs(logit)))
        steps.append(step)
        rates.append(step * neg_rate)
    spare = SPAN - blocks * heads
    steps = jnp.concatenate(steps + [jnp.ones((spare, SPAN), F32)], axis=0)
    rates = jnp.concatenate(rates + [jnp.zeros((spare, SPAN), F32)], axis=0)
    row = iota((SPAN, SPAN), 0)
    lane = iota((SPAN, SPAN), 1)
    upper = jnp.where(row <= lane, 1.0, 0.0)
    cum_rows = jnp.dot(
        rates, upper, precision=lax.Precision.HIGHEST, preferred_element_type=F32
    )
    rrow_ref[...] = LOG2E * (cum_rows - jnp.log(steps))
    cum = cum_rows.T
    step_cols = steps.T
    shift = heads.bit_length() - 1
    lane_block = lax.shift_right_logical(lane, shift)
    row_block = lax.shift_right_logical(row, shift)
    block_start = first + lane_block * SPAN
    pos = block_start + row
    doc_start = jnp.zeros((SPAN, SPAN), jnp.int32)
    begin = jnp.int32(0)
    for d in range(docs):
        doc_start = jnp.where(pos >= begin, begin, doc_start)
        begin = begin + lengths_ref[d]
    last_start = doc_start[SPAN - 1 : SPAN, :]
    last = cum[SPAN - 1 : SPAN, :]
    same_head = (lane & (heads - 1)) == (row & (heads - 1))
    before = jnp.where(same_head & (row_block < lane_block), 1.0, 0.0)
    offset = jnp.dot(
        jnp.broadcast_to(last, (8, SPAN)),
        before,
        precision=lax.Precision.HIGHEST,
        preferred_element_type=F32,
    )[0:1, :]
    w_cols = jnp.where(pos >= last_start, jnp.exp(last - cum) * step_cols, 0.0)
    entry = jnp.where(doc_start < block_start, jnp.exp(cum), 0.0)
    entry_shard = jnp.where(doc_start < first, jnp.exp(cum + offset), 0.0)
    carried = jnp.where(last_start < block_start[0:1, :], jnp.exp(last), 0.0)
    shard_decay = jnp.where(last_start < first, jnp.exp(last + offset), 0.0)
    carried = jnp.broadcast_to(carried, (8, SPAN))
    for b in range(blocks):
        turn = (SPAN - b * heads) % SPAN
        cols_ref[b] = pltpu.roll(LOG2E * cum, turn, 1) if turn else LOG2E * cum
        for kind, array in enumerate((w_cols, entry, entry_shard)):
            array = pltpu.roll(array, turn, 1) if turn else array
            rough = array.astype(BF16)
            fine = (array - rough.astype(F32)).astype(BF16)
            part_ref[kind, b * SPAN : (b + 1) * SPAN, 0:SPAN] = rough
            part_ref[kind, b * SPAN : (b + 1) * SPAN, SPAN:] = fine
        ds_ref[b] = pltpu.roll(doc_start, turn, 1) if turn else doc_start
        car_ref[b] = pltpu.roll(carried, turn, 1) if turn else carried
    for quad in range(quads):
        key = iota((2 * SPAN, WIDE), 0) & (SPAN - 1)
        head = lax.shift_right_logical(iota((2 * SPAN, WIDE), 1), 6) + 4 * quad
        head_ref[quad] = one_hot(key == head)
    decay_at = (blocks - 1) * heads

    low = iota((1, SPAN), 1) < SPAN // 2

    def spread(cols, quad, at=0):
        parts = []
        for pair in range(2):
            h = at + 4 * quad + 2 * pair
            parts.append(jnp.where(low, cols[:, h : h + 1], cols[:, h + 1 : h + 2]))
        return jnp.concatenate(parts, axis=1)

    def rows_of(b):
        return pl.ds(pl.multiple_of(b * SPAN, SPAN), SPAN)

    def pack_conv(chunk, home=None):
        if home is None:
            home = mm(home_ref[...], source(chunk))
        for way in range(2):

            @pl.when(may_get[way])
            def _():
                exchange(chunk, way).wait_recv()

        if chunk == 0:
            taps = convbc_ref[...].astype(F32)
        else:
            taps = convx_ref[:, (chunk - 1) * WIDE : chunk * WIDE].astype(F32)
        for half in range(2):
            at = slice(half * SPAN, (half + 1) * SPAN)
            xext[half, 0:TILE, :] = rcvp[chunk, margin : margin + TILE, at].astype(F32) + snd[
                chunk, tok : tok + TILE, at
            ].astype(F32)
            xext[half, TILE : TILE + margin, :] = home[0:margin, at] + rcvp[
                chunk, 0:margin, at
            ].astype(F32)
            xext[half, TILE + margin :, :] = home[margin:, at] + rcvn[chunk, :, at].astype(F32)
        with scope("conv"):
            for half in range(2):
                at = slice(half * SPAN, (half + 1) * SPAN)
                for b in range(blocks):
                    base = b * SPAN + TILE
                    total = taps[3:4, at] * xext[half, base : base + SPAN, :]
                    for tap in range(KCONV - 1):
                        back = KCONV - 1 - tap
                        piece = xext[half, base - back : base - back + SPAN, :]
                        usable = mask_ref[tap, b * SPAN : (b + 1) * SPAN, :]
                        total = total + taps[tap : tap + 1, at] * (usable * piece)
                    conv_ref[chunk, b * SPAN : (b + 1) * SPAN, at] = half_silu(total).astype(BF16)

    for b in range(blocks):
        begins = jnp.broadcast_to(ds_ref[b][:, 0:1], (SPAN, SPAN)) - (first + b * SPAN) - row
        for tap in range(KCONV - 1):
            usable = jnp.where(begins <= tap + 1 - KCONV, 1.0, 0.0)
            mask_ref[tap, b * SPAN : (b + 1) * SPAN, :] = usable

    pack_conv(0, home_first)

    eye = one_hot(row == lane)

    def prepare(b, _):
        bmat = conv_ref[0, rows_of(b), 0:N]
        cmat = conv_ref[0, rows_of(b), N : 2 * N]
        bt_ref[b] = nt(eye, bmat).astype(BF16)
        begins = ds_ref[b][:, 0:1] - (first + b * SPAN)
        score_ref[b] = jnp.where((lane <= row) & (lane >= begins), nt(cmat, bmat), 0.0)
        return 0

    lax.fori_loop(0, blocks, prepare, 0, unroll=True)

    def state_copy(quad, group, owner):
        return pltpu.make_async_remote_copy(
            src_ref=sa.at[quad, group],
            dst_ref=ra.at[lax.rem(me + nctx - owner, nctx)],
            send_sem=as_sem,
            recv_sem=ar_sem,
            device_id={"ctx": owner},
        )

    def decay_copy(quad, owner):
        return pltpu.make_async_remote_copy(
            src_ref=da.at[quad, pl.ds(0, 1)],
            dst_ref=rd.at[lax.rem(me + nctx - owner, nctx), pl.ds(0, 1)],
            send_sem=ads_sem,
            recv_sem=adr_sem,
            device_id={"ctx": owner},
        )

    def shard_state(quad):
        weights = mm(part_ref[0], head_ref[quad])
        state = jnp.zeros((N, WIDE), F32)
        for b in range(blocks):
            sloc[quad, b] = state.astype(BF16)
            weight = weights[b * SPAN : (b + 1) * SPAN]
            x_float = conv_ref[quad + 1, b * SPAN : (b + 1) * SPAN, :].astype(F32)
            inner_sum = mm(bt_ref[b], (weight * x_float).astype(BF16))
            state = state * spread(car_ref[b][0:1, :], quad) + inner_sum

        sa[quad] = state.astype(BF16).reshape(groups, TILE, WIDE)
        da[quad] = jnp.broadcast_to(spread(shard_decay, quad, decay_at), (8, WIDE))

        def give(j, _):
            group = lax.rem(j + me, groups)
            owner = group * quads + quad

            @pl.when(owner != me)
            def _():
                state_copy(quad, group, owner).start()
                decay_copy(quad, owner).start()

            @pl.when(owner == me)
            def _():
                ra[0] = sa[quad, group]
                rd[0] = da[quad]

            return 0

        lax.fori_loop(0, groups, give, 0)

    def inner(quad):
        entries = mm(part_ref[1], head_ref[quad])
        es_ref[quad] = mm(part_ref[2], head_ref[quad])

        for b in range(blocks):
            xs = conv_ref[quad + 1, rows_of(b), :]
            cmat = conv_ref[0, rows_of(b), N : 2 * N]
            cum_cols = cols_ref[b]
            gaps = rrow_ref[b * heads : (b + 1) * heads, :]
            score = score_ref[b]
            x_float = xs.astype(F32)
            y = mm(cmat, sloc[quad, b]) * entries[b * SPAN : (b + 1) * SPAN]
            parts = []
            for pair in range(2):
                mixing = []
                for h in (4 * quad + 2 * pair, 4 * quad + 2 * pair + 1):
                    gap = jnp.minimum(cum_cols[:, h : h + 1] - gaps[h : h + 1, :], 80.0)
                    mixing.append((jnp.exp2(gap) * score).astype(BF16))
                x_pair = x_float[:, pair * SPAN : (pair + 1) * SPAN]
                x_both = jnp.concatenate(
                    [jnp.where(low, x_pair, 0.0), jnp.where(low, 0.0, x_pair)], axis=0
                ).astype(BF16)
                h = 4 * quad + 2 * pair
                skip = jnp.where(low, skip_ref[h], skip_ref[h + 1])
                parts.append(mm(jnp.concatenate(mixing, axis=1), x_both) + skip * x_pair)
            ypart[quad, rows_of(b), :] = y + jnp.concatenate(parts, axis=1)

    my_quad = lax.rem(me, quads)
    my_group = lax.div(me, quads)

    def back_copy(shard, quad, group):
        return pltpu.make_async_remote_copy(
            src_ref=ret.at[shard],
            dst_ref=inc.at[quad, group],
            send_sem=rs_sem,
            recv_sem=rr_sems.at[quad],
            device_id={"ctx": shard},
        )

    def scan(shard, state):
        ret[shard] = state.astype(BF16)

        @pl.when(shard != me)
        def _():
            back_copy(shard, my_quad, my_group).start()

        @pl.when(shard == me)
        def _():
            inc[my_quad, my_group] = state.astype(BF16)

        place = lax.rem(shard + nctx - me, nctx)
        return state * rd[place, 0:1, :] + ra[place].astype(F32)

    def scan_slice(quad):
        @pl.when(my_quad == quad)
        def _():
            wait_for(ra.at[pl.ds(1, nctx - 1)], ar_sem)
            wait_for(rd.at[pl.ds(1, nctx - 1), pl.ds(0, 1)], adr_sem)
            lax.fori_loop(0, nctx, scan, jnp.zeros((TILE, WIDE), F32))

    def y_copy(quad, way):
        if way == 0:
            src, dst = pl.ds(margin, margin), pl.ds(0, margin)
        else:
            src, dst = pl.ds(0, margin), pl.ds(margin, margin)
        return pltpu.make_async_remote_copy(
            src_ref=y_home.at[quad, src],
            dst_ref=y_away.at[quad, dst],
            send_sem=ys_sems.at[way],
            recv_sem=yr_sems.at[quad, way],
            device_id={"ctx": around[way]},
        )

    def finish(quad):
        @pl.when(my_quad != quad)
        def _():
            wait_for(inc.at[quad], rr_sems.at[quad])

        @pl.when(my_quad == quad)
        def _():
            wait_for(inc.at[quad, pl.ds(1, groups - 1)], rr_sems.at[quad])

        incoming = inc[quad].reshape(N, WIDE)
        fix = mm(conv_ref[0, :, N : 2 * N], incoming)
        y_home[quad] = (ypart[quad] + fix * es_ref[quad]).astype(BF16)
        for way in range(2):

            @pl.when(may_send[way])
            def _():
                y_copy(quad, way).start()


    def work(quad):
        with scope("pack%d" % quad):
            pack_conv(quad + 1)
        with scope("state%d" % quad):
            shard_state(quad)

    with scope("out3"):
        send_out(3)
    work(0)
    with scope("out4"):
        send_out(4)
    work(1)
    with scope("inner0"):
        inner(0)
    work(2)
    with scope("scan0"):
        scan_slice(0)
    work(3)
    with scope("scan1"):
        scan_slice(1)
    with scope("inner1"):
        inner(1)
    with scope("scan2"):
        scan_slice(2)
    with scope("finish0"):
        finish(0)
    with scope("inner2"):
        inner(2)
        inner(3)
    with scope("scan3"):
        scan_slice(3)
    with scope("finish1"):
        finish(1)
    with scope("finish2"):
        finish(2)
    with scope("finish3"):
        finish(3)

    for i in range(blocks):
        across = jnp.broadcast_to(dest_ref[i : i + 1, :], (SPAN, SPAN)).T - first
        beside = across + jnp.where(across < 0, margin, -margin)
        beside = jnp.where((across < 0) | (across >= tok), beside, -1)
        for j in range(blocks):
            at = slice(i * SPAN, (i + 1) * SPAN), slice(j * SPAN, (j + 1) * SPAN)
            qhome_ref[at] = one_hot(across == lane + j * SPAN)
            qaway_ref[at] = one_hot(beside == lane + j * SPAN)
    for quad in range(quads):
        ypart[quad] = mm(qhome_ref[...], y_home[quad])
    z_load.wait()
    rbuf[0] = jnp.zeros_like(rbuf[0])
    wait_for(w_ref, w_sem)

    def gate(quad, at, z_at):
        y_rows = ypart[quad, at, :] + mm(qaway_ref[at, :], y_away[quad])
        gated = y_rows * half_silu(z_ref[at, z_at].astype(F32))
        square = gated * gated
        return gated, square[:, 0:SPAN] + square[:, SPAN:]

    for quad in range(quads):
        for way in range(2):

            @pl.when(may_get[way])
            def _():
                y_copy(quad, way).wait_recv()

        if quad < quads - 1:
            gated, square = gate(quad, pl.ds(0, tok), pl.ds(quad * WIDE, WIDE))
            ypart[quad] = gated
            ss_ref[...] = square if quad == 0 else ss_ref[...] + square

    def ready(chunk):
        at = pl.ds(pl.multiple_of(chunk * rows, rows), rows)
        gated, square = gate(quads - 1, at, pl.ds((quads - 1) * WIDE, WIDE))
        total = jnp.sum(ss_ref[at, :] + square, axis=1, keepdims=True)
        inv = lax.rsqrt(total * (1.0 / (quads * WIDE)) + 1e-05)
        for quad in range(quads):
            gain = jnp.concatenate([gain_ref[2 * quad + i : 2 * quad + i + 1, :] for i in range(2)], axis=1)
            value = gated if quad == quads - 1 else ypart[quad, at, :]
            normed_ref[at, quad * WIDE : (quad + 1) * WIDE] = (
                value * inv * gain.astype(F32)
            ).astype(BF16)

    def ring(step, way, sub):
        return pltpu.make_async_remote_copy(
            src_ref=sbuf.at[step, way, sub],
            dst_ref=rbuf.at[step + 1, way, sub],
            send_sem=send_sems.at[way, sub],
            recv_sem=recv_sems.at[step, way, sub],
            device_id={"head": hops[way]},
        )

    def chunk_of(step, way):
        back = lax.rem(mz + 2 * nhead - 1 - step, nhead)
        return jnp.where(way == 0, back, lax.rem(mz + 1 + step, nhead))

    def one(step, _):
        def ready_way(way, _):
            @pl.when((step < nhead // 2) & ((step < nhead // 2 - 1) | (way == 0)))
            def _():
                ready(chunk_of(step, way))

            return 0

        lax.fori_loop(0, 2, ready_way, 0)

        @pl.when(step == nhead // 2)
        def _():
            ready(mz)

        for sub in range(SUBS):
            for way in range(2):
                chunk = chunk_of(step, way)
                at = (way * SUBS + sub) * width
                part = mm(
                    normed_ref[pl.ds(pl.multiple_of(chunk * rows, rows), rows), :],
                    w_ref[:, at : at + width],
                )

                @pl.when(step > 0)
                def _():
                    ring(step - 1, way, sub).wait_recv()
                    ring(step - 1, way, sub).wait_send()

                total = (part + rbuf[step, way, sub].astype(F32)).astype(BF16)

                @pl.when(step < nhead - 1)
                def _():
                    sbuf[step, way, sub] = total
                    ring(step, way, sub).start()

                @pl.when(step == nhead - 1)
                def _():
                    out_ref[:, at : at + width] = total

        return 0

    lax.fori_loop(0, nhead - 1, one, 0)

    for way in range(2):

        @pl.when(may_send[way])
        def _():
            dt_copy(way).wait_send()
            sent = (pl.ds(0, margin + TILE), pl.ds(margin + TILE, margin))[way]
            wait_for(snd.at[:, sent], xs_sems.at[way])
            wait_for(y_home.at[:, pl.ds(0, margin)], ys_sems.at[way])

    wait_for(ra.at[pl.ds(1, nctx - 1)], as_sem)
    wait_for(rd.at[pl.ds(1, nctx - 1), pl.ds(0, 1)], ads_sem)
    wait_for(ret.at[pl.ds(1, nctx - 1)], rs_sem)
    lax.fori_loop(nhead - 1, nhead, one, 0)


def per_device(
    x_in,
    z_in,
    bc_in,
    dt_in,
    destination,
    doc_lengths,
    conv_x,
    conv_bc,
    dt_bias,
    a_log,
    skip_gain,
    norm_gain,
    out_weight,
):
    nctx = lax.axis_size("ctx")
    nhead = lax.axis_size("head")
    tok, channels = x_in.shape
    heads = dt_in.shape[1]
    bc_width = bc_in.shape[1]
    margin = tok // 2
    blocks = tok // SPAN
    quads = channels // WIDE
    groups = N // TILE
    rows = tok // nhead
    depth, wide = out_weight.shape
    width = wide // (2 * SUBS)
    dma = pltpu.SemaphoreType.DMA
    vmem = pl.BlockSpec(memory_space=pltpu.VMEM)
    smem = pl.BlockSpec(memory_space=pltpu.SMEM)
    anywhere = pl.BlockSpec(memory_space=pl.ANY)
    scratch = [
        pltpu.VMEM((heads, tok), BF16),
        pltpu.VMEM((blocks, SPAN), jnp.int32),
        pltpu.VMEM(conv_x.shape, BF16),
        pltpu.VMEM(conv_bc.shape, BF16),
        pltpu.VMEM((channels // SPAN, SPAN), BF16),
        pltpu.VMEM((tok, bc_width), BF16),
        pltpu.VMEM((quads, tok, WIDE), BF16),
        pltpu.VMEM((tok, channels), BF16),
        pltpu.VMEM((depth, wide), BF16),
        pltpu.VMEM((tok + TILE, tok), BF16),
        pltpu.VMEM((tok, tok), BF16),
        pltpu.VMEM((tok, tok), BF16),
        pltpu.VMEM((tok, tok), BF16),
        pltpu.VMEM((quads + 1, tok + TILE, WIDE), BF16),
        pltpu.VMEM((quads + 1, margin + TILE, WIDE), BF16),
        pltpu.VMEM((quads + 1, margin, WIDE), BF16),
        pltpu.VMEM((2, heads, margin), BF16),
        pltpu.VMEM((2, heads, margin), BF16),
        pltpu.VMEM((2, tok + TILE, SPAN), F32),
        pltpu.VMEM((KCONV - 1, tok, SPAN), F32),
        pltpu.VMEM((quads + 1, tok, WIDE), BF16),
        pltpu.VMEM((blocks, SPAN, SPAN), F32),
        pltpu.VMEM((3, tok, 2 * SPAN), BF16),
        pltpu.VMEM((quads, 2 * SPAN, WIDE), BF16),
        pltpu.VMEM((blocks, SPAN, SPAN), jnp.int32),
        pltpu.VMEM((blocks, 8, SPAN), F32),
        pltpu.VMEM((SPAN, SPAN), F32),
        pltpu.VMEM((blocks, SPAN, SPAN), F32),
        pltpu.VMEM((blocks, N, SPAN), BF16),
        pltpu.VMEM((quads, blocks, N, WIDE), BF16),
        pltpu.VMEM((quads, tok, WIDE), F32),
        pltpu.VMEM((quads, tok, WIDE), F32),
        pltpu.VMEM((quads, tok, WIDE), BF16),
        pltpu.VMEM((quads, tok, WIDE), BF16),
        pltpu.VMEM((tok, SPAN), F32),
        pltpu.VMEM((tok, channels), BF16),
        pltpu.VMEM((quads, groups, TILE, WIDE), BF16),
        pltpu.VMEM((nctx, TILE, WIDE), BF16),
        pltpu.VMEM((quads, 8, WIDE), F32),
        pltpu.VMEM((nctx, 8, WIDE), F32),
        pltpu.VMEM((nctx, TILE, WIDE), BF16),
        pltpu.VMEM((quads, groups, TILE, WIDE), BF16),
        pltpu.VMEM((nhead - 1, 2, SUBS, rows, width), BF16),
        pltpu.VMEM((nhead, 2, SUBS, rows, width), BF16),
        dma((5,)),
        dma(()),
        dma((quads,)),
        dma(()),
        dma(()),
        dma((2,)),
        dma((quads + 1, 2)),
        dma((2,)),
        dma((2,)),
        dma(()),
        dma(()),
        dma(()),
        dma(()),
        dma(()),
        dma((quads,)),
        dma((2,)),
        dma((quads, 2)),
        dma((2, SUBS)),
        dma((nhead - 1, 2, SUBS)),
    ]
    return pl.pallas_call(
        layer_kernel,
        out_shape=pltpu.VMEM((rows, wide), BF16),
        in_specs=[
            anywhere,
            anywhere,
            anywhere,
            anywhere,
            anywhere,
            smem,
            anywhere,
            anywhere,
            smem,
            smem,
            smem,
            anywhere,
            anywhere,
        ],
        out_specs=vmem,
        scratch_shapes=scratch,
        compiler_params=pltpu.CompilerParams(
            collective_id=0, has_side_effects=True, vmem_limit_bytes=60 << 20
        ),
    )(
        x_in,
        z_in,
        bc_in,
        dt_in.T,
        destination.reshape(blocks, SPAN),
        doc_lengths,
        conv_x,
        conv_bc,
        dt_bias,
        a_log,
        skip_gain,
        norm_gain.reshape(channels // SPAN, SPAN),
        out_weight,
    )


def solution(mesh):
    placed = (
        P("ctx", "head"),
        P("ctx", "head"),
        P("ctx", "head"),
        P("ctx", "head"),
        P("ctx"),
        P(),
        P(None, "head"),
        P(None, "head"),
        P("head"),
        P("head"),
        P("head"),
        P("head"),
        P("head", None),
    )
    return jax.shard_map(
        per_device, mesh=mesh, in_specs=placed, out_specs=P(("ctx", "head"), None), check_vma=False
    )
```

```python
import jax
import jax.numpy as jnp
from jax import lax
from jax.experimental import pallas as pl
from jax.experimental.pallas import tpu as pltpu
from jax.sharding import PartitionSpec as P

N = 128
SPAN = 128
KCONV = 4
SUBS = 4
WIDE = 256
TILE = 16
LOG2E = 1.4426950408889634
F32 = jnp.float32
BF16 = jnp.bfloat16


def nt(a, b):
    return lax.dot_general(a, b, (((1,), (1,)), ((), ())), preferred_element_type=F32)


def mm(a, b):
    return jnp.dot(a, b, preferred_element_type=F32)


def iota(shape, dim):
    return lax.broadcasted_iota(jnp.int32, shape, dim)


def one_hot(hit):
    return jnp.where(hit, 1.0, 0.0).astype(BF16)


def half_silu(v):
    half = 0.5 * v
    return half + half * jnp.tanh(half)


def scope(name):
    return jax.named_scope(name)


def layer_kernel(
    x_hbm,
    z_hbm,
    bc_hbm,
    dt_hbm,
    dest_hbm,
    lengths_hbm,
    convx_hbm,
    convbc_hbm,
    bias_hbm,
    alog_hbm,
    skip_hbm,
    gain_hbm,
    w_hbm,
    out_ref,
    lengths_ref,
    bias_ref,
    alog_ref,
    skip_ref,
    dt_ref,
    dest_ref,
    convx_ref,
    convbc_ref,
    gain_ref,
    bc_ref,
    x_ref,
    z_ref,
    w_ref,
    pout_ref,
    home_ref,
    qhome_ref,
    qaway_ref,
    snd,
    rcvp,
    rcvn,
    dts,
    dtr,
    xext,
    mask_ref,
    conv_ref,
    later_ref,
    cols_ref,
    part_ref,
    head_ref,
    ds_ref,
    car_ref,
    rrow_ref,
    score_ref,
    bt_ref,
    sloc,
    ypart,
    es_ref,
    y_home,
    y_away,
    ss_ref,
    normed_ref,
    sa,
    ra,
    da,
    rd,
    ret,
    inc,
    sbuf,
    rbuf,
    small_sems,
    bc_sem,
    x_sems,
    z_sem,
    w_sem,
    xs_sems,
    xr_sems,
    ds_sems,
    dr_sems,
    as_sem,
    ar_sem,
    ads_sem,
    adr_sem,
    rs_sem,
    rr_sems,
    ys_sems,
    yr_sems,
    send_sems,
    recv_sems,
):
    nctx = lax.axis_size("ctx")
    nhead = lax.axis_size("head")
    me = lax.axis_index("ctx")
    mz = lax.axis_index("head")
    tok = bc_ref.shape[0]
    margin = tok // 2
    blocks = tok // SPAN
    quads = x_ref.shape[0]
    groups = SPAN // TILE
    heads = dt_ref.shape[0]
    docs = lengths_ref.shape[0]
    first = me * tok
    around = (lax.rem(me + 1, nctx), lax.rem(me + nctx - 1, nctx))
    hops = (lax.rem(mz + 1, nhead), lax.rem(mz + nhead - 1, nhead))

    may_send = (me != nctx - 1, me != 0)
    may_get = (me != 0, me != nctx - 1)

    def wait_for(ref, sem):
        pltpu.make_async_copy(ref, ref, sem).wait()

    small_loads = [
        pltpu.make_async_copy(src, dst, small_sems.at[i])
        for i, (src, dst) in enumerate(
            (
                (dest_hbm, dest_ref),
                (dt_hbm, dt_ref),
                (convx_hbm, convx_ref),
                (convbc_hbm, convbc_ref),
                (gain_hbm, gain_ref),
                (lengths_hbm, lengths_ref),
                (bias_hbm, bias_ref),
                (alog_hbm, alog_ref),
                (skip_hbm, skip_ref),
            )
        )
    ]
    bc_load = pltpu.make_async_copy(bc_hbm, bc_ref, bc_sem)
    small_loads[0].start()
    bc_load.start()
    barrier = pltpu.get_barrier_semaphore()

    def greet(j, _):
        pl.semaphore_signal(barrier, inc=1, device_id={"ctx": lax.rem(me + j, nctx)})
        return 0

    lax.fori_loop(1, nctx, greet, 0, unroll=True)
    for hop in hops:
        pl.semaphore_signal(barrier, inc=1, device_id={"head": hop})
    for load in small_loads[1:]:
        load.start()

    x_loads = [
        pltpu.make_async_copy(x_hbm.at[:, pl.ds(c * WIDE, WIDE)], x_ref.at[c], x_sems.at[c])
        for c in range(quads)
    ]
    z_load = pltpu.make_async_copy(z_hbm, z_ref, z_sem)
    wide = w_ref.shape[1]
    rows = out_ref.shape[0]
    width = wide // (2 * SUBS)
    w_loads = []
    for sub in range(SUBS):
        for way in range(2):
            w_cols = pl.ds((way * SUBS + sub) * width, width)
            w_loads.append(
                pltpu.make_async_copy(w_hbm.at[:, w_cols], w_ref.at[:, w_cols], w_sem)
            )

    small_loads[0].wait()
    rel_row = jnp.concatenate([dest_ref[i : i + 1, :] for i in range(blocks)], axis=1) - first
    slot = iota((margin + TILE, tok), 0)
    goal = jnp.where(slot < margin, slot + tok, slot + (tok - TILE - margin))
    pout_ref[0 : margin + TILE, :] = one_hot(goal == rel_row)
    pout_ref[margin + TILE :, :] = one_hot(iota((margin, tok), 0) - margin == rel_row)

    def exchange(chunk, way):
        if way == 0:
            src, dst = snd.at[chunk, pl.ds(0, margin + TILE)], rcvp.at[chunk]
        else:
            src, dst = snd.at[chunk, pl.ds(margin + TILE, margin)], rcvn.at[chunk]
        return pltpu.make_async_remote_copy(
            src_ref=src,
            dst_ref=dst,
            send_sem=xs_sems.at[way],
            recv_sem=xr_sems.at[chunk, way],
            device_id={"ctx": around[way]},
        )

    def dt_copy(way):
        return pltpu.make_async_remote_copy(
            src_ref=dts.at[way],
            dst_ref=dtr.at[way],
            send_sem=ds_sems.at[way],
            recv_sem=dr_sems.at[way],
            device_id={"ctx": around[way]},
        )

    def source(chunk):
        return bc_ref[...] if chunk == 0 else x_ref[chunk - 1]

    small_loads[1].wait()
    dt_rows = dt_ref[...]
    dts[0] = nt(dt_rows, pout_ref[0:margin, :]).astype(BF16)
    dts[1] = nt(dt_rows, pout_ref[margin + TILE :, :]).astype(BF16)
    bc_load.wait()
    for load in x_loads:
        load.start()
    snd[0] = mm(pout_ref[...], source(0)).astype(BF16)

    pl.semaphore_wait(barrier, nctx + 1)
    for way in range(2):

        @pl.when(may_send[way])
        def _():
            dt_copy(way).start()
            exchange(0, way).start()


    def make_out(chunk):
        snd[chunk] = mm(pout_ref[...], source(chunk)).astype(BF16)

    def start_out(chunk):
        for way in range(2):

            @pl.when(may_send[way])
            def _():
                exchange(chunk, way).start()


    for chunk in (1, 2):
        x_loads[chunk - 1].wait()
        make_out(chunk)
        start_out(chunk)

    z_load.start()
    for load in w_loads:
        load.start()

    home_ref[...] = one_hot(iota((tok, tok), 0) == rel_row)
    for way in range(2):

        @pl.when(jnp.logical_not(may_get[way]))
        def _():
            landing = (rcvp, rcvn)[way]
            landing[...] = jnp.zeros_like(landing)
            dtr[way] = jnp.zeros_like(dtr[way])
            at = pl.ds(way * margin, margin)
            y_away[:, at, :] = jnp.zeros((quads, margin, WIDE), BF16)


    for load in x_loads[2:]:
        load.wait()
    make_out(3)
    start_out(3)

    for load in small_loads[2:]:
        load.wait()
    row16 = iota((heads, SPAN), 0)
    bias = jnp.zeros((heads, SPAN), F32)
    alog = jnp.zeros((heads, SPAN), F32)
    for h in range(heads):
        bias = jnp.where(row16 == h, bias_ref[h], bias)
        alog = jnp.where(row16 == h, alog_ref[h], alog)
    neg_rate = -jnp.exp(alog)
    for way in range(2):

        @pl.when(may_get[way])
        def _():
            dt_copy(way).wait_recv()

    dt_home = nt(dt_rows, home_ref[...])
    home_first = mm(home_ref[...], source(0))
    dt_raw = dt_home + jnp.concatenate([dtr[0].astype(F32), dtr[1].astype(F32)], axis=1)
    steps = []
    rates = []
    for b in range(blocks):
        logit = dt_raw[:, b * SPAN : (b + 1) * SPAN] + bias
        step = jnp.maximum(logit, 0.0) + jnp.log1p(jnp.exp(-jnp.abs(logit)))
        steps.append(step)
        rates.append(step * neg_rate)
    spare = SPAN - blocks * heads
    steps = jnp.concatenate(steps + [jnp.ones((spare, SPAN), F32)], axis=0)
    rates = jnp.concatenate(rates + [jnp.zeros((spare, SPAN), F32)], axis=0)
    row = iota((SPAN, SPAN), 0)
    lane = iota((SPAN, SPAN), 1)
    upper = jnp.where(row <= lane, 1.0, 0.0)
    cum_rows = jnp.dot(
        rates, upper, precision=lax.Precision.HIGHEST, preferred_element_type=F32
    )
    rrow_ref[...] = LOG2E * (cum_rows - jnp.log(steps))
    cum = cum_rows.T
    step_cols = steps.T
    shift = heads.bit_length() - 1
    lane_block = lax.shift_right_logical(lane, shift)
    row_block = lax.shift_right_logical(row, shift)
    block_start = first + lane_block * SPAN
    pos = block_start + row
    doc_start = jnp.zeros((SPAN, SPAN), jnp.int32)
    begin = jnp.int32(0)
    for d in range(docs):
        doc_start = jnp.where(pos >= begin, begin, doc_start)
        begin = begin + lengths_ref[d]
    last_start = doc_start[SPAN - 1 : SPAN, :]
    last = cum[SPAN - 1 : SPAN, :]
    same_head = (lane & (heads - 1)) == (row & (heads - 1))
    before = jnp.where(same_head & (row_block < lane_block), 1.0, 0.0)
    offset = jnp.dot(
        jnp.broadcast_to(last, (8, SPAN)),
        before,
        precision=lax.Precision.HIGHEST,
        preferred_element_type=F32,
    )[0:1, :]
    w_cols = jnp.where(pos >= last_start, jnp.exp(last - cum) * step_cols, 0.0)
    entry = jnp.where(doc_start < block_start, jnp.exp(cum), 0.0)
    entry_shard = jnp.where(doc_start < first, jnp.exp(cum + offset), 0.0)
    carried = jnp.where(last_start < block_start[0:1, :], jnp.exp(last), 0.0)
    shard_decay = jnp.where(last_start < first, jnp.exp(last + offset), 0.0)
    carried = jnp.broadcast_to(carried, (8, SPAN))
    later_ref[0] = LOG2E * cum
    later_ref[1] = entry
    later_ref[2] = entry_shard

    def turned(array, b):
        turn = (SPAN - b * heads) % SPAN
        return pltpu.roll(array, turn, 1) if turn else array

    def split(kind, b, array):
        array = turned(array, b)
        rough = array.astype(BF16)
        fine = (array - rough.astype(F32)).astype(BF16)
        part_ref[kind, b * SPAN : (b + 1) * SPAN, 0:SPAN] = rough
        part_ref[kind, b * SPAN : (b + 1) * SPAN, SPAN:] = fine

    def later():
        for b in range(blocks):
            cols_ref[b] = turned(later_ref[0], b)
            split(1, b, later_ref[1])
            split(2, b, later_ref[2])

    for b in range(blocks):
        split(0, b, w_cols)
        ds_ref[b] = turned(doc_start, b)
        car_ref[b] = turned(carried, b)
    for quad in range(quads):
        key = iota((2 * SPAN, WIDE), 0) & (SPAN - 1)
        head = lax.shift_right_logical(iota((2 * SPAN, WIDE), 1), 6) + 4 * quad
        head_ref[quad] = one_hot(key == head)
    decay_at = (blocks - 1) * heads

    low = iota((1, SPAN), 1) < SPAN // 2

    def spread(cols, quad, at=0):
        parts = []
        for pair in range(2):
            h = at + 4 * quad + 2 * pair
            parts.append(jnp.where(low, cols[:, h : h + 1], cols[:, h + 1 : h + 2]))
        return jnp.concatenate(parts, axis=1)

    def rows_of(b):
        return pl.ds(pl.multiple_of(b * SPAN, SPAN), SPAN)

    def pack_conv(chunk, home):
        for way in range(2):

            @pl.when(may_get[way])
            def _():
                exchange(chunk, way).wait_recv()

        if chunk == 0:
            make_out(quads)
        if chunk < quads:
            ypart[chunk] = mm(home_ref[...], source(chunk + 1))
        if chunk == 0:
            taps = convbc_ref[...].astype(F32)
        else:
            taps = convx_ref[:, (chunk - 1) * WIDE : chunk * WIDE].astype(F32)
        for half in range(2):
            at = slice(half * SPAN, (half + 1) * SPAN)
            xext[half, 0:TILE, :] = rcvp[chunk, margin : margin + TILE, at].astype(F32) + snd[
                chunk, tok : tok + TILE, at
            ].astype(F32)
            xext[half, TILE : TILE + margin, :] = home[0:margin, at] + rcvp[
                chunk, 0:margin, at
            ].astype(F32)
            xext[half, TILE + margin :, :] = home[margin:, at] + rcvn[chunk, :, at].astype(F32)
        for half in range(2):
            at = slice(half * SPAN, (half + 1) * SPAN)
            for b in range(blocks):
                base = b * SPAN + TILE
                total = taps[3:4, at] * xext[half, base : base + SPAN, :]
                for tap in range(KCONV - 1):
                    back = KCONV - 1 - tap
                    piece = xext[half, base - back : base - back + SPAN, :]
                    usable = mask_ref[tap, b * SPAN : (b + 1) * SPAN, :]
                    total = total + taps[tap : tap + 1, at] * (usable * piece)
                conv_ref[chunk, b * SPAN : (b + 1) * SPAN, at] = half_silu(total).astype(BF16)

    for b in range(blocks):
        begins = jnp.broadcast_to(ds_ref[b][:, 0:1], (SPAN, SPAN)) - (first + b * SPAN) - row
        for tap in range(KCONV - 1):
            usable = jnp.where(begins <= tap + 1 - KCONV, 1.0, 0.0)
            mask_ref[tap, b * SPAN : (b + 1) * SPAN, :] = usable

    pack_conv(0, home_first)

    eye = one_hot(row == lane)

    def prepare(b, _):
        bmat = conv_ref[0, rows_of(b), 0:N]
        cmat = conv_ref[0, rows_of(b), N : 2 * N]
        bt_ref[b] = nt(eye, bmat).astype(BF16)
        begins = ds_ref[b][:, 0:1] - (first + b * SPAN)
        score_ref[b] = jnp.where((lane <= row) & (lane >= begins), nt(cmat, bmat), 0.0)
        return 0

    lax.fori_loop(0, blocks, prepare, 0, unroll=True)

    def state_copy(quad, group, owner):
        return pltpu.make_async_remote_copy(
            src_ref=sa.at[quad, group],
            dst_ref=ra.at[lax.rem(me + nctx - owner, nctx)],
            send_sem=as_sem,
            recv_sem=ar_sem,
            device_id={"ctx": owner},
        )

    def decay_copy(quad, owner):
        return pltpu.make_async_remote_copy(
            src_ref=da.at[quad, pl.ds(0, 1)],
            dst_ref=rd.at[lax.rem(me + nctx - owner, nctx), pl.ds(0, 1)],
            send_sem=ads_sem,
            recv_sem=adr_sem,
            device_id={"ctx": owner},
        )

    def shard_state(quad):
        weights = mm(part_ref[0], head_ref[quad])
        state = jnp.zeros((N, WIDE), F32)
        for b in range(blocks):
            sloc[quad, b] = state.astype(BF16)
            weight = weights[b * SPAN : (b + 1) * SPAN]
            x_float = conv_ref[quad + 1, b * SPAN : (b + 1) * SPAN, :].astype(F32)
            inner_sum = mm(bt_ref[b], (weight * x_float).astype(BF16))
            state = state * spread(car_ref[b][0:1, :], quad) + inner_sum

        sa[quad] = state.astype(BF16).reshape(groups, TILE, WIDE)
        da[quad] = jnp.broadcast_to(spread(shard_decay, quad, decay_at), (8, WIDE))

        def give(j, _):
            group = lax.rem(j + me, groups)
            owner = group * quads + quad

            @pl.when(owner != me)
            def _():
                state_copy(quad, group, owner).start()
                decay_copy(quad, owner).start()

            @pl.when(owner == me)
            def _():
                ra[0] = sa[quad, group]
                rd[0] = da[quad]

            return 0

        lax.fori_loop(0, groups, give, 0)

    def inner(quad):
        entries = mm(part_ref[1], head_ref[quad])
        es_ref[quad] = mm(part_ref[2], head_ref[quad])

        for b in range(blocks):
            xs = conv_ref[quad + 1, rows_of(b), :]
            cmat = conv_ref[0, rows_of(b), N : 2 * N]
            cum_cols = cols_ref[b]
            gaps = rrow_ref[b * heads : (b + 1) * heads, :]
            score = score_ref[b]
            x_float = xs.astype(F32)
            y = mm(cmat, sloc[quad, b]) * entries[b * SPAN : (b + 1) * SPAN]
            parts = []
            for pair in range(2):
                mixing = []
                for h in (4 * quad + 2 * pair, 4 * quad + 2 * pair + 1):
                    gap = jnp.minimum(cum_cols[:, h : h + 1] - gaps[h : h + 1, :], 80.0)
                    mixing.append((jnp.exp2(gap) * score).astype(BF16))
                x_pair = x_float[:, pair * SPAN : (pair + 1) * SPAN]
                x_both = jnp.concatenate(
                    [jnp.where(low, x_pair, 0.0), jnp.where(low, 0.0, x_pair)], axis=0
                ).astype(BF16)
                h = 4 * quad + 2 * pair
                skip = jnp.where(low, skip_ref[h], skip_ref[h + 1])
                parts.append(mm(jnp.concatenate(mixing, axis=1), x_both) + skip * x_pair)
            ypart[quad, rows_of(b), :] = y + jnp.concatenate(parts, axis=1)

    my_quad = lax.rem(me, quads)
    my_group = lax.div(me, quads)

    def back_copy(shard, quad, group):
        return pltpu.make_async_remote_copy(
            src_ref=ret.at[shard],
            dst_ref=inc.at[quad, group],
            send_sem=rs_sem,
            recv_sem=rr_sems.at[quad],
            device_id={"ctx": shard},
        )

    def scan(shard, state):
        ret[shard] = state.astype(BF16)

        @pl.when(shard != me)
        def _():
            back_copy(shard, my_quad, my_group).start()

        @pl.when(shard == me)
        def _():
            inc[my_quad, my_group] = state.astype(BF16)

        place = lax.rem(shard + nctx - me, nctx)
        return state * rd[place, 0:1, :] + ra[place].astype(F32)

    def scan_slice(quad):
        @pl.when(my_quad == quad)
        def _():
            wait_for(ra.at[pl.ds(1, nctx - 1)], ar_sem)
            wait_for(rd.at[pl.ds(1, nctx - 1), pl.ds(0, 1)], adr_sem)
            lax.fori_loop(0, nctx, scan, jnp.zeros((TILE, WIDE), F32))

    def y_copy(quad, way):
        if way == 0:
            src, dst = pl.ds(margin, margin), pl.ds(0, margin)
        else:
            src, dst = pl.ds(0, margin), pl.ds(margin, margin)
        return pltpu.make_async_remote_copy(
            src_ref=y_home.at[quad, src],
            dst_ref=y_away.at[quad, dst],
            send_sem=ys_sems.at[way],
            recv_sem=yr_sems.at[quad, way],
            device_id={"ctx": around[way]},
        )

    def finish(quad):
        @pl.when(my_quad != quad)
        def _():
            wait_for(inc.at[quad], rr_sems.at[quad])

        @pl.when(my_quad == quad)
        def _():
            wait_for(inc.at[quad, pl.ds(1, groups - 1)], rr_sems.at[quad])

        incoming = inc[quad].reshape(N, WIDE)
        fix = mm(conv_ref[0, :, N : 2 * N], incoming)
        y_home[quad] = (ypart[quad] + fix * es_ref[quad]).astype(BF16)
        for way in range(2):

            @pl.when(may_send[way])
            def _():
                y_copy(quad, way).start()


    def work(quad):
        with scope("work%d" % quad):
            pack_conv(quad + 1, ypart[quad])
            shard_state(quad)

    work(0)
    start_out(quads)
    work(1)
    with scope("inner0"):
        later()
        inner(0)
    work(2)
    with scope("scan0"):
        scan_slice(0)
    work(3)
    with scope("scan1"):
        scan_slice(1)
    with scope("inner1"):
        inner(1)
    with scope("scan2"):
        scan_slice(2)
    with scope("finish0"):
        finish(0)
    with scope("inner2"):
        inner(2)
        inner(3)
    with scope("scan3"):
        scan_slice(3)
    with scope("finish1"):
        finish(1)
    with scope("finish2"):
        finish(2)
    for i in range(blocks):
        across = jnp.broadcast_to(dest_ref[i : i + 1, :], (SPAN, SPAN)).T - first
        beside = across + jnp.where(across < 0, margin, -margin)
        beside = jnp.where((across < 0) | (across >= tok), beside, -1)
        for j in range(blocks):
            at = slice(i * SPAN, (i + 1) * SPAN), slice(j * SPAN, (j + 1) * SPAN)
            qhome_ref[at] = one_hot(across == lane + j * SPAN)
            qaway_ref[at] = one_hot(beside == lane + j * SPAN)
    z_load.wait()
    rbuf[0] = jnp.zeros_like(rbuf[0])
    wait_for(w_ref, w_sem)

    def gather_home(quad):
        ypart[quad] = mm(qhome_ref[...], y_home[quad])

    def gate(quad, at, z_at):
        y_rows = ypart[quad, at, :] + mm(qaway_ref[at, :], y_away[quad])
        gated = y_rows * half_silu(z_ref[at, z_at].astype(F32))
        square = gated * gated
        return gated, square[:, 0:SPAN] + square[:, SPAN:]

    def gather(quad):
        for way in range(2):

            @pl.when(may_get[way])
            def _():
                y_copy(quad, way).wait_recv()

        if quad == 1:
            gather_home(quads - 1)
        if quad < quads - 1:
            gated, square = gate(quad, pl.ds(0, tok), pl.ds(quad * WIDE, WIDE))
            ypart[quad] = gated
            ss_ref[...] = square if quad == 0 else ss_ref[...] + square

    for quad in range(quads - 1):
        gather_home(quad)
    with scope("gather0"):
        gather(0)
    with scope("finish3"):
        finish(3)
    for quad in range(1, quads):
        with scope("gather%d" % quad):
            gather(quad)

    def ready(chunk):
        at = pl.ds(pl.multiple_of(chunk * rows, rows), rows)
        gated, square = gate(quads - 1, at, pl.ds((quads - 1) * WIDE, WIDE))
        total = jnp.sum(ss_ref[at, :] + square, axis=1, keepdims=True)
        inv = lax.rsqrt(total * (1.0 / (quads * WIDE)) + 1e-05)
        for quad in range(quads):
            gain = jnp.concatenate([gain_ref[2 * quad + i : 2 * quad + i + 1, :] for i in range(2)], axis=1)
            value = gated if quad == quads - 1 else ypart[quad, at, :]
            normed_ref[at, quad * WIDE : (quad + 1) * WIDE] = (
                value * inv * gain.astype(F32)
            ).astype(BF16)

    def ring(step, way, sub):
        return pltpu.make_async_remote_copy(
            src_ref=sbuf.at[step, way, sub],
            dst_ref=rbuf.at[step + 1, way, sub],
            send_sem=send_sems.at[way, sub],
            recv_sem=recv_sems.at[step, way, sub],
            device_id={"head": hops[way]},
        )

    def chunk_of(step, way):
        back = lax.rem(mz + 2 * nhead - 1 - step, nhead)
        return jnp.where(way == 0, back, lax.rem(mz + 1 + step, nhead))

    def one(step, _):
        def ready_way(way, _):
            @pl.when((step < nhead // 2) & ((step < nhead // 2 - 1) | (way == 0)))
            def _():
                ready(chunk_of(step, way))

            return 0

        lax.fori_loop(0, 2, ready_way, 0)

        @pl.when(step == nhead // 2)
        def _():
            ready(mz)

        for sub in range(SUBS):
            for way in range(2):
                chunk = chunk_of(step, way)
                at = (way * SUBS + sub) * width
                part = mm(
                    normed_ref[pl.ds(pl.multiple_of(chunk * rows, rows), rows), :],
                    w_ref[:, at : at + width],
                )

                @pl.when(step > 0)
                def _():
                    ring(step - 1, way, sub).wait_recv()
                    ring(step - 1, way, sub).wait_send()

                total = (part + rbuf[step, way, sub].astype(F32)).astype(BF16)

                @pl.when(step < nhead - 1)
                def _():
                    sbuf[step, way, sub] = total
                    ring(step, way, sub).start()

                @pl.when(step == nhead - 1)
                def _():
                    out_ref[:, at : at + width] = total

        return 0

    lax.fori_loop(0, nhead - 1, one, 0)

    for way in range(2):

        @pl.when(may_send[way])
        def _():
            dt_copy(way).wait_send()
            sent = (pl.ds(0, margin + TILE), pl.ds(margin + TILE, margin))[way]
            wait_for(snd.at[:, sent], xs_sems.at[way])
            wait_for(y_home.at[:, pl.ds(0, margin)], ys_sems.at[way])

    wait_for(ra.at[pl.ds(1, nctx - 1)], as_sem)
    wait_for(rd.at[pl.ds(1, nctx - 1), pl.ds(0, 1)], ads_sem)
    wait_for(ret.at[pl.ds(1, nctx - 1)], rs_sem)
    lax.fori_loop(nhead - 1, nhead, one, 0)


def per_device(
    x_in,
    z_in,
    bc_in,
    dt_in,
    destination,
    doc_lengths,
    conv_x,
    conv_bc,
    dt_bias,
    a_log,
    skip_gain,
    norm_gain,
    out_weight,
):
    nctx = lax.axis_size("ctx")
    nhead = lax.axis_size("head")
    tok, channels = x_in.shape
    heads = dt_in.shape[1]
    bc_width = bc_in.shape[1]
    margin = tok // 2
    blocks = tok // SPAN
    quads = channels // WIDE
    groups = N // TILE
    rows = tok // nhead
    depth, wide = out_weight.shape
    width = wide // (2 * SUBS)
    dma = pltpu.SemaphoreType.DMA
    vmem = pl.BlockSpec(memory_space=pltpu.VMEM)
    anywhere = pl.BlockSpec(memory_space=pl.ANY)
    scratch = [
        pltpu.SMEM(doc_lengths.shape, jnp.int32),
        pltpu.SMEM((heads,), F32),
        pltpu.SMEM((heads,), F32),
        pltpu.SMEM((heads,), F32),
        pltpu.VMEM((heads, tok), BF16),
        pltpu.VMEM((blocks, SPAN), jnp.int32),
        pltpu.VMEM(conv_x.shape, BF16),
        pltpu.VMEM(conv_bc.shape, BF16),
        pltpu.VMEM((channels // SPAN, SPAN), BF16),
        pltpu.VMEM((tok, bc_width), BF16),
        pltpu.VMEM((quads, tok, WIDE), BF16),
        pltpu.VMEM((tok, channels), BF16),
        pltpu.VMEM((depth, wide), BF16),
        pltpu.VMEM((tok + TILE, tok), BF16),
        pltpu.VMEM((tok, tok), BF16),
        pltpu.VMEM((tok, tok), BF16),
        pltpu.VMEM((tok, tok), BF16),
        pltpu.VMEM((quads + 1, tok + TILE, WIDE), BF16),
        pltpu.VMEM((quads + 1, margin + TILE, WIDE), BF16),
        pltpu.VMEM((quads + 1, margin, WIDE), BF16),
        pltpu.VMEM((2, heads, margin), BF16),
        pltpu.VMEM((2, heads, margin), BF16),
        pltpu.VMEM((2, tok + TILE, SPAN), F32),
        pltpu.VMEM((KCONV - 1, tok, SPAN), F32),
        pltpu.VMEM((quads + 1, tok, WIDE), BF16),
        pltpu.VMEM((3, SPAN, SPAN), F32),
        pltpu.VMEM((blocks, SPAN, SPAN), F32),
        pltpu.VMEM((3, tok, 2 * SPAN), BF16),
        pltpu.VMEM((quads, 2 * SPAN, WIDE), BF16),
        pltpu.VMEM((blocks, SPAN, SPAN), jnp.int32),
        pltpu.VMEM((blocks, 8, SPAN), F32),
        pltpu.VMEM((SPAN, SPAN), F32),
        pltpu.VMEM((blocks, SPAN, SPAN), F32),
        pltpu.VMEM((blocks, N, SPAN), BF16),
        pltpu.VMEM((quads, blocks, N, WIDE), BF16),
        pltpu.VMEM((quads, tok, WIDE), F32),
        pltpu.VMEM((quads, tok, WIDE), F32),
        pltpu.VMEM((quads, tok, WIDE), BF16),
        pltpu.VMEM((quads, tok, WIDE), BF16),
        pltpu.VMEM((tok, SPAN), F32),
        pltpu.VMEM((tok, channels), BF16),
        pltpu.VMEM((quads, groups, TILE, WIDE), BF16),
        pltpu.VMEM((nctx, TILE, WIDE), BF16),
        pltpu.VMEM((quads, 8, WIDE), F32),
        pltpu.VMEM((nctx, 8, WIDE), F32),
        pltpu.VMEM((nctx, TILE, WIDE), BF16),
        pltpu.VMEM((quads, groups, TILE, WIDE), BF16),
        pltpu.VMEM((nhead - 1, 2, SUBS, rows, width), BF16),
        pltpu.VMEM((nhead, 2, SUBS, rows, width), BF16),
        dma((9,)),
        dma(()),
        dma((quads,)),
        dma(()),
        dma(()),
        dma((2,)),
        dma((quads + 1, 2)),
        dma((2,)),
        dma((2,)),
        dma(()),
        dma(()),
        dma(()),
        dma(()),
        dma(()),
        dma((quads,)),
        dma((2,)),
        dma((quads, 2)),
        dma((2, SUBS)),
        dma((nhead - 1, 2, SUBS)),
    ]
    return pl.pallas_call(
        layer_kernel,
        out_shape=pltpu.VMEM((rows, wide), BF16),
        in_specs=[
            anywhere,
            anywhere,
            anywhere,
            anywhere,
            anywhere,
            anywhere,
            anywhere,
            anywhere,
            anywhere,
            anywhere,
            anywhere,
            anywhere,
            anywhere,
        ],
        out_specs=vmem,
        scratch_shapes=scratch,
        compiler_params=pltpu.CompilerParams(
            collective_id=0, has_side_effects=True, vmem_limit_bytes=60 << 20
        ),
    )(
        x_in,
        z_in,
        bc_in,
        dt_in.T,
        destination.reshape(blocks, SPAN),
        doc_lengths,
        conv_x,
        conv_bc,
        dt_bias,
        a_log,
        skip_gain,
        norm_gain.reshape(channels // SPAN, SPAN),
        out_weight,
    )


def solution(mesh):
    placed = (
        P("ctx", "head"),
        P("ctx", "head"),
        P("ctx", "head"),
        P("ctx", "head"),
        P("ctx"),
        P(),
        P(None, "head"),
        P(None, "head"),
        P("head"),
        P("head"),
        P("head"),
        P("head"),
        P("head", None),
    )
    return jax.shard_map(
        per_device, mesh=mesh, in_specs=placed, out_specs=P(("ctx", "head"), None), check_vma=False
    )
```

```python
import jax
import jax.numpy as jnp
from jax import lax
from jax.experimental import pallas as pl
from jax.experimental.pallas import tpu as pltpu
from jax.sharding import PartitionSpec as P

N = 128
SPAN = 128
KCONV = 4
SUBS = 4
WIDE = 256
TILE = 16
LOG2E = 1.4426950408889634
F32 = jnp.float32
BF16 = jnp.bfloat16


def nt(a, b):
    return lax.dot_general(a, b, (((1,), (1,)), ((), ())), preferred_element_type=F32)


def mm(a, b):
    return jnp.dot(a, b, preferred_element_type=F32)


def iota(shape, dim):
    return lax.broadcasted_iota(jnp.int32, shape, dim)


def one_hot(hit):
    return jnp.where(hit, 1.0, 0.0).astype(BF16)


def half_silu(v):
    half = 0.5 * v
    return half + half * jnp.tanh(half)


def scope(name):
    return jax.named_scope(name)


def layer_kernel(
    x_hbm,
    z_hbm,
    bc_hbm,
    dt_hbm,
    dest_hbm,
    lengths_hbm,
    convx_hbm,
    convbc_hbm,
    bias_hbm,
    alog_hbm,
    skip_hbm,
    gain_hbm,
    w_hbm,
    out_ref,
    lengths_ref,
    bias_ref,
    alog_ref,
    skip_ref,
    dt_ref,
    dest_ref,
    convx_ref,
    convbc_ref,
    gain_ref,
    bc_ref,
    x_ref,
    z_ref,
    w_ref,
    pout_ref,
    home_ref,
    qhome_ref,
    qaway_ref,
    snd,
    rcvp,
    rcvn,
    dts,
    dtr,
    xext,
    mask_ref,
    conv_ref,
    later_ref,
    cols_ref,
    part_ref,
    head_ref,
    ds_ref,
    car_ref,
    rrow_ref,
    score_ref,
    bt_ref,
    sloc,
    ypart,
    es_ref,
    y_home,
    y_away,
    ss_ref,
    normed_ref,
    sa,
    ra,
    da,
    rd,
    ret,
    inc,
    sbuf,
    rbuf,
    small_sems,
    bc_sem,
    x_sems,
    z_sem,
    w_sem,
    xs_sems,
    xr_sems,
    ds_sems,
    dr_sems,
    as_sem,
    ar_sem,
    ads_sem,
    adr_sem,
    rs_sem,
    rr_sems,
    ys_sems,
    yr_sems,
    send_sems,
    recv_sems,
):
    nctx = lax.axis_size("ctx")
    nhead = lax.axis_size("head")
    me = lax.axis_index("ctx")
    mz = lax.axis_index("head")
    tok = bc_ref.shape[0]
    margin = tok // 2
    blocks = tok // SPAN
    quads = x_ref.shape[0]
    groups = SPAN // TILE
    heads = dt_ref.shape[0]
    docs = lengths_ref.shape[0]
    first = me * tok
    around = (lax.rem(me + 1, nctx), lax.rem(me + nctx - 1, nctx))
    hops = (lax.rem(mz + 1, nhead), lax.rem(mz + nhead - 1, nhead))

    may_send = (me != nctx - 1, me != 0)
    may_get = (me != 0, me != nctx - 1)

    def wait_for(ref, sem):
        pltpu.make_async_copy(ref, ref, sem).wait()

    small_loads = [
        pltpu.make_async_copy(src, dst, small_sems.at[i])
        for i, (src, dst) in enumerate(
            (
                (dest_hbm, dest_ref),
                (dt_hbm, dt_ref),
                (convx_hbm, convx_ref),
                (convbc_hbm, convbc_ref),
                (gain_hbm, gain_ref),
                (lengths_hbm, lengths_ref),
                (bias_hbm, bias_ref),
                (alog_hbm, alog_ref),
                (skip_hbm, skip_ref),
            )
        )
    ]
    bc_load = pltpu.make_async_copy(bc_hbm, bc_ref, bc_sem)
    small_loads[0].start()
    bc_load.start()
    barrier = pltpu.get_barrier_semaphore()

    def greet(j, _):
        pl.semaphore_signal(barrier, inc=1, device_id={"ctx": lax.rem(me + j, nctx)})
        return 0

    lax.fori_loop(1, nctx, greet, 0, unroll=True)
    for hop in hops:
        pl.semaphore_signal(barrier, inc=1, device_id={"head": hop})
    for load in small_loads[1:]:
        load.start()

    x_loads = [
        pltpu.make_async_copy(x_hbm.at[:, pl.ds(c * WIDE, WIDE)], x_ref.at[c], x_sems.at[c])
        for c in range(quads)
    ]
    z_load = pltpu.make_async_copy(z_hbm, z_ref, z_sem)
    wide = w_ref.shape[1]
    rows = out_ref.shape[0]
    width = wide // (2 * SUBS)
    w_loads = []
    for sub in range(SUBS):
        for way in range(2):
            w_cols = pl.ds((way * SUBS + sub) * width, width)
            w_loads.append(
                pltpu.make_async_copy(w_hbm.at[:, w_cols], w_ref.at[:, w_cols], w_sem)
            )

    small_loads[0].wait()
    rel_row = jnp.concatenate([dest_ref[i : i + 1, :] for i in range(blocks)], axis=1) - first
    slot = iota((margin + TILE, tok), 0)
    goal = jnp.where(slot < margin, slot + tok, slot + (tok - TILE - margin))
    pout_ref[0 : margin + TILE, :] = one_hot(goal == rel_row)
    pout_ref[margin + TILE :, :] = one_hot(iota((margin, tok), 0) - margin == rel_row)

    def exchange(chunk, way):
        if way == 0:
            src, dst = snd.at[chunk, pl.ds(0, margin + TILE)], rcvp.at[chunk]
        else:
            src, dst = snd.at[chunk, pl.ds(margin + TILE, margin)], rcvn.at[chunk]
        return pltpu.make_async_remote_copy(
            src_ref=src,
            dst_ref=dst,
            send_sem=xs_sems.at[way],
            recv_sem=xr_sems.at[chunk, way],
            device_id={"ctx": around[way]},
        )

    def dt_copy(way):
        return pltpu.make_async_remote_copy(
            src_ref=dts.at[way],
            dst_ref=dtr.at[way],
            send_sem=ds_sems.at[way],
            recv_sem=dr_sems.at[way],
            device_id={"ctx": around[way]},
        )

    def source(chunk):
        return bc_ref[...] if chunk == 0 else x_ref[chunk - 1]

    small_loads[1].wait()
    dt_rows = dt_ref[...]
    dts[0] = nt(dt_rows, pout_ref[0:margin, :]).astype(BF16)
    dts[1] = nt(dt_rows, pout_ref[margin + TILE :, :]).astype(BF16)
    bc_load.wait()
    for load in x_loads:
        load.start()
    snd[0] = mm(pout_ref[...], source(0)).astype(BF16)

    pl.semaphore_wait(barrier, nctx + 1)
    for way in range(2):

        @pl.when(may_send[way])
        def _():
            dt_copy(way).start()
            exchange(0, way).start()


    def make_out(chunk):
        snd[chunk] = mm(pout_ref[...], source(chunk)).astype(BF16)

    def start_out(chunk):
        for way in range(2):

            @pl.when(may_send[way])
            def _():
                exchange(chunk, way).start()


    for chunk in (1, 2):
        x_loads[chunk - 1].wait()
        make_out(chunk)
        start_out(chunk)

    z_load.start()
    for load in w_loads:
        load.start()

    home_ref[...] = one_hot(iota((tok, tok), 0) == rel_row)
    for way in range(2):

        @pl.when(jnp.logical_not(may_get[way]))
        def _():
            landing = (rcvp, rcvn)[way]
            landing[...] = jnp.zeros_like(landing)
            dtr[way] = jnp.zeros_like(dtr[way])
            at = pl.ds(way * margin, margin)
            y_away[:, at, :] = jnp.zeros((quads, margin, WIDE), BF16)


    for load in x_loads[2:]:
        load.wait()
    make_out(3)
    start_out(3)

    for load in small_loads[2:]:
        load.wait()
    row16 = iota((heads, SPAN), 0)
    bias = jnp.zeros((heads, SPAN), F32)
    alog = jnp.zeros((heads, SPAN), F32)
    for h in range(heads):
        bias = jnp.where(row16 == h, bias_ref[h], bias)
        alog = jnp.where(row16 == h, alog_ref[h], alog)
    neg_rate = -jnp.exp(alog)
    for way in range(2):

        @pl.when(may_get[way])
        def _():
            dt_copy(way).wait_recv()

    dt_home = nt(dt_rows, home_ref[...])
    home_first = mm(home_ref[...], source(0))
    dt_raw = dt_home + jnp.concatenate([dtr[0].astype(F32), dtr[1].astype(F32)], axis=1)
    steps = []
    rates = []
    for b in range(blocks):
        logit = dt_raw[:, b * SPAN : (b + 1) * SPAN] + bias
        step = jnp.maximum(logit, 0.0) + jnp.log1p(jnp.exp(-jnp.abs(logit)))
        steps.append(step)
        rates.append(step * neg_rate)
    spare = SPAN - blocks * heads
    steps = jnp.concatenate(steps + [jnp.ones((spare, SPAN), F32)], axis=0)
    rates = jnp.concatenate(rates + [jnp.zeros((spare, SPAN), F32)], axis=0)
    row = iota((SPAN, SPAN), 0)
    lane = iota((SPAN, SPAN), 1)
    upper = jnp.where(row <= lane, 1.0, 0.0)
    cum_rows = jnp.dot(
        rates, upper, precision=lax.Precision.HIGHEST, preferred_element_type=F32
    )
    rrow_ref[...] = LOG2E * (cum_rows - jnp.log(steps))
    cum = cum_rows.T
    step_cols = steps.T
    shift = heads.bit_length() - 1
    lane_block = lax.shift_right_logical(lane, shift)
    row_block = lax.shift_right_logical(row, shift)
    block_start = first + lane_block * SPAN
    pos = block_start + row
    doc_start = jnp.zeros((SPAN, SPAN), jnp.int32)
    begin = jnp.int32(0)
    for d in range(docs):
        doc_start = jnp.where(pos >= begin, begin, doc_start)
        begin = begin + lengths_ref[d]
    last_start = doc_start[SPAN - 1 : SPAN, :]
    last = cum[SPAN - 1 : SPAN, :]
    same_head = (lane & (heads - 1)) == (row & (heads - 1))
    before = jnp.where(same_head & (row_block < lane_block), 1.0, 0.0)
    offset = jnp.dot(
        jnp.broadcast_to(last, (8, SPAN)),
        before,
        precision=lax.Precision.HIGHEST,
        preferred_element_type=F32,
    )[0:1, :]
    w_cols = jnp.where(pos >= last_start, jnp.exp(last - cum) * step_cols, 0.0)
    entry = jnp.where(doc_start < block_start, jnp.exp(cum), 0.0)
    entry_shard = jnp.where(doc_start < first, jnp.exp(cum + offset), 0.0)
    carried = jnp.where(last_start < block_start[0:1, :], jnp.exp(last), 0.0)
    shard_decay = jnp.where(last_start < first, jnp.exp(last + offset), 0.0)
    carried = jnp.broadcast_to(carried, (8, SPAN))
    later_ref[0] = LOG2E * cum
    later_ref[1] = entry
    later_ref[2] = entry_shard

    def turned(array, b):
        turn = (SPAN - b * heads) % SPAN
        return pltpu.roll(array, turn, 1) if turn else array

    def split(kind, b, array):
        array = turned(array, b)
        rough = array.astype(BF16)
        fine = (array - rough.astype(F32)).astype(BF16)
        part_ref[kind, b * SPAN : (b + 1) * SPAN, 0:SPAN] = rough
        part_ref[kind, b * SPAN : (b + 1) * SPAN, SPAN:] = fine

    def later():
        for b in range(blocks):
            cols_ref[b] = turned(later_ref[0], b)
            split(1, b, later_ref[1])
            split(2, b, later_ref[2])

    for b in range(blocks):
        split(0, b, w_cols)
        ds_ref[b] = turned(doc_start, b)
        car_ref[b] = turned(carried, b)
    for quad in range(quads):
        key = iota((2 * SPAN, WIDE), 0) & (SPAN - 1)
        head = lax.shift_right_logical(iota((2 * SPAN, WIDE), 1), 6) + 4 * quad
        head_ref[quad] = one_hot(key == head)
    decay_at = (blocks - 1) * heads

    low = iota((1, SPAN), 1) < SPAN // 2

    def spread(cols, quad, at=0):
        parts = []
        for pair in range(2):
            h = at + 4 * quad + 2 * pair
            parts.append(jnp.where(low, cols[:, h : h + 1], cols[:, h + 1 : h + 2]))
        return jnp.concatenate(parts, axis=1)

    def rows_of(b):
        return pl.ds(pl.multiple_of(b * SPAN, SPAN), SPAN)

    def pack_conv(chunk, home):
        for way in range(2):

            @pl.when(may_get[way])
            def _():
                exchange(chunk, way).wait_recv()

        if chunk == 0:
            make_out(quads)
        if chunk < quads:
            ypart[chunk] = mm(home_ref[...], source(chunk + 1))
        if chunk == 0:
            taps = convbc_ref[...].astype(F32)
        else:
            taps = convx_ref[:, (chunk - 1) * WIDE : chunk * WIDE].astype(F32)
        for half in range(2):
            at = slice(half * SPAN, (half + 1) * SPAN)
            xext[half, 0:TILE, :] = rcvp[chunk, margin : margin + TILE, at].astype(F32) + snd[
                chunk, tok : tok + TILE, at
            ].astype(F32)
            xext[half, TILE : TILE + margin, :] = home[0:margin, at] + rcvp[
                chunk, 0:margin, at
            ].astype(F32)
            xext[half, TILE + margin :, :] = home[margin:, at] + rcvn[chunk, :, at].astype(F32)
        for half in range(2):
            at = slice(half * SPAN, (half + 1) * SPAN)
            for b in range(blocks):
                base = b * SPAN + TILE
                total = taps[3:4, at] * xext[half, base : base + SPAN, :]
                for tap in range(KCONV - 1):
                    back = KCONV - 1 - tap
                    piece = xext[half, base - back : base - back + SPAN, :]
                    usable = mask_ref[tap, b * SPAN : (b + 1) * SPAN, :]
                    total = total + taps[tap : tap + 1, at] * (usable * piece)
                conv_ref[chunk, b * SPAN : (b + 1) * SPAN, at] = half_silu(total).astype(BF16)

    for b in range(blocks):
        begins = jnp.broadcast_to(ds_ref[b][:, 0:1], (SPAN, SPAN)) - (first + b * SPAN) - row
        for tap in range(KCONV - 1):
            usable = jnp.where(begins <= tap + 1 - KCONV, 1.0, 0.0)
            mask_ref[tap, b * SPAN : (b + 1) * SPAN, :] = usable

    pack_conv(0, home_first)

    eye = one_hot(row == lane)

    def prepare(b, _):
        bmat = conv_ref[0, rows_of(b), 0:N]
        cmat = conv_ref[0, rows_of(b), N : 2 * N]
        bt_ref[b] = nt(eye, bmat).astype(BF16)
        begins = ds_ref[b][:, 0:1] - (first + b * SPAN)
        score_ref[b] = jnp.where((lane <= row) & (lane >= begins), nt(cmat, bmat), 0.0)
        return 0

    lax.fori_loop(0, blocks, prepare, 0, unroll=True)

    def state_copy(quad, group, owner):
        return pltpu.make_async_remote_copy(
            src_ref=sa.at[quad, group],
            dst_ref=ra.at[lax.rem(me + nctx - owner, nctx)],
            send_sem=as_sem,
            recv_sem=ar_sem,
            device_id={"ctx": owner},
        )

    def decay_copy(quad, owner):
        return pltpu.make_async_remote_copy(
            src_ref=da.at[quad, pl.ds(0, 1)],
            dst_ref=rd.at[lax.rem(me + nctx - owner, nctx), pl.ds(0, 1)],
            send_sem=ads_sem,
            recv_sem=adr_sem,
            device_id={"ctx": owner},
        )

    def shard_state(quad):
        weights = mm(part_ref[0], head_ref[quad])
        state = jnp.zeros((N, WIDE), F32)
        for b in range(blocks):
            sloc[quad, b] = state.astype(BF16)
            weight = weights[b * SPAN : (b + 1) * SPAN]
            x_float = conv_ref[quad + 1, b * SPAN : (b + 1) * SPAN, :].astype(F32)
            inner_sum = mm(bt_ref[b], (weight * x_float).astype(BF16))
            state = state * spread(car_ref[b][0:1, :], quad) + inner_sum

        sa[quad] = state.astype(BF16).reshape(groups, TILE, WIDE)
        da[quad] = jnp.broadcast_to(spread(shard_decay, quad, decay_at), (8, WIDE))

        def give(j, _):
            group = lax.rem(j + me, groups)
            owner = group * quads + quad

            @pl.when(owner != me)
            def _():
                state_copy(quad, group, owner).start()
                decay_copy(quad, owner).start()

            @pl.when(owner == me)
            def _():
                ra[0] = sa[quad, group]
                rd[0] = da[quad]

            return 0

        lax.fori_loop(0, groups, give, 0)

    def inner(quad):
        entries = mm(part_ref[1], head_ref[quad])
        es_ref[quad] = mm(part_ref[2], head_ref[quad])

        for b in range(blocks):
            xs = conv_ref[quad + 1, rows_of(b), :]
            cmat = conv_ref[0, rows_of(b), N : 2 * N]
            cum_cols = cols_ref[b]
            gaps = rrow_ref[b * heads : (b + 1) * heads, :]
            score = score_ref[b]
            x_float = xs.astype(F32)
            y = mm(cmat, sloc[quad, b]) * entries[b * SPAN : (b + 1) * SPAN]
            parts = []
            for pair in range(2):
                mixing = []
                for h in (4 * quad + 2 * pair, 4 * quad + 2 * pair + 1):
                    gap = jnp.minimum(cum_cols[:, h : h + 1] - gaps[h : h + 1, :], 80.0)
                    mixing.append((jnp.exp2(gap) * score).astype(BF16))
                x_pair = x_float[:, pair * SPAN : (pair + 1) * SPAN]
                x_both = jnp.concatenate(
                    [jnp.where(low, x_pair, 0.0), jnp.where(low, 0.0, x_pair)], axis=0
                ).astype(BF16)
                h = 4 * quad + 2 * pair
                skip = jnp.where(low, skip_ref[h], skip_ref[h + 1])
                parts.append(mm(jnp.concatenate(mixing, axis=1), x_both) + skip * x_pair)
            ypart[quad, rows_of(b), :] = y + jnp.concatenate(parts, axis=1)

    my_quad = lax.rem(me, quads)
    my_group = lax.div(me, quads)

    def back_copy(shard, quad, group):
        return pltpu.make_async_remote_copy(
            src_ref=ret.at[shard],
            dst_ref=inc.at[quad, group],
            send_sem=rs_sem,
            recv_sem=rr_sems.at[quad],
            device_id={"ctx": shard},
        )

    def scan(shard, state):
        ret[shard] = state.astype(BF16)

        @pl.when(shard != me)
        def _():
            back_copy(shard, my_quad, my_group).start()

        @pl.when(shard == me)
        def _():
            inc[my_quad, my_group] = state.astype(BF16)

        place = lax.rem(shard + nctx - me, nctx)
        return state * rd[place, 0:1, :] + ra[place].astype(F32)

    def scan_slice(quad):
        @pl.when(my_quad == quad)
        def _():
            wait_for(ra.at[pl.ds(1, nctx - 1)], ar_sem)
            wait_for(rd.at[pl.ds(1, nctx - 1), pl.ds(0, 1)], adr_sem)
            lax.fori_loop(0, nctx, scan, jnp.zeros((TILE, WIDE), F32))

    def y_copy(quad, way):
        if way == 0:
            src, dst = pl.ds(margin, margin), pl.ds(0, margin)
        else:
            src, dst = pl.ds(0, margin), pl.ds(margin, margin)
        return pltpu.make_async_remote_copy(
            src_ref=y_home.at[quad, src],
            dst_ref=y_away.at[quad, dst],
            send_sem=ys_sems.at[way],
            recv_sem=yr_sems.at[quad, way],
            device_id={"ctx": around[way]},
        )

    def finish(quad):
        @pl.when(my_quad != quad)
        def _():
            wait_for(inc.at[quad], rr_sems.at[quad])

        @pl.when(my_quad == quad)
        def _():
            wait_for(inc.at[quad, pl.ds(1, groups - 1)], rr_sems.at[quad])

        incoming = inc[quad].reshape(N, WIDE)
        fix = mm(conv_ref[0, :, N : 2 * N], incoming)
        y_home[quad] = (ypart[quad] + fix * es_ref[quad]).astype(BF16)
        for way in range(2):

            @pl.when(may_send[way])
            def _():
                y_copy(quad, way).start()


    def work(quad):
        with scope("work%d" % quad):
            pack_conv(quad + 1, ypart[quad])
            shard_state(quad)

    work(0)
    start_out(quads)
    work(1)
    with scope("inner0"):
        later()
        inner(0)
    work(2)
    with scope("scan0"):
        scan_slice(0)
    work(3)
    with scope("scan1"):
        scan_slice(1)
    with scope("inner1"):
        inner(1)
    with scope("scan2"):
        scan_slice(2)
    with scope("finish0"):
        finish(0)
    with scope("inner2"):
        inner(2)
    with scope("scan3"):
        scan_slice(3)
    with scope("finish1"):
        finish(1)
    with scope("finish2"):
        finish(2)
    with scope("inner3"):
        inner(3)
    for i in range(blocks):
        across = jnp.broadcast_to(dest_ref[i : i + 1, :], (SPAN, SPAN)).T - first
        beside = across + jnp.where(across < 0, margin, -margin)
        beside = jnp.where((across < 0) | (across >= tok), beside, -1)
        for j in range(blocks):
            at = slice(i * SPAN, (i + 1) * SPAN), slice(j * SPAN, (j + 1) * SPAN)
            qhome_ref[at] = one_hot(across == lane + j * SPAN)
            qaway_ref[at] = one_hot(beside == lane + j * SPAN)
    z_load.wait()
    rbuf[0] = jnp.zeros_like(rbuf[0])
    wait_for(w_ref, w_sem)

    def gather_home(quad):
        ypart[quad] = mm(qhome_ref[...], y_home[quad])

    def gate(quad, at, z_at):
        y_rows = ypart[quad, at, :] + mm(qaway_ref[at, :], y_away[quad])
        gated = y_rows * half_silu(z_ref[at, z_at].astype(F32))
        square = gated * gated
        return gated, square[:, 0:SPAN] + square[:, SPAN:]

    def gather(quad):
        for way in range(2):

            @pl.when(may_get[way])
            def _():
                y_copy(quad, way).wait_recv()

        if quad < quads - 1:
            gather_home(quad + 1)
        if quad < quads - 1:
            gated, square = gate(quad, pl.ds(0, tok), pl.ds(quad * WIDE, WIDE))
            ypart[quad] = gated
            ss_ref[...] = square if quad == 0 else ss_ref[...] + square

    gather_home(0)
    with scope("finish3"):
        finish(3)
    for quad in range(quads):
        with scope("gather%d" % quad):
            gather(quad)

    def ready(chunk):
        at = pl.ds(pl.multiple_of(chunk * rows, rows), rows)
        gains = gain_ref[...].astype(F32)
        gated, square = gate(quads - 1, at, pl.ds((quads - 1) * WIDE, WIDE))
        total = jnp.sum(ss_ref[at, :] + square, axis=1, keepdims=True)
        inv = lax.rsqrt(total * (1.0 / (quads * WIDE)) + 1e-05)
        for quad in range(quads):
            gain = jnp.concatenate(
                [gains[2 * quad + i : 2 * quad + i + 1, :] for i in range(2)], axis=1
            )
            value = gated if quad == quads - 1 else ypart[quad, at, :]
            normed_ref[at, quad * WIDE : (quad + 1) * WIDE] = (
                value * inv * gain
            ).astype(BF16)

    def ring(step, way, sub):
        return pltpu.make_async_remote_copy(
            src_ref=sbuf.at[step, way, sub],
            dst_ref=rbuf.at[step + 1, way, sub],
            send_sem=send_sems.at[way, sub],
            recv_sem=recv_sems.at[step, way, sub],
            device_id={"head": hops[way]},
        )

    def chunk_of(step, way):
        back = lax.rem(mz + 2 * nhead - 1 - step, nhead)
        return jnp.where(way == 0, back, lax.rem(mz + 1 + step, nhead))

    def one(step, _):
        def ready_way(way, _):
            @pl.when((step < nhead // 2) & ((step < nhead // 2 - 1) | (way == 0)))
            def _():
                ready(chunk_of(step, way))

            return 0

        lax.fori_loop(0, 2, ready_way, 0)

        @pl.when(step == nhead // 2)
        def _():
            ready(mz)

        for sub in range(SUBS):
            for way in range(2):
                chunk = chunk_of(step, way)
                at = (way * SUBS + sub) * width
                part = mm(
                    normed_ref[pl.ds(pl.multiple_of(chunk * rows, rows), rows), :],
                    w_ref[:, at : at + width],
                )

                @pl.when(step > 0)
                def _():
                    ring(step - 1, way, sub).wait_recv()
                    ring(step - 1, way, sub).wait_send()

                total = (part + rbuf[step, way, sub].astype(F32)).astype(BF16)

                @pl.when(step < nhead - 1)
                def _():
                    sbuf[step, way, sub] = total
                    ring(step, way, sub).start()

                @pl.when(step == nhead - 1)
                def _():
                    out_ref[:, at : at + width] = total

        return 0

    lax.fori_loop(0, nhead - 1, one, 0)

    for way in range(2):

        @pl.when(may_send[way])
        def _():
            dt_copy(way).wait_send()
            sent = (pl.ds(0, margin + TILE), pl.ds(margin + TILE, margin))[way]
            wait_for(snd.at[:, sent], xs_sems.at[way])
            wait_for(y_home.at[:, pl.ds(0, margin)], ys_sems.at[way])

    wait_for(ra.at[pl.ds(1, nctx - 1)], as_sem)
    wait_for(rd.at[pl.ds(1, nctx - 1), pl.ds(0, 1)], ads_sem)
    wait_for(ret.at[pl.ds(1, nctx - 1)], rs_sem)
    lax.fori_loop(nhead - 1, nhead, one, 0)


def per_device(
    x_in,
    z_in,
    bc_in,
    dt_in,
    destination,
    doc_lengths,
    conv_x,
    conv_bc,
    dt_bias,
    a_log,
    skip_gain,
    norm_gain,
    out_weight,
):
    nctx = lax.axis_size("ctx")
    nhead = lax.axis_size("head")
    tok, channels = x_in.shape
    heads = dt_in.shape[1]
    bc_width = bc_in.shape[1]
    margin = tok // 2
    blocks = tok // SPAN
    quads = channels // WIDE
    groups = N // TILE
    rows = tok // nhead
    depth, wide = out_weight.shape
    width = wide // (2 * SUBS)
    dma = pltpu.SemaphoreType.DMA
    vmem = pl.BlockSpec(memory_space=pltpu.VMEM)
    anywhere = pl.BlockSpec(memory_space=pl.ANY)
    scratch = [
        pltpu.SMEM(doc_lengths.shape, jnp.int32),
        pltpu.SMEM((heads,), F32),
        pltpu.SMEM((heads,), F32),
        pltpu.SMEM((heads,), F32),
        pltpu.VMEM((heads, tok), BF16),
        pltpu.VMEM((blocks, SPAN), jnp.int32),
        pltpu.VMEM(conv_x.shape, BF16),
        pltpu.VMEM(conv_bc.shape, BF16),
        pltpu.VMEM((channels // SPAN, SPAN), BF16),
        pltpu.VMEM((tok, bc_width), BF16),
        pltpu.VMEM((quads, tok, WIDE), BF16),
        pltpu.VMEM((tok, channels), BF16),
        pltpu.VMEM((depth, wide), BF16),
        pltpu.VMEM((tok + TILE, tok), BF16),
        pltpu.VMEM((tok, tok), BF16),
        pltpu.VMEM((tok, tok), BF16),
        pltpu.VMEM((tok, tok), BF16),
        pltpu.VMEM((quads + 1, tok + TILE, WIDE), BF16),
        pltpu.VMEM((quads + 1, margin + TILE, WIDE), BF16),
        pltpu.VMEM((quads + 1, margin, WIDE), BF16),
        pltpu.VMEM((2, heads, margin), BF16),
        pltpu.VMEM((2, heads, margin), BF16),
        pltpu.VMEM((2, tok + TILE, SPAN), F32),
        pltpu.VMEM((KCONV - 1, tok, SPAN), F32),
        pltpu.VMEM((quads + 1, tok, WIDE), BF16),
        pltpu.VMEM((3, SPAN, SPAN), F32),
        pltpu.VMEM((blocks, SPAN, SPAN), F32),
        pltpu.VMEM((3, tok, 2 * SPAN), BF16),
        pltpu.VMEM((quads, 2 * SPAN, WIDE), BF16),
        pltpu.VMEM((blocks, SPAN, SPAN), jnp.int32),
        pltpu.VMEM((blocks, 8, SPAN), F32),
        pltpu.VMEM((SPAN, SPAN), F32),
        pltpu.VMEM((blocks, SPAN, SPAN), F32),
        pltpu.VMEM((blocks, N, SPAN), BF16),
        pltpu.VMEM((quads, blocks, N, WIDE), BF16),
        pltpu.VMEM((quads, tok, WIDE), F32),
        pltpu.VMEM((quads, tok, WIDE), F32),
        pltpu.VMEM((quads, tok, WIDE), BF16),
        pltpu.VMEM((quads, tok, WIDE), BF16),
        pltpu.VMEM((tok, SPAN), F32),
        pltpu.VMEM((tok, channels), BF16),
        pltpu.VMEM((quads, groups, TILE, WIDE), BF16),
        pltpu.VMEM((nctx, TILE, WIDE), BF16),
        pltpu.VMEM((quads, 8, WIDE), F32),
        pltpu.VMEM((nctx, 8, WIDE), F32),
        pltpu.VMEM((nctx, TILE, WIDE), BF16),
        pltpu.VMEM((quads, groups, TILE, WIDE), BF16),
        pltpu.VMEM((nhead - 1, 2, SUBS, rows, width), BF16),
        pltpu.VMEM((nhead, 2, SUBS, rows, width), BF16),
        dma((9,)),
        dma(()),
        dma((quads,)),
        dma(()),
        dma(()),
        dma((2,)),
        dma((quads + 1, 2)),
        dma((2,)),
        dma((2,)),
        dma(()),
        dma(()),
        dma(()),
        dma(()),
        dma(()),
        dma((quads,)),
        dma((2,)),
        dma((quads, 2)),
        dma((2, SUBS)),
        dma((nhead - 1, 2, SUBS)),
    ]
    return pl.pallas_call(
        layer_kernel,
        out_shape=pltpu.VMEM((rows, wide), BF16),
        in_specs=[
            anywhere,
            anywhere,
            anywhere,
            anywhere,
            anywhere,
            anywhere,
            anywhere,
            anywhere,
            anywhere,
            anywhere,
            anywhere,
            anywhere,
            anywhere,
        ],
        out_specs=vmem,
        scratch_shapes=scratch,
        compiler_params=pltpu.CompilerParams(
            collective_id=0, has_side_effects=True, vmem_limit_bytes=60 << 20
        ),
    )(
        x_in,
        z_in,
        bc_in,
        dt_in.T,
        destination.reshape(blocks, SPAN),
        doc_lengths,
        conv_x,
        conv_bc,
        dt_bias,
        a_log,
        skip_gain,
        norm_gain.reshape(channels // SPAN, SPAN),
        out_weight,
    )


def solution(mesh):
    placed = (
        P("ctx", "head"),
        P("ctx", "head"),
        P("ctx", "head"),
        P("ctx", "head"),
        P("ctx"),
        P(),
        P(None, "head"),
        P(None, "head"),
        P("head"),
        P("head"),
        P("head"),
        P("head"),
        P("head", None),
    )
    return jax.shard_map(
        per_device, mesh=mesh, in_specs=placed, out_specs=P(("ctx", "head"), None), check_vma=False
    )
```

```python
import jax
import jax.numpy as jnp
from jax import lax
from jax.experimental import pallas as pl
from jax.experimental.pallas import tpu as pltpu
from jax.sharding import PartitionSpec as P

N = 128
SPAN = 128
KCONV = 4
SUBS = 4
WIDE = 256
TILE = 16
LOG2E = 1.4426950408889634
F32 = jnp.float32
BF16 = jnp.bfloat16


def nt(a, b):
    return lax.dot_general(a, b, (((1,), (1,)), ((), ())), preferred_element_type=F32)


def mm(a, b):
    return jnp.dot(a, b, preferred_element_type=F32)


def iota(shape, dim):
    return lax.broadcasted_iota(jnp.int32, shape, dim)


def one_hot(hit):
    return jnp.where(hit, 1.0, 0.0).astype(BF16)


def half_silu(v):
    half = 0.5 * v
    return half + half * jnp.tanh(half)


def scope(name):
    return jax.named_scope(name)


def layer_kernel(
    x_hbm,
    z_hbm,
    bc_hbm,
    dt_hbm,
    dest_hbm,
    lengths_hbm,
    convx_hbm,
    convbc_hbm,
    bias_hbm,
    alog_hbm,
    skip_hbm,
    gain_hbm,
    w_hbm,
    out_ref,
    lengths_ref,
    bias_ref,
    alog_ref,
    skip_ref,
    dt_ref,
    dest_ref,
    convx_ref,
    convbc_ref,
    gain_ref,
    bc_ref,
    x_ref,
    z_ref,
    w_ref,
    pout_ref,
    home_ref,
    qhome_ref,
    qaway_ref,
    snd,
    rcvp,
    rcvn,
    dts,
    dtr,
    xext,
    mask_ref,
    conv_ref,
    later_ref,
    cols_ref,
    part_ref,
    head_ref,
    ds_ref,
    car_ref,
    rrow_ref,
    score_ref,
    bt_ref,
    sloc,
    ypart,
    es_ref,
    y_home,
    y_away,
    ss_ref,
    normed_ref,
    sa,
    ra,
    da,
    rd,
    ret,
    inc,
    sbuf,
    rbuf,
    small_sems,
    bc_sem,
    x_sems,
    z_sem,
    w_sem,
    xs_sems,
    xr_sems,
    ds_sems,
    dr_sems,
    as_sem,
    ar_sem,
    ads_sem,
    adr_sem,
    rs_sem,
    rr_sems,
    ys_sems,
    yr_sems,
    send_sems,
    recv_sems,
):
    nctx = lax.axis_size("ctx")
    nhead = lax.axis_size("head")
    me = lax.axis_index("ctx")
    mz = lax.axis_index("head")
    tok = bc_ref.shape[0]
    margin = tok // 2
    blocks = tok // SPAN
    quads = x_ref.shape[0]
    groups = SPAN // TILE
    heads = dt_ref.shape[0]
    docs = lengths_ref.shape[0]
    first = me * tok
    around = (lax.rem(me + 1, nctx), lax.rem(me + nctx - 1, nctx))
    hops = (lax.rem(mz + 1, nhead), lax.rem(mz + nhead - 1, nhead))

    may_send = (me != nctx - 1, me != 0)
    may_get = (me != 0, me != nctx - 1)

    def wait_for(ref, sem):
        pltpu.make_async_copy(ref, ref, sem).wait()

    small_loads = [
        pltpu.make_async_copy(src, dst, small_sems.at[i])
        for i, (src, dst) in enumerate(
            (
                (dest_hbm, dest_ref),
                (dt_hbm, dt_ref),
                (convx_hbm, convx_ref),
                (convbc_hbm, convbc_ref),
                (gain_hbm, gain_ref),
                (lengths_hbm, lengths_ref),
                (bias_hbm, bias_ref),
                (alog_hbm, alog_ref),
                (skip_hbm, skip_ref),
            )
        )
    ]
    bc_load = pltpu.make_async_copy(bc_hbm, bc_ref, bc_sem)
    small_loads[0].start()
    bc_load.start()
    barrier = pltpu.get_barrier_semaphore()

    def greet(j, _):
        pl.semaphore_signal(barrier, inc=1, device_id={"ctx": lax.rem(me + j, nctx)})
        return 0

    lax.fori_loop(1, nctx, greet, 0, unroll=True)
    for hop in hops:
        pl.semaphore_signal(barrier, inc=1, device_id={"head": hop})
    for load in small_loads[1:]:
        load.start()

    x_loads = [
        pltpu.make_async_copy(x_hbm.at[:, pl.ds(c * WIDE, WIDE)], x_ref.at[c], x_sems.at[c])
        for c in range(quads)
    ]
    z_load = pltpu.make_async_copy(z_hbm, z_ref, z_sem)
    wide = w_ref.shape[1]
    rows = out_ref.shape[0]
    width = wide // (2 * SUBS)
    w_loads = []
    for sub in range(SUBS):
        for way in range(2):
            w_cols = pl.ds((way * SUBS + sub) * width, width)
            w_loads.append(
                pltpu.make_async_copy(w_hbm.at[:, w_cols], w_ref.at[:, w_cols], w_sem)
            )

    small_loads[0].wait()
    rel_row = jnp.concatenate([dest_ref[i : i + 1, :] for i in range(blocks)], axis=1) - first
    slot = iota((margin + TILE, tok), 0)
    goal = jnp.where(slot < margin, slot + tok, slot + (tok - TILE - margin))
    pout_ref[0 : margin + TILE, :] = one_hot(goal == rel_row)
    pout_ref[margin + TILE :, :] = one_hot(iota((margin, tok), 0) - margin == rel_row)

    def exchange(chunk, way):
        if way == 0:
            src, dst = snd.at[chunk, pl.ds(0, margin + TILE)], rcvp.at[chunk]
        else:
            src, dst = snd.at[chunk, pl.ds(margin + TILE, margin)], rcvn.at[chunk]
        return pltpu.make_async_remote_copy(
            src_ref=src,
            dst_ref=dst,
            send_sem=xs_sems.at[way],
            recv_sem=xr_sems.at[chunk, way],
            device_id={"ctx": around[way]},
        )

    def dt_copy(way):
        return pltpu.make_async_remote_copy(
            src_ref=dts.at[way],
            dst_ref=dtr.at[way],
            send_sem=ds_sems.at[way],
            recv_sem=dr_sems.at[way],
            device_id={"ctx": around[way]},
        )

    def source(chunk):
        return bc_ref[...] if chunk == 0 else x_ref[chunk - 1]

    small_loads[1].wait()
    dt_rows = dt_ref[...]
    dts[0] = nt(dt_rows, pout_ref[0:margin, :]).astype(BF16)
    dts[1] = nt(dt_rows, pout_ref[margin + TILE :, :]).astype(BF16)
    bc_load.wait()
    for load in x_loads:
        load.start()
    snd[0] = mm(pout_ref[...], source(0)).astype(BF16)

    pl.semaphore_wait(barrier, nctx + 1)
    for way in range(2):

        @pl.when(may_send[way])
        def _():
            dt_copy(way).start()
            exchange(0, way).start()


    def make_out(chunk):
        snd[chunk] = mm(pout_ref[...], source(chunk)).astype(BF16)

    def start_out(chunk):
        for way in range(2):

            @pl.when(may_send[way])
            def _():
                exchange(chunk, way).start()


    for chunk in (1, 2):
        x_loads[chunk - 1].wait()
        make_out(chunk)
        start_out(chunk)

    z_load.start()
    for load in w_loads:
        load.start()

    home_ref[...] = one_hot(iota((tok, tok), 0) == rel_row)
    for way in range(2):

        @pl.when(jnp.logical_not(may_get[way]))
        def _():
            landing = (rcvp, rcvn)[way]
            landing[...] = jnp.zeros_like(landing)
            dtr[way] = jnp.zeros_like(dtr[way])
            at = pl.ds(way * margin, margin)
            y_away[:, at, :] = jnp.zeros((quads, margin, WIDE), BF16)


    for load in x_loads[2:]:
        load.wait()
    make_out(3)
    start_out(3)

    for load in small_loads[2:]:
        load.wait()
    row16 = iota((heads, SPAN), 0)
    bias = jnp.zeros((heads, SPAN), F32)
    alog = jnp.zeros((heads, SPAN), F32)
    for h in range(heads):
        bias = jnp.where(row16 == h, bias_ref[h], bias)
        alog = jnp.where(row16 == h, alog_ref[h], alog)
    neg_rate = -jnp.exp(alog)
    for way in range(2):

        @pl.when(may_get[way])
        def _():
            dt_copy(way).wait_recv()

    dt_home = nt(dt_rows, home_ref[...])
    home_first = mm(home_ref[...], source(0))
    dt_raw = dt_home + jnp.concatenate([dtr[0].astype(F32), dtr[1].astype(F32)], axis=1)
    steps = []
    rates = []
    for b in range(blocks):
        logit = dt_raw[:, b * SPAN : (b + 1) * SPAN] + bias
        step = jnp.maximum(logit, 0.0) + jnp.log1p(jnp.exp(-jnp.abs(logit)))
        steps.append(step)
        rates.append(step * neg_rate)
    spare = SPAN - blocks * heads
    steps = jnp.concatenate(steps + [jnp.ones((spare, SPAN), F32)], axis=0)
    rates = jnp.concatenate(rates + [jnp.zeros((spare, SPAN), F32)], axis=0)
    row = iota((SPAN, SPAN), 0)
    lane = iota((SPAN, SPAN), 1)
    upper = jnp.where(row <= lane, 1.0, 0.0)
    cum_rows = jnp.dot(
        rates, upper, precision=lax.Precision.HIGHEST, preferred_element_type=F32
    )
    rrow_ref[...] = LOG2E * (cum_rows - jnp.log(steps))
    cum = cum_rows.T
    step_cols = steps.T
    shift = heads.bit_length() - 1
    lane_block = lax.shift_right_logical(lane, shift)
    row_block = lax.shift_right_logical(row, shift)
    block_start = first + lane_block * SPAN
    pos = block_start + row
    doc_start = jnp.zeros((SPAN, SPAN), jnp.int32)
    begin = jnp.int32(0)
    for d in range(docs):
        doc_start = jnp.where(pos >= begin, begin, doc_start)
        begin = begin + lengths_ref[d]
    last_start = doc_start[SPAN - 1 : SPAN, :]
    last = cum[SPAN - 1 : SPAN, :]
    same_head = (lane & (heads - 1)) == (row & (heads - 1))
    before = jnp.where(same_head & (row_block < lane_block), 1.0, 0.0)
    offset = jnp.dot(
        jnp.broadcast_to(last, (8, SPAN)),
        before,
        precision=lax.Precision.HIGHEST,
        preferred_element_type=F32,
    )[0:1, :]
    w_cols = jnp.where(pos >= last_start, jnp.exp(last - cum) * step_cols, 0.0)
    entry = jnp.where(doc_start < block_start, jnp.exp(cum), 0.0)
    entry_shard = jnp.where(doc_start < first, jnp.exp(cum + offset), 0.0)
    carried = jnp.where(last_start < block_start[0:1, :], jnp.exp(last), 0.0)
    shard_decay = jnp.where(last_start < first, jnp.exp(last + offset), 0.0)
    carried = jnp.broadcast_to(carried, (8, SPAN))
    later_ref[0] = LOG2E * cum
    later_ref[1] = entry
    later_ref[2] = entry_shard

    def turned(array, b):
        turn = (SPAN - b * heads) % SPAN
        return pltpu.roll(array, turn, 1) if turn else array

    def split(kind, b, array):
        array = turned(array, b)
        rough = array.astype(BF16)
        fine = (array - rough.astype(F32)).astype(BF16)
        part_ref[kind, b * SPAN : (b + 1) * SPAN, 0:SPAN] = rough
        part_ref[kind, b * SPAN : (b + 1) * SPAN, SPAN:] = fine

    def later():
        for b in range(blocks):
            cols_ref[b] = turned(later_ref[0], b)
            split(1, b, later_ref[1])
            split(2, b, later_ref[2])

    for b in range(blocks):
        split(0, b, w_cols)
        ds_ref[b] = turned(doc_start, b)
        car_ref[b] = turned(carried, b)
    for quad in range(quads):
        key = iota((2 * SPAN, WIDE), 0) & (SPAN - 1)
        head = lax.shift_right_logical(iota((2 * SPAN, WIDE), 1), 6) + 4 * quad
        head_ref[quad] = one_hot(key == head)
    decay_at = (blocks - 1) * heads

    low = iota((1, SPAN), 1) < SPAN // 2

    def spread(cols, quad, at=0):
        parts = []
        for pair in range(2):
            h = at + 4 * quad + 2 * pair
            parts.append(jnp.where(low, cols[:, h : h + 1], cols[:, h + 1 : h + 2]))
        return jnp.concatenate(parts, axis=1)

    def rows_of(b):
        return pl.ds(pl.multiple_of(b * SPAN, SPAN), SPAN)

    def pack_conv(chunk, home):
        for way in range(2):

            @pl.when(may_get[way])
            def _():
                exchange(chunk, way).wait_recv()

        if chunk == 0:
            make_out(quads)
        if chunk < quads:
            ypart[chunk] = mm(home_ref[...], source(chunk + 1))
        if chunk == 0:
            taps = convbc_ref[...].astype(F32)
        else:
            taps = convx_ref[:, (chunk - 1) * WIDE : chunk * WIDE].astype(F32)
        for half in range(2):
            at = slice(half * SPAN, (half + 1) * SPAN)
            xext[half, 0:TILE, :] = rcvp[chunk, margin : margin + TILE, at].astype(F32) + snd[
                chunk, tok : tok + TILE, at
            ].astype(F32)
            xext[half, TILE : TILE + margin, :] = home[0:margin, at] + rcvp[
                chunk, 0:margin, at
            ].astype(F32)
            xext[half, TILE + margin :, :] = home[margin:, at] + rcvn[chunk, :, at].astype(F32)
        for half in range(2):
            at = slice(half * SPAN, (half + 1) * SPAN)
            for b in range(blocks):
                base = b * SPAN + TILE
                total = taps[3:4, at] * xext[half, base : base + SPAN, :]
                for tap in range(KCONV - 1):
                    back = KCONV - 1 - tap
                    piece = xext[half, base - back : base - back + SPAN, :]
                    usable = mask_ref[tap, b * SPAN : (b + 1) * SPAN, :]
                    total = total + taps[tap : tap + 1, at] * (usable * piece)
                conv_ref[chunk, b * SPAN : (b + 1) * SPAN, at] = half_silu(total).astype(BF16)

    for b in range(blocks):
        begins = jnp.broadcast_to(ds_ref[b][:, 0:1], (SPAN, SPAN)) - (first + b * SPAN) - row
        for tap in range(KCONV - 1):
            usable = jnp.where(begins <= tap + 1 - KCONV, 1.0, 0.0)
            mask_ref[tap, b * SPAN : (b + 1) * SPAN, :] = usable

    pack_conv(0, home_first)

    eye = one_hot(row == lane)

    def prepare(b, _):
        bmat = conv_ref[0, rows_of(b), 0:N]
        cmat = conv_ref[0, rows_of(b), N : 2 * N]
        bt_ref[b] = nt(eye, bmat).astype(BF16)
        begins = ds_ref[b][:, 0:1] - (first + b * SPAN)
        score_ref[b] = jnp.where((lane <= row) & (lane >= begins), nt(cmat, bmat), 0.0)
        return 0

    lax.fori_loop(0, blocks, prepare, 0, unroll=True)

    def state_copy(quad, group, owner):
        return pltpu.make_async_remote_copy(
            src_ref=sa.at[quad, group],
            dst_ref=ra.at[lax.rem(me + nctx - owner, nctx)],
            send_sem=as_sem,
            recv_sem=ar_sem,
            device_id={"ctx": owner},
        )

    def decay_copy(quad, owner):
        return pltpu.make_async_remote_copy(
            src_ref=da.at[quad, pl.ds(0, 1)],
            dst_ref=rd.at[lax.rem(me + nctx - owner, nctx), pl.ds(0, 1)],
            send_sem=ads_sem,
            recv_sem=adr_sem,
            device_id={"ctx": owner},
        )

    def shard_state(quad):
        weights = mm(part_ref[0], head_ref[quad])
        state = jnp.zeros((N, WIDE), F32)
        for b in range(blocks):
            sloc[quad, b] = state.astype(BF16)
            weight = weights[b * SPAN : (b + 1) * SPAN]
            x_float = conv_ref[quad + 1, b * SPAN : (b + 1) * SPAN, :].astype(F32)
            inner_sum = mm(bt_ref[b], (weight * x_float).astype(BF16))
            state = state * spread(car_ref[b][0:1, :], quad) + inner_sum

        sa[quad] = state.astype(BF16).reshape(groups, TILE, WIDE)
        da[quad] = jnp.broadcast_to(spread(shard_decay, quad, decay_at), (8, WIDE))

        def give(j, _):
            group = lax.rem(j + me, groups)
            owner = group * quads + quad

            @pl.when(owner != me)
            def _():
                state_copy(quad, group, owner).start()
                decay_copy(quad, owner).start()

            @pl.when(owner == me)
            def _():
                ra[0] = sa[quad, group]
                rd[0] = da[quad]

            return 0

        lax.fori_loop(0, groups, give, 0)

    def inner(quad):
        entries = mm(part_ref[1], head_ref[quad])
        es_ref[quad] = mm(part_ref[2], head_ref[quad])

        for b in range(blocks):
            xs = conv_ref[quad + 1, rows_of(b), :]
            cmat = conv_ref[0, rows_of(b), N : 2 * N]
            cum_cols = cols_ref[b]
            gaps = rrow_ref[b * heads : (b + 1) * heads, :]
            score = score_ref[b]
            x_float = xs.astype(F32)
            y = mm(cmat, sloc[quad, b]) * entries[b * SPAN : (b + 1) * SPAN]
            parts = []
            for pair in range(2):
                mixing = []
                for h in (4 * quad + 2 * pair, 4 * quad + 2 * pair + 1):
                    gap = jnp.minimum(cum_cols[:, h : h + 1] - gaps[h : h + 1, :], 80.0)
                    mixing.append((jnp.exp2(gap) * score).astype(BF16))
                x_pair = x_float[:, pair * SPAN : (pair + 1) * SPAN]
                x_both = jnp.concatenate(
                    [jnp.where(low, x_pair, 0.0), jnp.where(low, 0.0, x_pair)], axis=0
                ).astype(BF16)
                h = 4 * quad + 2 * pair
                skip = jnp.where(low, skip_ref[h], skip_ref[h + 1])
                parts.append(mm(jnp.concatenate(mixing, axis=1), x_both) + skip * x_pair)
            ypart[quad, rows_of(b), :] = y + jnp.concatenate(parts, axis=1)

    my_quad = lax.rem(me, quads)
    my_group = lax.div(me, quads)

    def back_copy(shard, quad, group):
        return pltpu.make_async_remote_copy(
            src_ref=ret.at[shard],
            dst_ref=inc.at[quad, group],
            send_sem=rs_sem,
            recv_sem=rr_sems.at[quad],
            device_id={"ctx": shard},
        )

    def scan(shard, state):
        ret[shard] = state.astype(BF16)

        @pl.when(shard != me)
        def _():
            back_copy(shard, my_quad, my_group).start()

        @pl.when(shard == me)
        def _():
            inc[my_quad, my_group] = state.astype(BF16)

        place = lax.rem(shard + nctx - me, nctx)
        return state * rd[place, 0:1, :] + ra[place].astype(F32)

    def scan_slice(quad):
        @pl.when(my_quad == quad)
        def _():
            wait_for(ra.at[pl.ds(1, nctx - 1)], ar_sem)
            wait_for(rd.at[pl.ds(1, nctx - 1), pl.ds(0, 1)], adr_sem)
            lax.fori_loop(0, nctx, scan, jnp.zeros((TILE, WIDE), F32))

    def y_copy(quad, way):
        if way == 0:
            src, dst = pl.ds(margin, margin), pl.ds(0, margin)
        else:
            src, dst = pl.ds(0, margin), pl.ds(margin, margin)
        return pltpu.make_async_remote_copy(
            src_ref=y_home.at[quad, src],
            dst_ref=y_away.at[quad, dst],
            send_sem=ys_sems.at[way],
            recv_sem=yr_sems.at[quad, way],
            device_id={"ctx": around[way]},
        )

    def finish(quad):
        @pl.when(my_quad != quad)
        def _():
            wait_for(inc.at[quad], rr_sems.at[quad])

        @pl.when(my_quad == quad)
        def _():
            wait_for(inc.at[quad, pl.ds(1, groups - 1)], rr_sems.at[quad])

        incoming = inc[quad].reshape(N, WIDE)
        fix = mm(conv_ref[0, :, N : 2 * N], incoming)
        y_home[quad] = (ypart[quad] + fix * es_ref[quad]).astype(BF16)
        for way in range(2):

            @pl.when(may_send[way])
            def _():
                y_copy(quad, way).start()


    def work(quad):
        with scope("work%d" % quad):
            pack_conv(quad + 1, ypart[quad])
            shard_state(quad)

    work(0)
    start_out(quads)
    work(1)
    with scope("inner0"):
        later()
        inner(0)
    work(2)
    with scope("scan0"):
        scan_slice(0)
    work(3)
    with scope("scan1"):
        scan_slice(1)
    with scope("inner1"):
        inner(1)
    with scope("scan2"):
        scan_slice(2)
    with scope("finish0"):
        finish(0)
    with scope("inner2"):
        inner(2)
    with scope("scan3"):
        scan_slice(3)
    with scope("finish1"):
        finish(1)
    with scope("finish2"):
        finish(2)
    with scope("inner3"):
        inner(3)
    for i in range(blocks):
        across = jnp.broadcast_to(dest_ref[i : i + 1, :], (SPAN, SPAN)).T - first
        beside = across + jnp.where(across < 0, margin, -margin)
        beside = jnp.where((across < 0) | (across >= tok), beside, -1)
        for j in range(blocks):
            at = slice(i * SPAN, (i + 1) * SPAN), slice(j * SPAN, (j + 1) * SPAN)
            qhome_ref[at] = one_hot(across == lane + j * SPAN)
            qaway_ref[at] = one_hot(beside == lane + j * SPAN)
    z_load.wait()
    rbuf[0] = jnp.zeros_like(rbuf[0])
    wait_for(w_ref, w_sem)

    def gather_home(quad):
        ypart[quad] = mm(qhome_ref[...], y_home[quad])

    def gate(quad, at, z_at):
        y_rows = ypart[quad, at, :] + mm(qaway_ref[at, :], y_away[quad])
        gated = y_rows * half_silu(z_ref[at, z_at].astype(F32))
        square = gated * gated
        return gated, square[:, 0:SPAN] + square[:, SPAN:]

    def gather(quad):
        for way in range(2):

            @pl.when(may_get[way])
            def _():
                y_copy(quad, way).wait_recv()

        if quad < quads - 1:
            gather_home(quad + 1)
        if quad < quads - 1:
            gated, square = gate(quad, pl.ds(0, tok), pl.ds(quad * WIDE, WIDE))
            ypart[quad] = gated
            ss_ref[...] = square if quad == 0 else ss_ref[...] + square

    gather_home(0)
    with scope("finish3"):
        finish(3)
    for quad in range(quads):
        with scope("gather%d" % quad):
            gather(quad)

    def ready(chunk):
        at = pl.ds(pl.multiple_of(chunk * rows, rows), rows)
        gains = gain_ref[...].astype(F32)
        gated, square = gate(quads - 1, at, pl.ds((quads - 1) * WIDE, WIDE))
        total = jnp.sum(ss_ref[at, :] + square, axis=1, keepdims=True)
        inv = lax.rsqrt(total * (1.0 / (quads * WIDE)) + 1e-05)
        for quad in range(quads):
            gain = jnp.concatenate(
                [gains[2 * quad + i : 2 * quad + i + 1, :] for i in range(2)], axis=1
            )
            value = gated if quad == quads - 1 else ypart[quad, at, :]
            normed_ref[at, quad * WIDE : (quad + 1) * WIDE] = (
                value * inv * gain
            ).astype(BF16)

    def ring(step, way, sub):
        return pltpu.make_async_remote_copy(
            src_ref=sbuf.at[step, way, sub],
            dst_ref=rbuf.at[step + 1, way, sub],
            send_sem=send_sems.at[way, sub],
            recv_sem=recv_sems.at[step, way, sub],
            device_id={"head": hops[way]},
        )

    def chunk_of(step, way):
        back = lax.rem(mz + 2 * nhead - 1 - step, nhead)
        return jnp.where(way == 0, back, lax.rem(mz + 1 + step, nhead))

    def one(step, _):
        @pl.when(step == nhead // 2)
        def _():
            ready(mz)

        for sub in range(SUBS):
            for way in range(2):
                chunk = chunk_of(step, way)
                if sub == 0:

                    @pl.when((step < nhead // 2) & ((step < nhead // 2 - 1) | (way == 0)))
                    def _():
                        ready(chunk)

                at = (way * SUBS + sub) * width
                part = mm(
                    normed_ref[pl.ds(pl.multiple_of(chunk * rows, rows), rows), :],
                    w_ref[:, at : at + width],
                )

                @pl.when(step > 0)
                def _():
                    ring(step - 1, way, sub).wait_recv()
                    ring(step - 1, way, sub).wait_send()

                total = (part + rbuf[step, way, sub].astype(F32)).astype(BF16)

                @pl.when(step < nhead - 1)
                def _():
                    sbuf[step, way, sub] = total
                    ring(step, way, sub).start()

                @pl.when(step == nhead - 1)
                def _():
                    out_ref[:, at : at + width] = total

        return 0

    lax.fori_loop(0, nhead - 1, one, 0)

    for way in range(2):

        @pl.when(may_send[way])
        def _():
            dt_copy(way).wait_send()
            sent = (pl.ds(0, margin + TILE), pl.ds(margin + TILE, margin))[way]
            wait_for(snd.at[:, sent], xs_sems.at[way])
            wait_for(y_home.at[:, pl.ds(0, margin)], ys_sems.at[way])

    wait_for(ra.at[pl.ds(1, nctx - 1)], as_sem)
    wait_for(rd.at[pl.ds(1, nctx - 1), pl.ds(0, 1)], ads_sem)
    wait_for(ret.at[pl.ds(1, nctx - 1)], rs_sem)
    lax.fori_loop(nhead - 1, nhead, one, 0)


def per_device(
    x_in,
    z_in,
    bc_in,
    dt_in,
    destination,
    doc_lengths,
    conv_x,
    conv_bc,
    dt_bias,
    a_log,
    skip_gain,
    norm_gain,
    out_weight,
):
    nctx = lax.axis_size("ctx")
    nhead = lax.axis_size("head")
    tok, channels = x_in.shape
    heads = dt_in.shape[1]
    bc_width = bc_in.shape[1]
    margin = tok // 2
    blocks = tok // SPAN
    quads = channels // WIDE
    groups = N // TILE
    rows = tok // nhead
    depth, wide = out_weight.shape
    width = wide // (2 * SUBS)
    dma = pltpu.SemaphoreType.DMA
    vmem = pl.BlockSpec(memory_space=pltpu.VMEM)
    anywhere = pl.BlockSpec(memory_space=pl.ANY)
    scratch = [
        pltpu.SMEM(doc_lengths.shape, jnp.int32),
        pltpu.SMEM((heads,), F32),
        pltpu.SMEM((heads,), F32),
        pltpu.SMEM((heads,), F32),
        pltpu.VMEM((heads, tok), BF16),
        pltpu.VMEM((blocks, SPAN), jnp.int32),
        pltpu.VMEM(conv_x.shape, BF16),
        pltpu.VMEM(conv_bc.shape, BF16),
        pltpu.VMEM((channels // SPAN, SPAN), BF16),
        pltpu.VMEM((tok, bc_width), BF16),
        pltpu.VMEM((quads, tok, WIDE), BF16),
        pltpu.VMEM((tok, channels), BF16),
        pltpu.VMEM((depth, wide), BF16),
        pltpu.VMEM((tok + TILE, tok), BF16),
        pltpu.VMEM((tok, tok), BF16),
        pltpu.VMEM((tok, tok), BF16),
        pltpu.VMEM((tok, tok), BF16),
        pltpu.VMEM((quads + 1, tok + TILE, WIDE), BF16),
        pltpu.VMEM((quads + 1, margin + TILE, WIDE), BF16),
        pltpu.VMEM((quads + 1, margin, WIDE), BF16),
        pltpu.VMEM((2, heads, margin), BF16),
        pltpu.VMEM((2, heads, margin), BF16),
        pltpu.VMEM((2, tok + TILE, SPAN), F32),
        pltpu.VMEM((KCONV - 1, tok, SPAN), F32),
        pltpu.VMEM((quads + 1, tok, WIDE), BF16),
        pltpu.VMEM((3, SPAN, SPAN), F32),
        pltpu.VMEM((blocks, SPAN, SPAN), F32),
        pltpu.VMEM((3, tok, 2 * SPAN), BF16),
        pltpu.VMEM((quads, 2 * SPAN, WIDE), BF16),
        pltpu.VMEM((blocks, SPAN, SPAN), jnp.int32),
        pltpu.VMEM((blocks, 8, SPAN), F32),
        pltpu.VMEM((SPAN, SPAN), F32),
        pltpu.VMEM((blocks, SPAN, SPAN), F32),
        pltpu.VMEM((blocks, N, SPAN), BF16),
        pltpu.VMEM((quads, blocks, N, WIDE), BF16),
        pltpu.VMEM((quads, tok, WIDE), F32),
        pltpu.VMEM((quads, tok, WIDE), F32),
        pltpu.VMEM((quads, tok, WIDE), BF16),
        pltpu.VMEM((quads, tok, WIDE), BF16),
        pltpu.VMEM((tok, SPAN), F32),
        pltpu.VMEM((tok, channels), BF16),
        pltpu.VMEM((quads, groups, TILE, WIDE), BF16),
        pltpu.VMEM((nctx, TILE, WIDE), BF16),
        pltpu.VMEM((quads, 8, WIDE), F32),
        pltpu.VMEM((nctx, 8, WIDE), F32),
        pltpu.VMEM((nctx, TILE, WIDE), BF16),
        pltpu.VMEM((quads, groups, TILE, WIDE), BF16),
        pltpu.VMEM((nhead - 1, 2, SUBS, rows, width), BF16),
        pltpu.VMEM((nhead, 2, SUBS, rows, width), BF16),
        dma((9,)),
        dma(()),
        dma((quads,)),
        dma(()),
        dma(()),
        dma((2,)),
        dma((quads + 1, 2)),
        dma((2,)),
        dma((2,)),
        dma(()),
        dma(()),
        dma(()),
        dma(()),
        dma(()),
        dma((quads,)),
        dma((2,)),
        dma((quads, 2)),
        dma((2, SUBS)),
        dma((nhead - 1, 2, SUBS)),
    ]
    return pl.pallas_call(
        layer_kernel,
        out_shape=pltpu.VMEM((rows, wide), BF16),
        in_specs=[
            anywhere,
            anywhere,
            anywhere,
            anywhere,
            anywhere,
            anywhere,
            anywhere,
            anywhere,
            anywhere,
            anywhere,
            anywhere,
            anywhere,
            anywhere,
        ],
        out_specs=vmem,
        scratch_shapes=scratch,
        compiler_params=pltpu.CompilerParams(
            collective_id=0, has_side_effects=True, vmem_limit_bytes=60 << 20
        ),
    )(
        x_in,
        z_in,
        bc_in,
        dt_in.T,
        destination.reshape(blocks, SPAN),
        doc_lengths,
        conv_x,
        conv_bc,
        dt_bias,
        a_log,
        skip_gain,
        norm_gain.reshape(channels // SPAN, SPAN),
        out_weight,
    )


def solution(mesh):
    placed = (
        P("ctx", "head"),
        P("ctx", "head"),
        P("ctx", "head"),
        P("ctx", "head"),
        P("ctx"),
        P(),
        P(None, "head"),
        P(None, "head"),
        P("head"),
        P("head"),
        P("head"),
        P("head"),
        P("head", None),
    )
    return jax.shard_map(
        per_device, mesh=mesh, in_specs=placed, out_specs=P(("ctx", "head"), None), check_vma=False
    )
```
